32 devices in a mesh: dp: 4 (over x, core), ctx: 4 (over z), expert: 2 (over y).
Axes of the slice: x: 2, y: 2, z: 4, core: 2. Of those that a mesh axis runs over, the one named last changes fastest.
Arguments:
- tokens: bfloat16 [8, 1024, 768], P(('dp', 'expert'), 'ctx'), may hold values from -6 to 6
- cotangent: bfloat16 [8, 1024, 768], P(('dp', 'expert'), 'ctx'), may hold values from -6 to 6
- routes: int32 [8, 1024, 1], P(('dp', 'expert'), 'ctx'), may hold values from 0 to 7
- buckets: int32 [2047], replicated, may hold values from 0 to 31
- gain_attn: float32 [768], replicated, may hold values from 0.5 to 1.5
- w_query: bfloat16 [768, 768], replicated, may hold values from -0.109375 to 0.109375
- w_key: bfloat16 [768, 768], replicated, may hold values from -0.109375 to 0.109375
- w_value: bfloat16 [768, 768], replicated, may hold values from -0.21875 to 0.21875
- w_output: bfloat16 [768, 768], replicated, may hold values from -0.875 to 0.875
- bias_table: float32 [32, 12], replicated, may hold values from -6 to 6
- gain_ffn: float32 [768], replicated, may hold values from 0.5 to 1.5
- w_router: bfloat16 [768, 8], replicated, may hold values from -0.15625 to 0.15625
- w_in: bfloat16 [8, 768, 3072], P(('dp', 'expert'), None, 'ctx'), may hold values from -0.21875 to 0.21875
- w_out: bfloat16 [8, 3072, 768], P(('dp', 'expert'), 'ctx'), may hold values from -0.875 to 0.875
Outputs:
- layer_out: bfloat16 [8, 1024, 768], P(('dp', 'expert'), 'ctx')
- grad_tokens: bfloat16 [8, 1024, 768], P(('dp', 'expert'), 'ctx')
- grad_gain_attn: float32 [768], replicated
- grad_query: float32 [768, 768], replicated
- grad_key: float32 [768, 768], replicated
- grad_value: float32 [768, 768], replicated
- grad_output: float32 [768, 768], replicated
- grad_bias_table: float32 [32, 12], replicated
- grad_gain_ffn: float32 [768], replicated
- grad_router: float32 [768, 8], replicated
- grad_w_in: float32 [8, 768, 3072], P(('dp', 'expert'), None, 'ctx')
- grad_w_out: float32 [8, 3072, 768], P(('dp', 'expert'), 'ctx')
The draws below stay inside these ranges and needn't reach their ends.
All inputs are finite; a program needn't handle non-finite values.
Results may differ from the reference program's by a relative error of at most 0.018.
Values may be sent and summed in bfloat16 or wider, within the bound.
No kernel may reach another device: no remote copies, remote signals or barrier semaphores. Data moves between devices by JAX's collectives and lax.ppermute only.
A program may use at most 256 MiB of HBM per device.

```python
import jax
import jax.numpy as jnp
from jax import lax

H = 12
HD = 64
D = 768
FF = 3072
NB = 32
SEQ_DEV = 1
BLK = 256
LEN = 1024
SEQS = 8
TOK_DEV = 256
GROUPS = 32
EXPERTS = 8
CAP = 40
N_CTX = 4


def with_ends(values, stream_key, smallest, top_value):
    longest = values.shape.index(max(values.shape))
    spots = []
    for shift in (0, 1):
        where = [jax.random.randint(jax.random.fold_in(stream_key, axis), (), 0, length) for axis, length in enumerate(values.shape)]
        where[longest] = (where[longest] + shift) % values.shape[longest]
        spots.append(tuple(where))
    return values.at[spots[0]].set(smallest).at[spots[1]].set(top_value)


def block_levels(key, dims, cuts, least, top_value):
    gain = 1.0
    for position, parts in cuts:
        draws = jax.random.uniform(jax.random.fold_in(jax.random.fold_in(key, 6), position), (parts,), jnp.float32, least / len(cuts), top_value / len(cuts))
        gain = gain * jnp.repeat(jnp.exp(draws), dims[position] // parts).reshape((-1,) + (1,) * (len(dims) - 1 - position))
    return gain


def choose_distinct(stream_key, rows, amount, top, lift):
    ranking = jax.random.permutation(jax.random.fold_in(stream_key, 1), amount)
    boost = ranking
    for power in range(3):
        boost = boost * boost // amount
    boost = boost * lift // amount
    tickets = jax.random.randint(jax.random.fold_in(stream_key, 2), (rows, amount), 0, 4096) + boost
    fixed_rows = jax.random.permutation(jax.random.fold_in(stream_key, 3), rows)[jnp.arange(amount) % rows]
    tickets = jnp.where(jnp.arange(rows)[:, None] == fixed_rows[None, :], 1 << 14, tickets)
    priority = tickets * amount + jnp.arange(amount)
    return lax.top_k(priority.astype(jnp.int32), top)[1].astype(jnp.int32)


def centred(own_key, extent, scale, reach, cuts=(), kind=jnp.bfloat16):
    gain = block_levels(own_key, extent, cuts, -0.22, 0.18) if cuts else 1.0
    values = jax.random.normal(own_key, extent, jnp.float32) * scale * gain
    return jnp.minimum(jnp.maximum(values, -reach), reach).astype(kind)


def setup_inputs(seed: int = 0) -> dict:
    splits = jax.random.split(jax.random.key(seed), 15)
    tokens = centred(splits[0], (SEQS, LEN, D), 1.0, 6.0, ((0, 8), (1, 4)))
    cotangent = centred(splits[1], (SEQS, LEN, D), 1.0, 6.0, ((0, 8), (1, 4)))
    routes = choose_distinct(splits[2], SEQS * LEN, EXPERTS, 1, 1024).reshape((SEQS, LEN, 1))
    buckets = with_ends(jax.random.randint(splits[3], (2 * LEN - 1,), 0, NB), jax.random.fold_in(splits[3], 1), 0, NB - 1).astype(jnp.int32)
    gain_attn = jnp.clip(1.0 + 0.1 * jax.random.normal(splits[4], (D,), jnp.float32), 0.5, 1.5)
    w_query = centred(splits[5], (D, D), (4 * D) ** -0.5, 0.109375)
    w_key = centred(splits[6], (D, D), (4 * D) ** -0.5, 0.109375)
    w_value = centred(splits[7], (D, D), D ** -0.5, 0.21875)
    w_output = centred(splits[8], (D, D), (D // 16) ** -0.5, 0.875)
    bias_table = centred(splits[9], (NB, H), 1.0, 6.0, (), jnp.float32)
    gain_ffn = jnp.clip(1.0 + 0.1 * jax.random.normal(splits[10], (D,), jnp.float32), 0.5, 1.5)
    w_router = centred(splits[11], (D, EXPERTS), (2 * D) ** -0.5, 0.15625)
    w_in = centred(splits[12], (EXPERTS, D, FF), D ** -0.5, 0.21875, ((0, 8), (2, 4)))
    w_out = centred(splits[13], (EXPERTS, FF, D), (max(FF // (EXPERTS * EXPERTS), 1)) ** -0.5, 0.875, ((0, 8), (1, 4)))
    return {"tokens": tokens, "cotangent": cotangent, "routes": routes, "buckets": buckets, "gain_attn": gain_attn, "w_query": w_query, "w_key": w_key, "w_value": w_value, "w_output": w_output, "bias_table": bias_table, "gain_ffn": gain_ffn, "w_router": w_router, "w_in": w_in, "w_out": w_out}


epsilon = 1e-06
exact_prec = lax.Precision.HIGHEST

@jax.custom_vjp
def low(v):
    return lax.optimization_barrier(v.astype(jnp.bfloat16)).astype(jnp.float32)

@jax.custom_vjp
def low_back(v):
    return v

def low_keep(v):
    return (low(v), None)

def low_pass(kept, grad):
    return (grad,)

def back_keep(v):
    return (v, None)

def back_low(kept, grad):
    return (low(grad),)
low.defvjp(low_keep, low_pass)
low_back.defvjp(back_keep, back_low)

def attention_block(block_in, bias_full):
    query_rows, key_rows, value_rows = block_in
    scores = jnp.einsum('sqhd,skhd->shqk', query_rows, key_rows, precision=exact_prec) + bias_full[None]
    scores = low_back(scores)
    weights = low(jax.nn.softmax(scores, axis=-1))
    return jnp.einsum('shqk,skhd->sqhd', weights, value_rows, precision=exact_prec)

def expert_block(block_in):
    row_data, first_proj, second_proj = block_in
    pre_act = low_back(jnp.dot(row_data, first_proj, precision=exact_prec))
    hidden = low(jax.nn.gelu(pre_act, approximate=False))
    return low_back(low(jnp.dot(hidden, second_proj, precision=exact_prec)))

def token_targets(route_grid):
    grouped = route_grid.reshape(SEQS // SEQ_DEV, SEQ_DEV, N_CTX, BLK).transpose(0, 2, 1, 3).reshape(GROUPS, TOK_DEV)
    route_hot = (grouped[:, :, None] == jnp.arange(EXPERTS, dtype=jnp.int32)[None, None, :]).astype(jnp.int32)
    slot_index = lax.optimization_barrier(jnp.sum((jnp.cumsum(route_hot, axis=1) - route_hot) * route_hot, axis=2))
    group_ids = jnp.broadcast_to(jnp.arange(GROUPS, dtype=jnp.int32)[:, None], (GROUPS, TOK_DEV))
    target = (group_ids * EXPERTS + grouped) * CAP + slot_index
    target = jnp.where(slot_index < CAP, target, GROUPS * EXPERTS * CAP).astype(jnp.int32)
    return target.reshape(SEQS // SEQ_DEV, N_CTX, SEQ_DEV, BLK).transpose(0, 2, 1, 3).reshape(-1)

def reference(tokens, cotangent, routes, buckets, gain_attn, w_query, w_key, w_value, w_output, bias_table, gain_ffn, w_router, w_in, w_out):
    route_flat = routes.reshape(-1).astype(jnp.int32)
    target = token_targets(route_flat.reshape(SEQS, LEN))
    total_slots = GROUPS * EXPERTS * CAP
    keep_mask = (target < total_slots).astype(jnp.float32)
    safe_target = jnp.minimum(target, total_slots - 1)
    route_hot = (route_flat[:, None] == jnp.arange(EXPERTS, dtype=jnp.int32)[None, :]).astype(jnp.float32)
    offset_index = (jnp.arange(LEN, dtype=jnp.int32)[None, :] - jnp.arange(LEN, dtype=jnp.int32)[:, None] + LEN - 1).astype(jnp.int32)

    def forward(row_data, gain_one, query_w, key_w, value_w, output_w, table, gain_two, router_w, first_w, second_w):
        scale_one = lax.rsqrt(lax.optimization_barrier(jnp.mean(row_data * row_data, axis=-1, keepdims=True)) + epsilon)
        normed_one = low(row_data * scale_one * gain_one)

        def project(weight):
            made = low_back(low(jnp.dot(normed_one, weight, precision=exact_prec)))
            return made.reshape(SEQS // SEQ_DEV, SEQ_DEV, LEN, H, HD)
        rel_bias = jnp.take(table, buckets, axis=0)
        bias_full = jnp.take(rel_bias, offset_index, axis=0).transpose(2, 0, 1)

        def attend(block_in):
            return attention_block(block_in, bias_full)
        attended = lax.map(jax.checkpoint(attend), (project(query_w), project(key_w), project(value_w)))
        attended = low_back(low(attended.reshape(-1, D)))
        branch = low_back(jnp.dot(attended, output_w, precision=exact_prec))
        resid = row_data + branch
        scale_two = lax.rsqrt(lax.optimization_barrier(jnp.mean(resid * resid, axis=-1, keepdims=True)) + epsilon)
        normed_two = low(resid * scale_two * gain_two)
        logits = low_back(jnp.dot(normed_two, router_w, precision=exact_prec))
        probs = jax.nn.softmax(logits, axis=-1)
        gate = lax.optimization_barrier(jnp.sum(probs * route_hot, axis=-1))
        buffer = jnp.zeros((total_slots, D), jnp.float32).at[target].set(normed_two, mode='drop')
        buffer = low_back(buffer)
        by_expert = buffer.reshape(GROUPS, EXPERTS, CAP, D).transpose(1, 0, 2, 3).reshape(EXPERTS, GROUPS * CAP, D)
        outputs = lax.map(jax.checkpoint(expert_block), (by_expert, first_w, second_w))
        flat_out = outputs.reshape(EXPERTS, GROUPS, CAP, D).transpose(1, 0, 2, 3).reshape(-1, D)
        picked = jnp.take(flat_out, safe_target, axis=0) * keep_mask[:, None]
        return resid + gate[:, None] * picked
    params = (gain_attn, w_query, w_key, w_value, w_output, bias_table, gain_ffn, w_router, w_in, w_out)
    params = tuple((item.astype(jnp.float32) for item in params))
    row_data = tokens.reshape(-1, D).astype(jnp.float32)
    result, pull_back = jax.vjp(forward, row_data, *params)
    grads = pull_back(cotangent.reshape(-1, D).astype(jnp.float32))
    return (result.reshape(SEQS, LEN, D).astype(jnp.bfloat16), grads[0].reshape(SEQS, LEN, D).astype(jnp.bfloat16), grads[1], grads[2], grads[3], grads[4], grads[5], grads[6], grads[7], grads[8], grads[9], grads[10])
```

```python
import jax
import jax.numpy as jnp
from jax import lax
from jax.sharding import PartitionSpec as P

H = 12
HD = 64
NB = 32


epsilon = 1e-06
exact_prec = lax.Precision.HIGHEST


def norm_scale(row_data):
    return lax.rsqrt(jnp.mean(row_data * row_data, axis=-1, keepdims=True) + epsilon)


def norm_back(grad_in, row_data, scale, gain):
    weighted = grad_in * gain
    inner = jnp.mean(weighted * row_data, axis=-1, keepdims=True)
    return scale * weighted - row_data * (scale * scale * scale) * inner


def smooth_act(values):
    return jax.nn.gelu(values, approximate=False)


def gelu_with_back(pre_act):
    return jax.vjp(smooth_act, pre_act)


def contract_rows(left, right):
    return lax.dot_general(
        left, right, (((0,), (0,)), ((), ())), preferred_element_type=jnp.float32
    )


def offset_start(query_start, query_count, key_start, full_len):
    return key_start - query_start + full_len - query_count


def bias_block(rel_bias, base, query_count, key_count):
    width = query_count + key_count - 1
    segment = lax.dynamic_slice_in_dim(rel_bias, base, width, 1)
    heads = segment.shape[0]
    spread = jnp.broadcast_to(segment[:, None, :], (heads, query_count, width)).reshape(
        heads, query_count * width
    )
    skewed = spread[:, query_count - 1 : query_count - 1 + query_count * (width - 1)]
    return skewed.reshape(heads, query_count, width - 1)[:, :, :key_count]


def bias_grad_block(grad_block, query_count, key_count):
    width = query_count + key_count - 1
    heads = grad_block.shape[0]
    padded = jnp.pad(grad_block, ((0, 0), (0, 0), (0, width - 1 - key_count)))
    flat = padded.reshape(heads, query_count * (width - 1))
    flat = jnp.pad(flat, ((0, 0), (query_count - 1, 1)))
    return jnp.sum(flat.reshape(heads, query_count, width), axis=1)


def shards(
    tokens,
    cotangent,
    routes,
    buckets,
    gain_attn,
    w_query,
    w_key,
    w_value,
    w_output,
    bias_table,
    gain_ffn,
    w_router,
    w_in,
    w_out,
):
    seq_dev, block_len, model_width = tokens.shape
    ctx_size = lax.axis_size("ctx")
    experts = lax.axis_size(("dp", "expert"))
    full_len = block_len * ctx_size
    tok_count = seq_dev * block_len
    capacity = max(2, (5 * tok_count + 4 * experts - 1) // (4 * experts))
    query_start = lax.axis_index("ctx") * block_len
    bfloat = jnp.bfloat16
    single = jnp.float32
    row_data = tokens.reshape(tok_count, model_width).astype(single)
    scale_one = norm_scale(row_data)
    normed_one = (row_data * scale_one * gain_attn).astype(bfloat)
    query_rows = jnp.dot(normed_one, w_query, preferred_element_type=single).astype(bfloat)
    key_rows = jnp.dot(normed_one, w_key, preferred_element_type=single).astype(bfloat)
    value_rows = jnp.dot(normed_one, w_value, preferred_element_type=single).astype(bfloat)
    query_heads = query_rows.reshape(seq_dev, block_len, H, HD)
    key_blocks = key_rows.reshape(seq_dev, block_len, model_width)
    value_blocks = value_rows.reshape(seq_dev, block_len, model_width)
    bucket_hot = (buckets[:, None] == jnp.arange(NB, dtype=jnp.int32)[None, :]).astype(single)
    rel_bias = lax.dot_general(
        bias_table, bucket_hot, (((0,), (1,)), ((), ())), precision=exact_prec
    )
    key_all, value_all = (
        lax.all_gather(key_blocks, "ctx", axis=1, tiled=True),
        lax.all_gather(value_blocks, "ctx", axis=1, tiled=True),
    )
    key_heads_all = key_all.reshape(seq_dev, full_len, H, HD)
    value_heads_all = value_all.reshape(seq_dev, full_len, H, HD)
    base_all = offset_start(query_start, block_len, 0, full_len)
    scores_all = jnp.einsum(
        "sqhd,skhd->shqk", query_heads, key_heads_all, preferred_element_type=single
    )
    scores_all = scores_all + bias_block(rel_bias, base_all, block_len, full_len)[None]
    row_max = jnp.max(scores_all, axis=-1)
    expd = jnp.exp(scores_all - row_max[..., None])
    row_sum = jnp.sum(expd, axis=-1)
    soft_all = expd / row_sum[..., None]
    attn_heads = jnp.einsum(
        "shqk,skhd->sqhd", soft_all.astype(bfloat), value_heads_all, preferred_element_type=single
    )
    attn_exact = jnp.einsum(
        "shqk,skhd->sqhd", soft_all, value_heads_all.astype(single), precision=exact_prec
    )
    attn_rows = attn_heads.reshape(tok_count, model_width).astype(bfloat)
    resid = row_data + jnp.dot(attn_rows, w_output, preferred_element_type=single)
    scale_two = norm_scale(resid)
    normed_two = (resid * scale_two * gain_ffn).astype(bfloat)
    logits = jnp.dot(normed_two, w_router, preferred_element_type=single)
    probs = jax.nn.softmax(logits, axis=-1)
    route_flat = routes.reshape(tok_count)
    route_hot = (route_flat[:, None] == jnp.arange(experts, dtype=jnp.int32)[None, :]).astype(
        jnp.int32
    )
    route_float = route_hot.astype(single)
    gate = jnp.sum(probs * route_float, axis=-1)
    earlier = jnp.tril(jnp.ones((tok_count, tok_count), bfloat), -1)
    counts = jnp.dot(earlier, route_hot.astype(bfloat), preferred_element_type=single)
    slot_index = jnp.sum(counts * route_float, axis=1).astype(jnp.int32)
    target = jnp.where(slot_index < capacity, route_flat * capacity + slot_index, -1)
    dispatch_mat = (
        target[:, None] == jnp.arange(experts * capacity, dtype=jnp.int32)[None, :]
    ).astype(bfloat)
    buffer = (
        contract_rows(dispatch_mat, normed_two)
        .astype(bfloat)
        .reshape(experts, capacity, model_width)
    )
    received = lax.all_to_all(buffer, ("dp", "expert"), split_axis=0, concat_axis=1, tiled=True)
    local_rows = received[0]
    first_full, second_full = (
        lax.all_gather(w_in, "ctx", axis=2, tiled=True),
        lax.all_gather(w_out, "ctx", axis=1, tiled=True),
    )
    first_proj = first_full[0]
    second_proj = second_full[0]
    pre_act = jnp.dot(local_rows, first_proj, preferred_element_type=single)
    hidden_full, act_pull = gelu_with_back(pre_act)
    hidden = hidden_full.astype(bfloat)
    expert_out = jnp.dot(hidden, second_proj, preferred_element_type=single).astype(bfloat)
    returned = lax.all_to_all(
        expert_out[None], ("dp", "expert"), split_axis=1, concat_axis=0, tiled=True
    )
    picked = jnp.dot(
        dispatch_mat,
        returned.reshape(experts * capacity, model_width),
        preferred_element_type=single,
    )
    layer_out = resid + gate[:, None] * picked
    grad_in = cotangent.reshape(tok_count, model_width).astype(single)
    grad_gate = jnp.sum(grad_in * picked, axis=-1)
    grad_picked = (gate[:, None] * grad_in).astype(bfloat)
    grad_buffer = (
        contract_rows(dispatch_mat, grad_picked)
        .astype(bfloat)
        .reshape(experts, capacity, model_width)
    )
    grad_received = lax.all_to_all(
        grad_buffer, ("dp", "expert"), split_axis=0, concat_axis=1, tiled=True
    )
    grad_local = grad_received[0]
    grad_hidden = jnp.dot(grad_local, second_proj.T, preferred_element_type=single)
    grad_pre = act_pull(grad_hidden)[0].astype(bfloat)
    full_second = contract_rows(hidden, grad_local)
    full_first = contract_rows(local_rows, grad_pre)
    grad_first, grad_second = (
        lax.psum_scatter(
            full_first[None].astype(jnp.bfloat16), "ctx", scatter_dimension=2, tiled=True
        ).astype(jnp.float32),
        lax.psum_scatter(
            full_second[None].astype(jnp.bfloat16), "ctx", scatter_dimension=1, tiled=True
        ).astype(jnp.float32),
    )
    grad_rows = jnp.dot(grad_pre, first_proj.T, preferred_element_type=single).astype(bfloat)
    grad_returned = lax.all_to_all(
        grad_rows[None], ("dp", "expert"), split_axis=1, concat_axis=0, tiled=True
    )
    grad_logits = (grad_gate[:, None] * probs * (route_float - gate[:, None])).astype(bfloat)
    grad_router = contract_rows(normed_two, grad_logits)
    grad_normed_two = jnp.dot(
        dispatch_mat,
        grad_returned.reshape(experts * capacity, model_width),
        preferred_element_type=single,
    )
    grad_normed_two = grad_normed_two + jnp.dot(
        grad_logits, w_router.T, preferred_element_type=single
    )
    grad_gain_ffn = jnp.sum(grad_normed_two * resid * scale_two, axis=0)
    grad_resid = grad_in + norm_back(grad_normed_two, resid, scale_two, gain_ffn)
    grad_branch = grad_resid.astype(bfloat)
    grad_output = contract_rows(attn_rows, grad_branch)
    grad_attn = jnp.dot(grad_branch, w_output.T, preferred_element_type=single).astype(bfloat)
    grad_attn_heads = grad_attn.reshape(seq_dev, block_len, H, HD)
    delta_rows = jnp.sum(grad_attn_heads.astype(single) * attn_exact, axis=-1).transpose(0, 2, 1)
    grad_rel = jnp.zeros((H, 2 * full_len - 1), single)
    key_part = lax.all_gather(key_blocks, "ctx", axis=1, tiled=True)
    value_part = lax.all_gather(value_blocks, "ctx", axis=1, tiled=True)
    seg_count = key_part.shape[1]
    key_heads = key_part.reshape(seq_dev, seg_count, H, HD)
    value_heads = value_part.reshape(seq_dev, seg_count, H, HD)
    base = offset_start(query_start, block_len, jnp.int32(0), full_len)
    scores = jnp.einsum("sqhd,skhd->shqk", query_heads, key_heads, preferred_element_type=single)
    scores = scores + bias_block(rel_bias, base, block_len, seg_count)[None]
    soft_weights = jnp.exp(scores - row_max[..., None]) / row_sum[..., None]
    grad_soft = jnp.einsum(
        "sqhd,skhd->shqk", grad_attn_heads, value_heads, preferred_element_type=single
    )
    grad_scores = (soft_weights * (grad_soft - delta_rows[..., None])).astype(bfloat)
    grad_query_acc = jnp.einsum(
        "shqk,skhd->sqhd", grad_scores, key_heads, preferred_element_type=single
    )
    key_term = jnp.einsum(
        "shqk,sqhd->skhd", grad_scores, query_heads, preferred_element_type=single
    ).reshape(seq_dev, seg_count, model_width)
    value_term = jnp.einsum(
        "shqk,sqhd->skhd",
        soft_weights.astype(bfloat),
        grad_attn_heads,
        preferred_element_type=single,
    ).reshape(seq_dev, seg_count, model_width)
    grad_key_all = key_term
    grad_value_all = value_term
    head_scores = jnp.sum(grad_scores.astype(single), axis=0)
    diagonal_sums = bias_grad_block(head_scores, block_len, seg_count)
    grad_rel = lax.dynamic_update_slice_in_dim(grad_rel, diagonal_sums, base, 1)
    grad_query_acc, grad_key_all, grad_value_all, grad_rel = (
        grad_query_acc,
        grad_key_all,
        grad_value_all,
        grad_rel,
    )
    grad_key_own, grad_value_own = (
        lax.psum_scatter(
            grad_key_all.astype(jnp.bfloat16), "ctx", scatter_dimension=1, tiled=True
        ).astype(jnp.float32),
        lax.psum_scatter(
            grad_value_all.astype(jnp.bfloat16), "ctx", scatter_dimension=1, tiled=True
        ).astype(jnp.float32),
    )
    grad_query_rows = grad_query_acc.reshape(tok_count, model_width).astype(bfloat)
    grad_key_rows = grad_key_own.reshape(tok_count, model_width).astype(bfloat)
    grad_value_rows = grad_value_own.reshape(tok_count, model_width).astype(bfloat)
    grad_query_w = contract_rows(normed_one, grad_query_rows)
    grad_key_w = contract_rows(normed_one, grad_key_rows)
    grad_value_w = contract_rows(normed_one, grad_value_rows)
    grad_normed_one = jnp.dot(grad_query_rows, w_query.T, preferred_element_type=single)
    grad_normed_one = grad_normed_one + jnp.dot(
        grad_key_rows, w_key.T, preferred_element_type=single
    )
    grad_normed_one = grad_normed_one + jnp.dot(
        grad_value_rows, w_value.T, preferred_element_type=single
    )
    grad_gain_attn = jnp.sum(grad_normed_one * row_data * scale_one, axis=0)
    grad_tokens = grad_resid + norm_back(grad_normed_one, row_data, scale_one, gain_attn)
    grad_table = lax.dot_general(
        bucket_hot, grad_rel, (((0,), (1,)), ((), ())), precision=exact_prec
    )
    summed = lax.psum(
        (
            grad_gain_attn,
            grad_query_w,
            grad_key_w,
            grad_value_w,
            grad_output,
            grad_table,
            grad_gain_ffn,
            grad_router,
        ),
        ("dp", "ctx", "expert"),
    )
    return (
        layer_out.reshape(seq_dev, block_len, model_width).astype(bfloat),
        grad_tokens.reshape(seq_dev, block_len, model_width).astype(bfloat),
        summed[0],
        summed[1],
        summed[2],
        summed[3],
        summed[4],
        summed[5],
        summed[6],
        summed[7],
        grad_first,
        grad_second,
    )


def solution(mesh):
    placed = (
        P(("dp", "expert"), "ctx", None),
        P(("dp", "expert"), "ctx", None),
        P(("dp", "expert"), "ctx", None),
        P(),
        P(),
        P(),
        P(),
        P(),
        P(),
        P(),
        P(),
        P(),
        P(("dp", "expert"), None, "ctx"),
        P(("dp", "expert"), "ctx", None),
    )
    return jax.shard_map(
        shards,
        mesh=mesh,
        in_specs=placed,
        out_specs=(
            P(("dp", "expert"), "ctx", None),
            P(("dp", "expert"), "ctx", None),
            P(),
            P(),
            P(),
            P(),
            P(),
            P(),
            P(),
            P(),
            P(("dp", "expert"), None, "ctx"),
            P(("dp", "expert"), "ctx", None),
        ),
        check_vma=False,
    )
```

```python
import functools

import jax
import jax.numpy as jnp
from jax import lax
from jax.experimental import pallas as pl
from jax.experimental.pallas import tpu as pltpu
from jax.sharding import PartitionSpec as P

H = 12
HD = 64
NB = 32
PLANE = ("dp", "expert")

epsilon = 1e-06
exact_prec = lax.Precision.HIGHEST
bfloat = jnp.bfloat16
single = jnp.float32
VMEM_LIMIT = 56 * 1024 * 1024


def norm_scale(row_data):
    return lax.rsqrt(jnp.mean(row_data * row_data, axis=-1, keepdims=True) + epsilon)


def norm_back(grad_in, row_data, scale, gain):
    weighted = grad_in * gain
    inner = jnp.mean(weighted * row_data, axis=-1, keepdims=True)
    return scale * weighted - row_data * (scale * scale * scale) * inner


def dot_nn(left, right):
    return lax.dot_general(
        left, right, (((1,), (0,)), ((), ())), preferred_element_type=single
    )


def dot_nt(left, right):
    return lax.dot_general(
        left, right, (((1,), (1,)), ((), ())), preferred_element_type=single
    )


def dot_tn(left, right):
    return lax.dot_general(
        left, right, (((0,), (0,)), ((), ())), preferred_element_type=single
    )


def pack_rows(rows):
    half = rows.shape[0] // 2
    return jnp.concatenate([rows[:half], rows[half:]], axis=1)


def unpack_rows(packed):
    width = packed.shape[1] // 2
    return jnp.concatenate([packed[:, :width], packed[:, width:]], axis=0)


def bias_strip(rel_row, rows, width):
    spread = jnp.broadcast_to(rel_row, (rows, width))
    return pltpu.roll(spread, width - (rows - 1), 1, stride=1, stride_axis=0)


def fold_strip(strip):
    rows = strip.shape[0]
    while rows > 1:
        rows //= 2
        strip = strip[rows:] + pltpu.roll(strip[:rows], rows, 1)
    return strip


def attend_kernel(n, heads, place_ref, *refs):
    blocks = refs[:n]
    gain_ref, w_ref, rel_ref, normed_ref, qkv_ref, lse_ref, out_ref, strip_ref = refs[n:]
    place = place_ref[0]
    block_len = blocks[0].shape[0]
    full_len = n * block_len
    width = heads * HD
    for r in range(n):
        start = pl.multiple_of(lax.rem(place - r + n, n) * block_len, block_len)
        row_data = blocks[r][...].astype(single)
        normed = (row_data * norm_scale(row_data) * gain_ref[...]).astype(bfloat)
        normed_ref[pl.ds(start, block_len), :] = normed
        qkv_ref[pl.ds(start, block_len), :] = dot_nn(normed, w_ref[...]).astype(bfloat)
    for h in range(heads):
        strip_ref[h] = bias_strip(rel_ref[h : h + 1, :], block_len, 2 * full_len)
    lse_ref[...] = jnp.zeros_like(lse_ref)

    def tile(t, carry):
        rows = pl.ds(pl.multiple_of(t * block_len, block_len), block_len)
        skew = pl.ds(pl.multiple_of((n - 1 - t) * block_len, block_len), full_len)
        made = []
        for h in range(heads):
            query = qkv_ref[rows, h * HD : (h + 1) * HD]
            key = qkv_ref[:, width + h * HD : width + (h + 1) * HD]
            value = qkv_ref[:, 2 * width + h * HD : 2 * width + (h + 1) * HD]
            scores = dot_nt(query, key) + strip_ref[h, :, skew]
            top = jnp.max(scores, axis=1, keepdims=True)
            expd = jnp.exp(scores - top)
            total = jnp.sum(expd, axis=1, keepdims=True)
            made.append(dot_nn(expd.astype(bfloat), value) / total)
            lse_ref[rows, h : h + 1] = top + jnp.log(total)
        joined = jnp.concatenate(made, axis=1).astype(bfloat)
        out_ref[lax.rem(t - place + n, n)] = pack_rows(joined)
        return carry

    lax.fori_loop(0, n, tile, 0)


def attend(place, blocks, gain, w_local, rel, heads):
    n = len(blocks)
    block_len, model_width = blocks[0].shape
    full_len = n * block_len
    width = heads * HD
    vmem = pl.BlockSpec(memory_space=pltpu.VMEM)
    return pl.pallas_call(
        functools.partial(attend_kernel, n, heads),
        out_shape=(
            jax.ShapeDtypeStruct((full_len, model_width), bfloat),
            jax.ShapeDtypeStruct((full_len, 3 * width), bfloat),
            jax.ShapeDtypeStruct((full_len, 128), single),
            jax.ShapeDtypeStruct((n, block_len // 2, 2 * width), bfloat),
        ),
        in_specs=[pl.BlockSpec(memory_space=pltpu.SMEM)] + [vmem] * (n + 3),
        out_specs=(vmem,) * 4,
        scratch_shapes=[pltpu.VMEM((heads, block_len, 2 * full_len), single)],
        compiler_params=pltpu.CompilerParams(vmem_limit_bytes=VMEM_LIMIT),
        cost_estimate=pl.CostEstimate(
            flops=2 * full_len * width * (3 * model_width + 2 * full_len),
            bytes_accessed=8 * full_len * model_width,
            transcendentals=heads * full_len * full_len,
        ),
        name="attend",
    )(place, *blocks, gain, w_local, rel)


def attend_back_kernel(n, heads, place_ref, *refs):
    blocks = refs[:n]
    (qkv_ref, lse_ref, rel_ref, w_ref, normed_ref, gain_ref,
     dqkv_ref, part_ref, gain_out_ref, rel_out_ref,
     da_ref, strip_ref, sums_ref, key_acc, value_acc) = refs[n:]
    place = place_ref[0]
    block_len = blocks[0].shape[0] * 2
    full_len = n * block_len
    width = heads * HD
    for r in range(n):
        start = pl.multiple_of(lax.rem(place + r, n) * block_len, block_len)
        da_ref[pl.ds(start, block_len), :] = unpack_rows(blocks[r][...])
    for h in range(heads):
        strip_ref[...] = bias_strip(rel_ref[h : h + 1, :], block_len, 2 * full_len)
        sums_ref[...] = jnp.zeros_like(sums_ref)
        key_acc[...] = jnp.zeros_like(key_acc)
        value_acc[...] = jnp.zeros_like(value_acc)

        def tile(t, carry, h=h):
            rows = pl.ds(pl.multiple_of(t * block_len, block_len), block_len)
            skew = pl.ds(pl.multiple_of((n - 1 - t) * block_len, block_len), full_len)
            query = qkv_ref[rows, h * HD : (h + 1) * HD]
            key = qkv_ref[:, width + h * HD : width + (h + 1) * HD]
            value = qkv_ref[:, 2 * width + h * HD : 2 * width + (h + 1) * HD]
            grad_attn = da_ref[rows, h * HD : (h + 1) * HD]
            scores = dot_nt(query, key) + strip_ref[:, skew]
            soft = jnp.exp(scores - lse_ref[rows, h : h + 1])
            value_acc[...] += dot_tn(grad_attn, soft.astype(bfloat))
            grad_soft = dot_nt(grad_attn, value)
            delta = jnp.sum(soft * grad_soft, axis=1, keepdims=True)
            grad_wide = soft * (grad_soft - delta)
            sums_ref[:, skew] += grad_wide
            grad_scores = grad_wide.astype(bfloat)
            dqkv_ref[rows, h * HD : (h + 1) * HD] = dot_nn(grad_scores, key).astype(bfloat)
            key_acc[...] += dot_tn(query, grad_scores)
            return carry

        lax.fori_loop(0, n, tile, 0)
        dqkv_ref[:, width + h * HD : width + (h + 1) * HD] = key_acc[...].T.astype(bfloat)
        dqkv_ref[:, 2 * width + h * HD : 2 * width + (h + 1) * HD] = (
            value_acc[...].T.astype(bfloat)
        )
        rel_out_ref[h : h + 1, :] = fold_strip(sums_ref[...])
    total = jnp.zeros((1, normed_ref.shape[1]), single)
    for r in range(n):
        start = pl.multiple_of(lax.rem(place + r, n) * block_len, block_len)
        rows = pl.ds(start, block_len)
        part = dot_nt(dqkv_ref[rows, :], w_ref[...])
        total += jnp.sum(part * normed_ref[rows, :].astype(single), axis=0, keepdims=True)
        part_ref[r] = part.astype(bfloat)
    gain_out_ref[...] = total / gain_ref[...]


def attend_back(place, blocks, qkv, lse, rel, w_local, normed, gain, heads):
    n = len(blocks)
    full_len, model_width = normed.shape
    block_len = full_len // n
    width = heads * HD
    vmem = pl.BlockSpec(memory_space=pltpu.VMEM)
    return pl.pallas_call(
        functools.partial(attend_back_kernel, n, heads),
        out_shape=(
            jax.ShapeDtypeStruct((full_len, 3 * width), bfloat),
            jax.ShapeDtypeStruct((n, block_len, model_width), bfloat),
            jax.ShapeDtypeStruct((1, model_width), single),
            jax.ShapeDtypeStruct((heads, 2 * full_len), single),
        ),
        in_specs=[pl.BlockSpec(memory_space=pltpu.SMEM)] + [vmem] * (n + 6),
        out_specs=(vmem,) * 4,
        scratch_shapes=[
            pltpu.VMEM((full_len, width), bfloat),
            pltpu.VMEM((block_len, 2 * full_len), single),
            pltpu.VMEM((block_len, 2 * full_len), single),
            pltpu.VMEM((HD, full_len), single),
            pltpu.VMEM((HD, full_len), single),
        ],
        compiler_params=pltpu.CompilerParams(vmem_limit_bytes=VMEM_LIMIT),
        cost_estimate=pl.CostEstimate(
            flops=2 * full_len * width * (3 * model_width + 5 * full_len),
            bytes_accessed=8 * full_len * model_width,
            transcendentals=heads * full_len * full_len,
        ),
        name="attend_back",
    )(place, *blocks, qkv, lse, rel, w_local, normed, gain)


def shift(block, by):
    n = lax.axis_size("ctx")
    return lax.ppermute(block, "ctx", [(i, (i + by) % n) for i in range(n)])


def swap_plane(block, mask):
    count = lax.axis_size(PLANE)
    return lax.ppermute(block, PLANE, [(i, i ^ mask) for i in range(count)])


def to_plane(blocks):
    return lax.all_to_all(blocks, PLANE, split_axis=0, concat_axis=0, tiled=True)


def sum_plane(piece):
    count = lax.axis_size(PLANE)
    rows, width = piece.shape
    parts = to_plane(piece.astype(bfloat).reshape(count, rows // count, width))
    return jnp.sum(parts.astype(single), axis=0).astype(bfloat)


def gather_all(piece):
    n = lax.axis_size("ctx")
    count = lax.axis_size(PLANE)
    stack = jnp.stack([piece] + [shift(piece, r) for r in range(1, n)])
    core = lax.axis_size("expert")
    held = {0: stack}
    for mask in range(1, count):
        if not mask & core:
            held[mask] = swap_plane(stack, mask)
    for mask in list(held):
        held[mask | core] = swap_plane(held[mask], core)
    return [held[mask] for mask in range(count)]


def place_late_kernel(count, n, width, spot_ref, *refs):
    spot, place = spot_ref[0], spot_ref[1]
    ins, outs, extra_ref = refs[:count], refs[count : count + 3], refs[count + 3]
    step = ins[0].shape[1]
    for mask in range(count):
        rows = pl.ds(pl.multiple_of((spot ^ mask) * step, step), step)
        for c in range(n):
            block = ins[mask][lax.rem(place - c + n, n)].astype(single)
            for i in range(3):
                outs[i][rows, c * width : (c + 1) * width] = block[:, i * width : (i + 1) * width]
            extra_ref[c, rows, :] = block[:, 3 * width :]


def place_output_kernel(count, n, spot_ref, *refs):
    spot, place = spot_ref[0], spot_ref[1]
    step = refs[0].shape[1]
    for mask in range(count):
        for c in range(n):
            start = (c * count + (spot ^ mask)) * step
            block = refs[mask][lax.rem(place - c + n, n)]
            refs[count][pl.ds(pl.multiple_of(start, step), step), :] = block.astype(single)


def placed(kernel, spots, held, shapes):
    vmem = pl.BlockSpec(memory_space=pltpu.VMEM)
    return pl.pallas_call(
        kernel,
        out_shape=[jax.ShapeDtypeStruct(s, single) for s in shapes],
        in_specs=[pl.BlockSpec(memory_space=pltpu.SMEM)] + [vmem] * len(held),
        out_specs=[vmem] * len(shapes),
        compiler_params=pltpu.CompilerParams(vmem_limit_bytes=VMEM_LIMIT),
        cost_estimate=pl.CostEstimate(flops=0, bytes_accessed=12_000_000, transcendentals=0),
        name="placed",
    )(spots, *held)


def gather_late(piece, width, model_width):
    n = lax.axis_size("ctx")
    count = lax.axis_size(PLANE)
    if piece.shape[0] % 8:
        whole = lax.all_gather(lax.all_gather(piece, "ctx"), PLANE).astype(single)
        whole = whole.transpose(1, 0, 2, 3).reshape(n, model_width, -1)
        own = [whole[:, :, i * width : (i + 1) * width] for i in range(3)]
        own = [o.transpose(1, 0, 2).reshape(model_width, n * width) for o in own]
        return own + [whole[:, :, 3 * width :]]
    spots = jnp.stack([lax.axis_index(PLANE), lax.axis_index("ctx")]).astype(jnp.int32)
    shapes = [(model_width, n * width)] * 3 + [(n, model_width, piece.shape[1] - 3 * width)]
    kernel = functools.partial(place_late_kernel, count, n, width)
    return placed(kernel, spots, gather_all(piece), shapes)


def gather_output(piece):
    n = lax.axis_size("ctx")
    count = lax.axis_size(PLANE)
    rows = n * count * piece.shape[0]
    if piece.shape[0] % 8:
        whole = lax.all_gather(lax.all_gather(piece, "ctx"), PLANE).astype(single)
        return whole.transpose(1, 0, 2, 3).reshape(rows, -1)
    spots = jnp.stack([lax.axis_index(PLANE), lax.axis_index("ctx")]).astype(jnp.int32)
    kernel = functools.partial(place_output_kernel, count, n)
    return placed(kernel, spots, gather_all(piece), [(rows, piece.shape[1])])[0]


def shards(
    tokens,
    cotangent,
    routes,
    buckets,
    gain_attn,
    w_query,
    w_key,
    w_value,
    w_output,
    bias_table,
    gain_ffn,
    w_router,
    w_in,
    w_out,
):
    seq_dev, block_len, model_width = tokens.shape
    n = lax.axis_size("ctx")
    experts = lax.axis_size(PLANE)
    heads = H // n
    width = heads * HD
    full_len = block_len * n
    tok_count = seq_dev * block_len
    capacity = max(2, (5 * tok_count + 4 * experts - 1) // (4 * experts))
    slots = experts * capacity
    place = lax.axis_index("ctx")
    spot = lax.axis_index(PLANE)
    place_in = place.astype(jnp.int32).reshape(1)

    block = tokens.reshape(tok_count, model_width)
    blocks = [block] + [shift(block, r) for r in range(1, n)]
    row_data = block.astype(single)

    own_heads = [
        lax.dynamic_slice_in_dim(w, place * width, width, 1) for w in (w_query, w_key, w_value)
    ]
    w_local = jnp.concatenate(own_heads, axis=1)
    turned = [
        lax.dynamic_slice_in_dim(w_output, (place - r) % n * width, width, 0) for r in range(n)
    ]
    w_turned = jnp.concatenate(turned, axis=0)
    bucket_hot = (buckets[:, None] == jnp.arange(NB, dtype=jnp.int32)[None, :]).astype(single)
    table_local = lax.dynamic_slice_in_dim(bias_table, place * heads, heads, 1)
    rel = lax.dot_general(
        table_local, bucket_hot, (((0,), (1,)), ((), ())), precision=exact_prec
    )
    rel = jnp.pad(rel, ((0, 0), (0, 1)))
    route_flat = routes.reshape(tok_count)
    route_hot = (
        route_flat[:, None] == jnp.arange(experts, dtype=jnp.int32)[None, :]
    ).astype(bfloat)
    earlier = jnp.tril(jnp.ones((tok_count, tok_count), bfloat), -1)
    counts = dot_nn(earlier, route_hot)
    slot_index = jnp.sum(counts * route_hot.astype(single), axis=1).astype(jnp.int32)
    target = jnp.where(slot_index < capacity, route_flat * capacity + slot_index, -1)
    dispatch_mat = (target[:, None] == jnp.arange(slots, dtype=jnp.int32)[None, :]).astype(bfloat)

    grad_block = cotangent.reshape(tok_count, model_width)
    grad_in = grad_block.astype(single)
    grad_sent = dot_tn(dispatch_mat, grad_block).astype(bfloat)
    grad_near = to_plane(grad_sent.reshape(experts, capacity, model_width))
    grad_near = grad_near.reshape(slots, model_width)

    normed_all, qkv, lse, attn_parts = attend(
        place_in, blocks, gain_attn.reshape(1, -1), w_local, rel, heads
    )
    tied = lax.optimization_barrier((attn_parts, grad_near, w_in[0], w_out[0]))
    attn_parts, grad_near, first_own, second_own = tied
    attn_turned = [attn_parts[0]] + [shift(attn_parts[r], r) for r in range(1, n)]
    attn_turned = [unpack_rows(a) for a in attn_turned]
    attn_rows = jnp.concatenate(attn_turned, axis=1)

    pair = [(i, i ^ 1) for i in range(n)]
    first_other = lax.ppermute(first_own, "ctx", pair)
    second_other = lax.ppermute(second_own, "ctx", pair)
    grad_far = shift(grad_near, n // 2)

    resid = row_data + dot_nn(attn_rows, w_turned)
    scale_two = norm_scale(resid)
    normed_two = (resid * scale_two * gain_ffn).astype(bfloat)
    sent = dot_tn(dispatch_mat, normed_two).astype(bfloat)
    near = to_plane(sent.reshape(experts, capacity, model_width)).reshape(slots, model_width)
    far = shift(near, n // 2)

    def expert(rows, grad_rows):
        logits = dot_nn(rows, w_router)
        probs = jax.nn.softmax(logits, axis=-1)
        hot = (jnp.arange(experts) == spot).astype(single)[None, :]
        gate = jnp.sum(probs * hot, axis=-1, keepdims=True)
        scaled = (gate * grad_rows.astype(single)).astype(bfloat)
        made, back, hidden_parts, pre_parts = 0.0, 0.0, [], []
        grad_gate = 0.0
        for first, second in ((first_own, second_own), (first_other, second_other)):
            pre = dot_nn(rows, first)
            normal = 0.5 * (1.0 + lax.erf(pre * (0.5**0.5)))
            density = jnp.exp(-0.5 * pre * pre) * 0.3989422804014327
            hidden = pre * normal
            pull = dot_nt(grad_rows, second)
            grad_gate = grad_gate + jnp.sum(hidden * pull, axis=-1, keepdims=True)
            grad_pre = (gate * pull * (normal + pre * density)).astype(bfloat)
            hidden = hidden.astype(bfloat)
            made = made + dot_nn(hidden, second)
            back = back + dot_nt(grad_pre, first)
            hidden_parts.append(hidden)
            pre_parts.append(grad_pre)
        grad_logits = (grad_gate * probs * (hot - gate)).astype(bfloat)
        back = back + dot_nt(grad_logits, w_router)
        return made, back, hidden_parts, pre_parts, grad_logits, scaled

    near_made, near_back, near_hidden, near_pre, near_logits, near_scaled = expert(near, grad_near)
    far_made, far_back, far_hidden, far_pre, far_logits, far_scaled = expert(far, grad_far)
    back_sum = near_back + shift(far_back.astype(bfloat), n // 2).astype(single)
    back_home = to_plane(back_sum.astype(bfloat).reshape(experts, capacity, model_width))
    made_sum = near_made + shift(far_made.astype(bfloat), n // 2).astype(single)
    made_home = to_plane(made_sum.astype(bfloat).reshape(experts, capacity, model_width))

    rows_two = jnp.concatenate([near, far], axis=0)
    scaled_two = jnp.concatenate([near_scaled, far_scaled], axis=0)
    hidden_two = [jnp.concatenate(p, axis=0) for p in zip(near_hidden, far_hidden)]
    pre_two = [jnp.concatenate(p, axis=0) for p in zip(near_pre, far_pre)]
    logits_two = jnp.concatenate([near_logits, far_logits], axis=0)
    first_sent = lax.ppermute(dot_tn(rows_two, pre_two[1]).astype(bfloat), "ctx", pair)
    second_sent = lax.ppermute(dot_tn(hidden_two[1], scaled_two).astype(bfloat), "ctx", pair)
    grad_first = dot_tn(rows_two, pre_two[0]) + first_sent.astype(single)
    grad_second = dot_tn(hidden_two[0], scaled_two) + second_sent.astype(single)
    grad_router = dot_tn(rows_two, logits_two)

    grad_normed_two = dot_nn(dispatch_mat, back_home.reshape(slots, model_width))
    grad_gain_ffn = jnp.sum(grad_normed_two * resid * scale_two, axis=0)
    grad_resid = grad_in + norm_back(grad_normed_two, resid, scale_two, gain_ffn)
    grad_branch = grad_resid.astype(bfloat)
    grad_attn = dot_nt(grad_branch, w_turned).astype(bfloat)
    attn_grads = [
        pack_rows(grad_attn[:, r * width : (r + 1) * width]) for r in range(n)
    ]
    attn_grads = [attn_grads[0]] + [shift(attn_grads[r], n - r) for r in range(1, n)]

    grad_output = dot_tn(attn_rows, grad_branch).astype(bfloat).reshape(n, width, model_width)
    slices = [grad_output[0]] + [shift(grad_output[r], n - r) for r in range(1, n)]
    output_slice = sum(s.astype(single) for s in slices)
    output_all = gather_output(sum_plane(output_slice))

    gate = jnp.sum(
        jax.nn.softmax(dot_nn(normed_two, w_router), axis=-1) * route_hot.astype(single), axis=-1
    )
    picked = dot_nn(dispatch_mat, made_home.reshape(slots, model_width))
    layer_out = resid + gate[:, None] * picked

    grad_qkv, parts, grad_gain_part, grad_rel = attend_back(
        place_in, attn_grads, qkv, lse, rel, w_local, normed_all, gain_attn.reshape(1, -1), heads
    )
    table_part = lax.dot_general(
        bucket_hot, grad_rel[:, :-1], (((0,), (1,)), ((), ())), precision=exact_prec
    )
    extra = jnp.concatenate(
        [
            grad_gain_part.reshape(model_width, 1),
            grad_gain_ffn.reshape(model_width, 1),
            jnp.pad(table_part, ((0, model_width - NB), (0, 0))),
            grad_router,
        ],
        axis=1,
    )
    extra = jnp.pad(extra, ((0, 0), (0, -(3 * width + extra.shape[1]) % 128)))
    late = jnp.concatenate([dot_tn(normed_all, grad_qkv), extra], axis=1)
    grads = gather_late(sum_plane(late), width, model_width)
    parts_in = [parts[0]] + [shift(parts[r], r) for r in range(1, n)]
    grad_normed_one = sum(p.astype(single) for p in parts_in)
    scale_one = norm_scale(row_data)
    grad_tokens = grad_resid + norm_back(grad_normed_one, row_data, scale_one, gain_attn)

    extra = grads[3]
    totals = jnp.sum(extra, axis=0)
    grad_gain_attn = totals[:, 0]
    grad_gain_ffn = totals[:, 1]
    grad_table = extra[:, :NB, 2 : 2 + heads].transpose(1, 0, 2).reshape(NB, H)
    grad_router = totals[:, 2 + heads : 2 + heads + experts]
    return (
        layer_out.reshape(seq_dev, block_len, model_width).astype(bfloat),
        grad_tokens.reshape(seq_dev, block_len, model_width).astype(bfloat),
        grad_gain_attn,
        grads[0],
        grads[1],
        grads[2],
        output_all,
        grad_table,
        grad_gain_ffn,
        grad_router,
        grad_first[None],
        grad_second[None],
    )


def solution(mesh):
    spread = P(("dp", "expert"), "ctx", None)
    first = P(("dp", "expert"), None, "ctx")
    return jax.shard_map(
        shards,
        mesh=mesh,
        in_specs=(spread,) * 3 + (P(),) * 9 + (first, spread),
        out_specs=(spread,) * 2 + (P(),) * 8 + (first, spread),
        check_vma=False,
    )
```

```python
import functools

import jax
import jax.numpy as jnp
from jax import lax
from jax.experimental import pallas as pl
from jax.experimental.pallas import tpu as pltpu
from jax.sharding import PartitionSpec as P

H = 12
HD = 64
NB = 32
PLANE = ("dp", "expert")

epsilon = 1e-06
exact_prec = lax.Precision.HIGHEST
bfloat = jnp.bfloat16
single = jnp.float32
VMEM_LIMIT = 56 * 1024 * 1024


def norm_scale(row_data):
    return lax.rsqrt(jnp.mean(row_data * row_data, axis=-1, keepdims=True) + epsilon)


def norm_back(grad_in, row_data, scale, gain):
    weighted = grad_in * gain
    inner = jnp.mean(weighted * row_data, axis=-1, keepdims=True)
    return scale * weighted - row_data * (scale * scale * scale) * inner


def dot_nn(left, right):
    return lax.dot_general(
        left, right, (((1,), (0,)), ((), ())), preferred_element_type=single
    )


def dot_nt(left, right):
    return lax.dot_general(
        left, right, (((1,), (1,)), ((), ())), preferred_element_type=single
    )


def dot_tn(left, right):
    return lax.dot_general(
        left, right, (((0,), (0,)), ((), ())), preferred_element_type=single
    )


def pack_rows(rows):
    half = rows.shape[0] // 2
    return jnp.concatenate([rows[:half], rows[half:]], axis=1)


def unpack_rows(packed):
    width = packed.shape[1] // 2
    return jnp.concatenate([packed[:, :width], packed[:, width:]], axis=0)


def bias_strip(rel_row, rows, width):
    spread = jnp.broadcast_to(rel_row, (rows, width))
    return pltpu.roll(spread, width - (rows - 1), 1, stride=1, stride_axis=0)


def fold_strip(strip):
    rows = strip.shape[0]
    while rows > 1:
        rows //= 2
        strip = strip[rows:] + pltpu.roll(strip[:rows], rows, 1)
    return strip


def attend_kernel(n, heads, place_ref, *refs):
    blocks = refs[:n]
    gain_ref, w_ref, rel_ref, normed_ref, qkv_ref, lse_ref, out_ref, strip_ref = refs[n:]
    place = place_ref[0]
    block_len = blocks[0].shape[0]
    full_len = n * block_len
    width = heads * HD
    for r in range(n):
        start = pl.multiple_of(lax.rem(place - r + n, n) * block_len, block_len)
        row_data = blocks[r][...].astype(single)
        normed = (row_data * norm_scale(row_data) * gain_ref[...]).astype(bfloat)
        normed_ref[pl.ds(start, block_len), :] = normed
        qkv_ref[pl.ds(start, block_len), :] = dot_nn(normed, w_ref[...]).astype(bfloat)
    for h in range(heads):
        strip_ref[h] = bias_strip(rel_ref[h : h + 1, :], block_len, 2 * full_len)
    lse_ref[...] = jnp.zeros_like(lse_ref)

    def tile(t, carry):
        rows = pl.ds(pl.multiple_of(t * block_len, block_len), block_len)
        skew = pl.ds(pl.multiple_of((n - 1 - t) * block_len, block_len), full_len)
        made = []
        for h in range(heads):
            query = qkv_ref[rows, h * HD : (h + 1) * HD]
            key = qkv_ref[:, width + h * HD : width + (h + 1) * HD]
            value = qkv_ref[:, 2 * width + h * HD : 2 * width + (h + 1) * HD]
            scores = dot_nt(query, key) + strip_ref[h, :, skew]
            top = jnp.max(scores, axis=1, keepdims=True)
            expd = jnp.exp(scores - top)
            total = jnp.sum(expd, axis=1, keepdims=True)
            made.append(dot_nn(expd.astype(bfloat), value) / total)
            lse_ref[rows, h : h + 1] = top + jnp.log(total)
        joined = jnp.concatenate(made, axis=1).astype(bfloat)
        out_ref[lax.rem(t - place + n, n)] = pack_rows(joined)
        return carry

    lax.fori_loop(0, n, tile, 0)


def attend(place, blocks, gain, w_local, rel, heads):
    n = len(blocks)
    block_len, model_width = blocks[0].shape
    full_len = n * block_len
    width = heads * HD
    vmem = pl.BlockSpec(memory_space=pltpu.VMEM)
    return pl.pallas_call(
        functools.partial(attend_kernel, n, heads),
        out_shape=(
            jax.ShapeDtypeStruct((full_len, model_width), bfloat),
            jax.ShapeDtypeStruct((full_len, 3 * width), bfloat),
            jax.ShapeDtypeStruct((full_len, 128), single),
            jax.ShapeDtypeStruct((n, block_len // 2, 2 * width), bfloat),
        ),
        in_specs=[pl.BlockSpec(memory_space=pltpu.SMEM)] + [vmem] * (n + 3),
        out_specs=(vmem,) * 4,
        scratch_shapes=[pltpu.VMEM((heads, block_len, 2 * full_len), single)],
        compiler_params=pltpu.CompilerParams(vmem_limit_bytes=VMEM_LIMIT),
        cost_estimate=pl.CostEstimate(
            flops=2 * full_len * width * (3 * model_width + 2 * full_len),
            bytes_accessed=8 * full_len * model_width,
            transcendentals=heads * full_len * full_len,
        ),
        name="attend",
    )(place, *blocks, gain, w_local, rel)


def attend_back_kernel(n, heads, place_ref, *refs):
    blocks = refs[:n]
    (qkv_ref, lse_ref, rel_ref, w_ref, normed_ref, gain_ref, buckets_ref, more_ref,
     part_ref, late_ref,
     da_ref, strip_ref, sums_ref, key_acc, value_acc, dqkv_ref, rel_out_ref) = refs[n:]
    place = place_ref[0]
    block_len = blocks[0].shape[0] * 2
    full_len = n * block_len
    width = heads * HD
    for r in range(n):
        start = pl.multiple_of(lax.rem(place + r, n) * block_len, block_len)
        da_ref[pl.ds(start, block_len), :] = unpack_rows(blocks[r][...])
    for h in range(heads):
        strip_ref[...] = bias_strip(rel_ref[h : h + 1, :], block_len, 2 * full_len)
        sums_ref[...] = jnp.zeros_like(sums_ref)
        key_acc[...] = jnp.zeros_like(key_acc)
        value_acc[...] = jnp.zeros_like(value_acc)

        def tile(t, carry, h=h):
            rows = pl.ds(pl.multiple_of(t * block_len, block_len), block_len)
            skew = pl.ds(pl.multiple_of((n - 1 - t) * block_len, block_len), full_len)
            query = qkv_ref[rows, h * HD : (h + 1) * HD]
            key = qkv_ref[:, width + h * HD : width + (h + 1) * HD]
            value = qkv_ref[:, 2 * width + h * HD : 2 * width + (h + 1) * HD]
            grad_attn = da_ref[rows, h * HD : (h + 1) * HD]
            scores = dot_nt(query, key) + strip_ref[:, skew]
            soft = jnp.exp(scores - lse_ref[rows, h : h + 1])
            value_acc[...] += dot_tn(grad_attn, soft.astype(bfloat))
            grad_soft = dot_nt(grad_attn, value)
            delta = jnp.sum(soft * grad_soft, axis=1, keepdims=True)
            grad_wide = soft * (grad_soft - delta)
            sums_ref[:, skew] += grad_wide
            grad_scores = grad_wide.astype(bfloat)
            dqkv_ref[rows, h * HD : (h + 1) * HD] = dot_nn(grad_scores, key).astype(bfloat)
            key_acc[...] += dot_tn(query, grad_scores)
            return carry

        lax.fori_loop(0, n, tile, 0)
        dqkv_ref[:, width + h * HD : width + (h + 1) * HD] = key_acc[...].T.astype(bfloat)
        dqkv_ref[:, 2 * width + h * HD : 2 * width + (h + 1) * HD] = (
            value_acc[...].T.astype(bfloat)
        )
        rel_out_ref[h : h + 1, :] = fold_strip(sums_ref[...])
    model_width = normed_ref.shape[1]
    total = jnp.zeros((1, model_width), single)
    for r in range(n):
        start = pl.multiple_of(lax.rem(place + r, n) * block_len, block_len)
        rows = pl.ds(start, block_len)
        part = dot_nt(dqkv_ref[rows, :], w_ref[...])
        total += jnp.sum(part * normed_ref[rows, :].astype(single), axis=0, keepdims=True)
        part_ref[r] = part.astype(bfloat)
    late_ref[:, : 3 * width] = dot_tn(normed_ref[...], dqkv_ref[...]).astype(bfloat)
    kinds = lax.broadcasted_iota(jnp.int32, (NB, 2 * full_len), 0)
    hot = (kinds == buckets_ref[...]).astype(single)
    table = lax.dot_general(
        rel_out_ref[...], hot, (((1,), (1,)), ((), ())),
        precision=exact_prec, preferred_element_type=single,
    )
    table = jnp.concatenate([table, jnp.zeros((heads, model_width - NB), single)], axis=1)
    extra = jnp.concatenate([total / gain_ref[...], table, more_ref[...]], axis=0)
    late_ref[:, 3 * width :] = extra.T.astype(bfloat)


def attend_back(place, blocks, qkv, lse, rel, w_local, normed, gain, buckets, more, heads):
    n = len(blocks)
    full_len, model_width = normed.shape
    block_len = full_len // n
    width = heads * HD
    late_width = 3 * width + 1 + heads + more.shape[0]
    vmem = pl.BlockSpec(memory_space=pltpu.VMEM)
    return pl.pallas_call(
        functools.partial(attend_back_kernel, n, heads),
        out_shape=(
            jax.ShapeDtypeStruct((n, block_len, model_width), bfloat),
            jax.ShapeDtypeStruct((model_width, late_width), bfloat),
        ),
        in_specs=[pl.BlockSpec(memory_space=pltpu.SMEM)] + [vmem] * (n + 8),
        out_specs=(vmem,) * 2,
        scratch_shapes=[
            pltpu.VMEM((full_len, width), bfloat),
            pltpu.VMEM((block_len, 2 * full_len), single),
            pltpu.VMEM((block_len, 2 * full_len), single),
            pltpu.VMEM((HD, full_len), single),
            pltpu.VMEM((HD, full_len), single),
            pltpu.VMEM((full_len, 3 * width), bfloat),
            pltpu.VMEM((heads, 2 * full_len), single),
        ],
        compiler_params=pltpu.CompilerParams(vmem_limit_bytes=VMEM_LIMIT),
        cost_estimate=pl.CostEstimate(
            flops=2 * full_len * width * (6 * model_width + 5 * full_len),
            bytes_accessed=8 * full_len * model_width,
            transcendentals=heads * full_len * full_len,
        ),
        name="attend_back",
    )(place, *blocks, qkv, lse, rel, w_local, normed, gain, buckets, more)


def shift(block, by):
    n = lax.axis_size("ctx")
    return lax.ppermute(block, "ctx", [(i, (i + by) % n) for i in range(n)])


def swap_plane(block, mask):
    count = lax.axis_size(PLANE)
    return lax.ppermute(block, PLANE, [(i, i ^ mask) for i in range(count)])


def to_plane(blocks):
    return lax.all_to_all(blocks, PLANE, split_axis=0, concat_axis=0, tiled=True)


def sum_first(parts):
    return jnp.sum(parts.astype(single), axis=0).astype(bfloat)


def gather_ctx(piece):
    n = lax.axis_size("ctx")
    return jnp.stack([piece] + [shift(piece, r) for r in range(1, n)])


def gather_chips(stack):
    count = lax.axis_size(PLANE)
    core = lax.axis_size("expert")
    return {mask: swap_plane(stack, mask) if mask else stack for mask in range(count) if not mask & core}


def gather_cores(held):
    core = lax.axis_size("expert")
    held = {**held, **{mask | core: swap_plane(held[mask], core) for mask in held}}
    return [held[mask] for mask in sorted(held)]


def tied(*arrays):
    return lax.optimization_barrier(arrays)


def place_late_kernel(count, n, width, spot_ref, *refs):
    spot, place = spot_ref[0], spot_ref[1]
    ins, outs, extra_ref = refs[:count], refs[count : count + 3], refs[count + 3]
    step = ins[0].shape[1]
    for mask in range(count):
        rows = pl.ds(pl.multiple_of((spot ^ mask) * step, step), step)
        for c in range(n):
            block = ins[mask][lax.rem(place - c + n, n)].astype(single)
            for i in range(3):
                outs[i][rows, c * width : (c + 1) * width] = block[:, i * width : (i + 1) * width]
            extra_ref[c, rows, :] = block[:, 3 * width :]


def place_output_kernel(count, n, spot_ref, *refs):
    spot, place = spot_ref[0], spot_ref[1]
    step = refs[0].shape[1]
    for mask in range(count):
        for c in range(n):
            start = (c * count + (spot ^ mask)) * step
            block = refs[mask][lax.rem(place - c + n, n)]
            refs[count][pl.ds(pl.multiple_of(start, step), step), :] = block.astype(single)


def placed(kernel, spots, held, shapes):
    vmem = pl.BlockSpec(memory_space=pltpu.VMEM)
    return pl.pallas_call(
        kernel,
        out_shape=[jax.ShapeDtypeStruct(s, single) for s in shapes],
        in_specs=[pl.BlockSpec(memory_space=pltpu.SMEM)] + [vmem] * len(held),
        out_specs=[vmem] * len(shapes),
        compiler_params=pltpu.CompilerParams(vmem_limit_bytes=VMEM_LIMIT),
        cost_estimate=pl.CostEstimate(flops=0, bytes_accessed=12_000_000, transcendentals=0),
        name="placed",
    )(spots, *held)


def spots():
    return jnp.stack([lax.axis_index(PLANE), lax.axis_index("ctx")]).astype(jnp.int32)


def place_late(held, width, model_width):
    n, step, wide = held[0].shape
    if step % 8:
        place, spot = lax.axis_index("ctx"), lax.axis_index(PLANE)
        whole = jnp.zeros((n, model_width, wide), single)
        for mask, stack in enumerate(held):
            for r in range(n):
                where = ((place - r) % n, (spot ^ mask) * step, 0)
                whole = lax.dynamic_update_slice(whole, stack[r : r + 1].astype(single), where)
        own = [whole[:, :, i * width : (i + 1) * width] for i in range(3)]
        own = [o.transpose(1, 0, 2).reshape(model_width, n * width) for o in own]
        return own + [whole[:, :, 3 * width :]]
    shapes = [(model_width, n * width)] * 3 + [(n, model_width, wide - 3 * width)]
    kernel = functools.partial(place_late_kernel, len(held), n, width)
    return placed(kernel, spots(), held, shapes)


def place_output(held):
    n, step, wide = held[0].shape
    count = len(held)
    if step % 8:
        place, spot = lax.axis_index("ctx"), lax.axis_index(PLANE)
        whole = jnp.zeros((n, count * step, wide), single)
        for mask, stack in enumerate(held):
            for r in range(n):
                where = ((place - r) % n, (spot ^ mask) * step, 0)
                whole = lax.dynamic_update_slice(whole, stack[r : r + 1].astype(single), where)
        return whole.reshape(n * count * step, wide)
    kernel = functools.partial(place_output_kernel, count, n)
    return placed(kernel, spots(), held, [(n * count * step, wide)])[0]


def shards(
    tokens,
    cotangent,
    routes,
    buckets,
    gain_attn,
    w_query,
    w_key,
    w_value,
    w_output,
    bias_table,
    gain_ffn,
    w_router,
    w_in,
    w_out,
):
    seq_dev, block_len, model_width = tokens.shape
    n = lax.axis_size("ctx")
    experts = lax.axis_size(PLANE)
    heads = H // n
    width = heads * HD
    full_len = block_len * n
    tok_count = seq_dev * block_len
    capacity = max(2, (5 * tok_count + 4 * experts - 1) // (4 * experts))
    slots = experts * capacity
    place = lax.axis_index("ctx")
    spot = lax.axis_index(PLANE)
    place_in = place.astype(jnp.int32).reshape(1)

    block = tokens.reshape(tok_count, model_width)
    blocks = [block] + [shift(block, r) for r in range(1, n)]
    row_data = block.astype(single)

    own_heads = [
        lax.dynamic_slice_in_dim(w, place * width, width, 1) for w in (w_query, w_key, w_value)
    ]
    w_local = jnp.concatenate(own_heads, axis=1)
    turned = [
        lax.dynamic_slice_in_dim(w_output, (place - r) % n * width, width, 0) for r in range(n)
    ]
    w_turned = jnp.concatenate(turned, axis=0)
    bucket_hot = (buckets[:, None] == jnp.arange(NB, dtype=jnp.int32)[None, :]).astype(single)
    table_local = lax.dynamic_slice_in_dim(bias_table, place * heads, heads, 1)
    rel = lax.dot_general(
        table_local, bucket_hot, (((0,), (1,)), ((), ())), precision=exact_prec
    )
    rel = jnp.pad(rel, ((0, 0), (0, 1)))
    route_flat = routes.reshape(tok_count)
    route_hot = (
        route_flat[:, None] == jnp.arange(experts, dtype=jnp.int32)[None, :]
    ).astype(bfloat)
    earlier = jnp.tril(jnp.ones((tok_count, tok_count), bfloat), -1)
    counts = dot_nn(earlier, route_hot)
    slot_index = jnp.sum(counts * route_hot.astype(single), axis=1).astype(jnp.int32)
    target = jnp.where(slot_index < capacity, route_flat * capacity + slot_index, -1)
    dispatch_mat = (target[:, None] == jnp.arange(slots, dtype=jnp.int32)[None, :]).astype(bfloat)

    grad_block = cotangent.reshape(tok_count, model_width)
    grad_in = grad_block.astype(single)
    grad_sent = dot_tn(dispatch_mat, grad_block).astype(bfloat)
    grad_near = to_plane(grad_sent.reshape(experts, capacity, model_width))
    grad_near = grad_near.reshape(slots, model_width)

    pair = [(i, i ^ 1) for i in range(n)]
    first_own, second_own = w_in[0], w_out[0]
    half = model_width // 2
    *blocks, first_own, second_own, grad_near = tied(*blocks, first_own, second_own, grad_near)
    first_top = lax.ppermute(first_own[:half], "ctx", pair)
    first_low = lax.ppermute(first_own[half:], "ctx", pair)
    second_other = lax.ppermute(second_own, "ctx", pair)
    grad_far = shift(grad_near, n // 2)

    normed_all, qkv, lse, attn_parts = attend(
        place_in, blocks, gain_attn.reshape(1, -1), w_local, rel, heads
    )
    attn_parts, first_top = tied(attn_parts, first_top)
    attn_turned = [attn_parts[0]] + [shift(attn_parts[r], r) for r in range(1, n)]
    *attn_turned, first_low = tied(*attn_turned, first_low)
    first_other = jnp.concatenate([first_top, first_low], axis=0)
    attn_turned = [unpack_rows(a) for a in attn_turned]
    attn_rows = jnp.concatenate(attn_turned, axis=1)

    resid = row_data + dot_nn(attn_rows, w_turned)
    scale_two = norm_scale(resid)
    normed_two = (resid * scale_two * gain_ffn).astype(bfloat)
    sent = dot_tn(dispatch_mat, normed_two).astype(bfloat)
    near = to_plane(sent.reshape(experts, capacity, model_width)).reshape(slots, model_width)
    near, grad_far = tied(near, grad_far)
    far = shift(near, n // 2)

    def expert(rows, grad_rows):
        logits = dot_nn(rows, w_router)
        probs = jax.nn.softmax(logits, axis=-1)
        hot = (jnp.arange(experts) == spot).astype(single)[None, :]
        gate = jnp.sum(probs * hot, axis=-1, keepdims=True)
        scaled = (gate * grad_rows.astype(single)).astype(bfloat)
        made, back, hidden_parts, pre_parts = 0.0, 0.0, [], []
        grad_gate = 0.0
        for first, second in ((first_own, second_own), (first_other, second_other)):
            pre = dot_nn(rows, first)
            normal = 0.5 * (1.0 + lax.erf(pre * (0.5**0.5)))
            density = jnp.exp(-0.5 * pre * pre) * 0.3989422804014327
            hidden = pre * normal
            pull = dot_nt(grad_rows, second)
            grad_gate = grad_gate + jnp.sum(hidden * pull, axis=-1, keepdims=True)
            grad_pre = (gate * pull * (normal + pre * density)).astype(bfloat)
            hidden = hidden.astype(bfloat)
            made = made + dot_nn(hidden, second)
            back = back + dot_nt(grad_pre, first)
            hidden_parts.append(hidden)
            pre_parts.append(grad_pre)
        grad_logits = (grad_gate * probs * (hot - gate)).astype(bfloat)
        back = back + dot_nt(grad_logits, w_router)
        return made, back, hidden_parts, pre_parts, grad_logits, scaled

    near_made, near_back, near_hidden, near_pre, near_logits, near_scaled = expert(near, grad_near)
    far_made, far_back, far_hidden, far_pre, far_logits, far_scaled = expert(far, grad_far)
    back_got = shift(far_back.astype(bfloat), n // 2)
    back_got, far_made, far_pre[1], far_hidden[1] = tied(
        back_got, far_made.astype(bfloat), far_pre[1], far_hidden[1]
    )
    back_sum = near_back + back_got.astype(single)
    back_home = to_plane(back_sum.astype(bfloat).reshape(experts, capacity, model_width))
    made_got = shift(far_made, n // 2)

    rows_two = jnp.concatenate([near, far], axis=0)
    scaled_two = jnp.concatenate([near_scaled, far_scaled], axis=0)
    hidden_two = [jnp.concatenate(p, axis=0) for p in zip(near_hidden, far_hidden)]
    pre_two = [jnp.concatenate(p, axis=0) for p in zip(near_pre, far_pre)]
    logits_two = jnp.concatenate([near_logits, far_logits], axis=0)
    first_sent = lax.ppermute(dot_tn(rows_two, pre_two[1]).astype(bfloat), "ctx", pair)
    second_sent = lax.ppermute(dot_tn(hidden_two[1], scaled_two).astype(bfloat), "ctx", pair)
    first_near = dot_tn(rows_two, pre_two[0])
    second_near = dot_tn(hidden_two[0], scaled_two)
    grad_router = dot_tn(logits_two, rows_two)

    grad_normed_two = dot_nn(dispatch_mat, back_home.reshape(slots, model_width))
    grad_gain_ffn = jnp.sum(grad_normed_two * resid * scale_two, axis=0)
    grad_resid = grad_in + norm_back(grad_normed_two, resid, scale_two, gain_ffn)
    grad_branch = grad_resid.astype(bfloat)
    grad_attn = dot_nt(grad_branch, w_turned).astype(bfloat)
    attn_grads = [
        pack_rows(grad_attn[:, r * width : (r + 1) * width]) for r in range(n)
    ]
    *attn_grads, made_got = tied(*attn_grads, made_got)
    attn_grads = [attn_grads[0]] + [shift(attn_grads[r], n - r) for r in range(1, n)]

    count = lax.axis_size(PLANE)
    grad_output = dot_tn(attn_rows, grad_branch).astype(bfloat)
    grad_output = grad_output.reshape(n, count, width // count, model_width)
    grad_output = lax.all_to_all(grad_output, PLANE, split_axis=1, concat_axis=1, tiled=True)
    grad_output = sum_first(grad_output.transpose(1, 0, 2, 3))
    *attn_grads, grad_output = tied(*attn_grads, grad_output)
    turns = [grad_output] + [shift(grad_output, r) for r in range(1, n)]

    more = jnp.concatenate([grad_gain_ffn[None, :], grad_router], axis=0)
    more = jnp.pad(more, ((0, -(3 * width + 1 + heads + more.shape[0]) % 128), (0, 0)))
    parts, late = attend_back(
        place_in,
        attn_grads,
        qkv,
        lse,
        rel,
        w_local,
        normed_all,
        gain_attn.reshape(1, -1),
        jnp.pad(buckets, (0, 1)).reshape(1, -1),
        more,
        heads,
    )
    late, first_sent, second_sent, *turns = tied(late, first_sent, second_sent, *turns)
    grad_first = first_near + first_sent.astype(single)
    grad_second = second_near + second_sent.astype(single)
    output_stack = jnp.stack(
        [sum_first(jnp.stack([turns[r][(q - r) % n] for r in range(n)])) for q in range(n)]
    )
    late = to_plane(late.reshape(count, model_width // count, -1))
    parts_in = {r: shift(parts[r], r) for r in range(1, n) if r != n // 2}
    late, output_stack, made_got, *got = tied(late, output_stack, made_got, *parts_in.values())
    parts_in = dict(zip(parts_in, got))
    late_stack = gather_ctx(sum_first(late))
    made_sum = near_made + made_got.astype(single)
    made_home = to_plane(made_sum.astype(bfloat).reshape(experts, capacity, model_width))
    output_held = gather_chips(output_stack)
    late_stack, made_home, mid_part, *got = tied(
        late_stack, made_home, parts[n // 2], *output_held.values()
    )
    output_held = dict(zip(output_held, got))
    late_held = gather_chips(late_stack)
    output_held = gather_cores(output_held)
    parts_in[n // 2] = shift(mid_part, n // 2)

    gate = jnp.sum(
        jax.nn.softmax(dot_nn(normed_two, w_router), axis=-1) * route_hot.astype(single), axis=-1
    )
    picked = dot_nn(dispatch_mat, made_home.reshape(slots, model_width))
    layer_out = resid + gate[:, None] * picked
    output_all = place_output(output_held)

    grad_normed_one = parts[0].astype(single) + sum(p.astype(single) for p in parts_in.values())
    scale_one = norm_scale(row_data)
    grad_tokens = grad_resid + norm_back(grad_normed_one, row_data, scale_one, gain_attn)
    grads = place_late(gather_cores(late_held), width, model_width)
    extra = grads[3]
    totals = jnp.sum(extra, axis=0)
    grad_gain_attn = totals[:, 0]
    grad_gain_ffn = totals[:, 1 + heads]
    grad_table = extra[:, :NB, 1 : 1 + heads].transpose(1, 0, 2).reshape(NB, H)
    grad_router = totals[:, 2 + heads : 2 + heads + experts]
    return (
        layer_out.reshape(seq_dev, block_len, model_width).astype(bfloat),
        grad_tokens.reshape(seq_dev, block_len, model_width).astype(bfloat),
        grad_gain_attn,
        grads[0],
        grads[1],
        grads[2],
        output_all,
        grad_table,
        grad_gain_ffn,
        grad_router,
        grad_first[None],
        grad_second[None],
    )


def solution(mesh):
    spread = P(("dp", "expert"), "ctx", None)
    first = P(("dp", "expert"), None, "ctx")
    return jax.shard_map(
        shards,
        mesh=mesh,
        in_specs=(spread,) * 3 + (P(),) * 9 + (first, spread),
        out_specs=(spread,) * 2 + (P(),) * 8 + (first, spread),
        check_vma=False,
    )
```

```python
import functools

import jax
import jax.numpy as jnp
from jax import lax
from jax.experimental import pallas as pl
from jax.experimental.pallas import tpu as pltpu
from jax.sharding import PartitionSpec as P

H = 12
HD = 64
NB = 32
PLANE = ("dp", "expert")

epsilon = 1e-06
exact_prec = lax.Precision.HIGHEST
bfloat = jnp.bfloat16
single = jnp.float32
VMEM_LIMIT = 56 * 1024 * 1024
PER_MICRO = 1.15e9
CUTS = (2, 6)


def norm_scale(row_data):
    return lax.rsqrt(jnp.mean(row_data * row_data, axis=-1, keepdims=True) + epsilon)


def norm_back(grad_in, row_data, scale, gain):
    weighted = grad_in * gain
    inner = jnp.mean(weighted * row_data, axis=-1, keepdims=True)
    return scale * weighted - row_data * (scale * scale * scale) * inner


def dot_nn(left, right):
    return lax.dot_general(
        left, right, (((1,), (0,)), ((), ())), preferred_element_type=single
    )


def dot_nt(left, right):
    return lax.dot_general(
        left, right, (((1,), (1,)), ((), ())), preferred_element_type=single
    )


def dot_tn(left, right):
    return lax.dot_general(
        left, right, (((0,), (0,)), ((), ())), preferred_element_type=single
    )


def pack_rows(rows):
    half = rows.shape[0] // 2
    return jnp.concatenate([rows[:half], rows[half:]], axis=1)


def unpack_rows(packed):
    width = packed.shape[1] // 2
    return jnp.concatenate([packed[:, :width], packed[:, width:]], axis=0)


def bias_strip(rel_row, rows, width):
    spread = jnp.broadcast_to(rel_row, (rows, width))
    return pltpu.roll(spread, width - (rows - 1), 1, stride=1, stride_axis=0)


def fold_strip(strip):
    rows = strip.shape[0]
    while rows > 1:
        rows //= 2
        strip = strip[rows:] + pltpu.roll(strip[:rows], rows, 1)
    return strip


def attend_kernel(n, heads, place_ref, *refs):
    blocks = refs[:n]
    gain_ref, w_ref, rel_ref, normed_ref, qkv_ref, lse_ref, *out_refs, strip_ref, out_ref = refs[n:]
    place = place_ref[0]
    block_len = blocks[0].shape[0]
    full_len = n * block_len
    width = heads * HD
    for r in range(n):
        start = pl.multiple_of(lax.rem(place - r + n, n) * block_len, block_len)
        row_data = blocks[r][...].astype(single)
        normed = (row_data * norm_scale(row_data) * gain_ref[...]).astype(bfloat)
        normed_ref[pl.ds(start, block_len), :] = normed
        qkv_ref[pl.ds(start, block_len), :] = dot_nn(normed, w_ref[...]).astype(bfloat)
    for h in range(heads):
        strip_ref[h] = bias_strip(rel_ref[h : h + 1, :], block_len, 2 * full_len)
    lse_ref[...] = jnp.zeros_like(lse_ref)

    def tile(t, carry):
        rows = pl.ds(pl.multiple_of(t * block_len, block_len), block_len)
        skew = pl.ds(pl.multiple_of((n - 1 - t) * block_len, block_len), full_len)
        made = []
        for h in range(heads):
            query = qkv_ref[rows, h * HD : (h + 1) * HD]
            key = qkv_ref[:, width + h * HD : width + (h + 1) * HD]
            value = qkv_ref[:, 2 * width + h * HD : 2 * width + (h + 1) * HD]
            scores = dot_nt(query, key) + strip_ref[h, :, skew]
            top = jnp.max(scores, axis=1, keepdims=True)
            expd = jnp.exp(scores - top)
            total = jnp.sum(expd, axis=1, keepdims=True)
            made.append(dot_nn(expd.astype(bfloat), value) / total)
            lse_ref[rows, h : h + 1] = top + jnp.log(total)
        joined = jnp.concatenate(made, axis=1).astype(bfloat)
        out_ref[lax.rem(t - place + n, n)] = pack_rows(joined)
        return carry

    lax.fori_loop(0, n, tile, 0, unroll=True)
    for r in range(n):
        out_refs[r][...] = out_ref[r]


def attend(place, blocks, gain, w_local, rel, heads):
    n = len(blocks)
    block_len, model_width = blocks[0].shape
    full_len = n * block_len
    width = heads * HD
    vmem = pl.BlockSpec(memory_space=pltpu.VMEM)
    return pl.pallas_call(
        functools.partial(attend_kernel, n, heads),
        out_shape=(
            jax.ShapeDtypeStruct((full_len, model_width), bfloat),
            jax.ShapeDtypeStruct((full_len, 3 * width), bfloat),
            jax.ShapeDtypeStruct((full_len, 128), single),
            *[jax.ShapeDtypeStruct((block_len // 2, 2 * width), bfloat)] * n,
        ),
        in_specs=[pl.BlockSpec(memory_space=pltpu.SMEM)] + [vmem] * (n + 3),
        out_specs=(vmem,) * (n + 3),
        scratch_shapes=[
            pltpu.VMEM((heads, block_len, 2 * full_len), single),
            pltpu.VMEM((n, block_len // 2, 2 * width), bfloat),
        ],
        compiler_params=pltpu.CompilerParams(vmem_limit_bytes=VMEM_LIMIT),
        cost_estimate=pl.CostEstimate(
            flops=int(11 * PER_MICRO),
            bytes_accessed=8 * full_len * model_width,
            transcendentals=heads * full_len * full_len,
        ),
        name="attend",
    )(place, *blocks, gain, w_local, rel)


def attend_back_kernel(n, heads, place_ref, *refs):
    blocks = refs[:n]
    (qkv_ref, lse_ref, rel_ref, w_ref, normed_ref, gain_ref, buckets_ref, more_ref,
     *part_refs, late_ref,
     da_ref, strip_ref, sums_ref, key_acc, value_acc, dqkv_ref, rel_out_ref) = refs[n:]
    place = place_ref[0]
    block_len = blocks[0].shape[0] * 2
    full_len = n * block_len
    width = heads * HD
    model_width = normed_ref.shape[1]
    for r in range(n):
        start = pl.multiple_of(lax.rem(place + r, n) * block_len, block_len)
        da_ref[pl.ds(start, block_len), :] = unpack_rows(blocks[r][...])
    for h in range(heads):
        strip_ref[h] = bias_strip(rel_ref[h : h + 1, :], block_len, 2 * full_len)
    sums_ref[...] = jnp.zeros_like(sums_ref)
    key_acc[...] = jnp.zeros_like(key_acc)
    value_acc[...] = jnp.zeros_like(value_acc)

    def tile(t, carry):
        rows = pl.ds(pl.multiple_of(t * block_len, block_len), block_len)
        skew = pl.ds(pl.multiple_of((n - 1 - t) * block_len, block_len), full_len)
        for h in range(heads):
            query = qkv_ref[rows, h * HD : (h + 1) * HD]
            key = qkv_ref[:, width + h * HD : width + (h + 1) * HD]
            value = qkv_ref[:, 2 * width + h * HD : 2 * width + (h + 1) * HD]
            grad_attn = da_ref[rows, h * HD : (h + 1) * HD]
            scores = dot_nt(query, key) + strip_ref[h, :, skew]
            soft = jnp.exp(scores - lse_ref[rows, h : h + 1])
            value_acc[h] += dot_tn(grad_attn, soft.astype(bfloat))
            grad_soft = dot_nt(grad_attn, value)
            delta = jnp.sum(soft * grad_soft, axis=1, keepdims=True)
            grad_wide = soft * (grad_soft - delta)
            sums_ref[h, :, skew] += grad_wide
            grad_scores = grad_wide.astype(bfloat)
            dqkv_ref[rows, h * HD : (h + 1) * HD] = dot_nn(grad_scores, key).astype(bfloat)
            key_acc[h] += dot_tn(query, grad_scores)
        return carry

    lax.fori_loop(0, n, tile, 0, unroll=True)
    for h in range(heads):
        dqkv_ref[:, width + h * HD : width + (h + 1) * HD] = key_acc[h].T.astype(bfloat)
        dqkv_ref[:, 2 * width + h * HD : 2 * width + (h + 1) * HD] = value_acc[h].T.astype(bfloat)
        rel_out_ref[h : h + 1, :] = fold_strip(sums_ref[h])
    for r in range(n):
        start = pl.multiple_of(lax.rem(place + r, n) * block_len, block_len)
        part_refs[r][...] = pack_rows(dqkv_ref[pl.ds(start, block_len), :])
    made = dot_tn(normed_ref[...], dqkv_ref[...])
    late_ref[:, : 3 * width] = made.astype(bfloat)
    total = jnp.sum(made * w_ref[...].astype(single), axis=1, keepdims=True)
    kinds = lax.broadcasted_iota(jnp.int32, (NB, 2 * full_len), 0)
    hot = (kinds == buckets_ref[...]).astype(single)
    table = lax.dot_general(
        rel_out_ref[...], hot, (((1,), (1,)), ((), ())),
        precision=exact_prec, preferred_element_type=single,
    )
    table = jnp.concatenate([table, jnp.zeros((heads, model_width - NB), single)], axis=1)
    extra = jnp.concatenate([1.0 / gain_ref[...], table, more_ref[...]], axis=0).T
    late_ref[:, 3 * width :] = extra.astype(bfloat)
    late_ref[:, 3 * width : 3 * width + 1] = (extra[:, :1] * total).astype(bfloat)


def attend_back(place, blocks, qkv, lse, rel, w_local, normed, gain, buckets, more, heads):
    n = len(blocks)
    full_len, model_width = normed.shape
    block_len = full_len // n
    width = heads * HD
    late_width = 3 * width + 1 + heads + more.shape[0]
    vmem = pl.BlockSpec(memory_space=pltpu.VMEM)
    return pl.pallas_call(
        functools.partial(attend_back_kernel, n, heads),
        out_shape=(
            *[jax.ShapeDtypeStruct((block_len // 2, 6 * width), bfloat)] * n,
            jax.ShapeDtypeStruct((model_width, late_width), bfloat),
        ),
        in_specs=[pl.BlockSpec(memory_space=pltpu.SMEM)] + [vmem] * (n + 8),
        out_specs=(vmem,) * (n + 1),
        scratch_shapes=[
            pltpu.VMEM((full_len, width), bfloat),
            pltpu.VMEM((heads, block_len, 2 * full_len), single),
            pltpu.VMEM((heads, block_len, 2 * full_len), single),
            pltpu.VMEM((heads, HD, full_len), single),
            pltpu.VMEM((heads, HD, full_len), single),
            pltpu.VMEM((full_len, 3 * width), bfloat),
            pltpu.VMEM((heads, 2 * full_len), single),
        ],
        compiler_params=pltpu.CompilerParams(vmem_limit_bytes=VMEM_LIMIT),
        cost_estimate=pl.CostEstimate(
            flops=int(19 * PER_MICRO),
            bytes_accessed=8 * full_len * model_width,
            transcendentals=heads * full_len * full_len,
        ),
        name="attend_back",
    )(place, *blocks, qkv, lse, rel, w_local, normed, gain, buckets, more)


def call(kernel, name, shapes, micros, *args, in_smem=(), scratch=()):
    vmem = pl.BlockSpec(memory_space=pltpu.VMEM)
    smem = pl.BlockSpec(memory_space=pltpu.SMEM)
    moved = sum(a.size * a.dtype.itemsize for a in args)
    return pl.pallas_call(
        kernel,
        out_shape=[jax.ShapeDtypeStruct(s, t) for s, t in shapes],
        in_specs=[smem if i in in_smem else vmem for i in range(len(args))],
        out_specs=[vmem] * len(shapes),
        scratch_shapes=scratch,
        compiler_params=pltpu.CompilerParams(vmem_limit_bytes=VMEM_LIMIT),
        cost_estimate=pl.CostEstimate(
            flops=int(micros * PER_MICRO), bytes_accessed=moved, transcendentals=0
        ),
        name=name,
    )(*args)


def middle_kernel(n, *refs):
    parts = refs[:n]
    x_ref, w_ref, gain_ref, dispatch_ref, sent_ref, resid_ref, attn_ref = refs[n:]
    width = w_ref.shape[0] // n
    for r in range(n):
        attn_ref[:, r * width : (r + 1) * width] = unpack_rows(parts[r][...])
    resid = x_ref[...].astype(single) + dot_nn(attn_ref[...], w_ref[...])
    resid_ref[...] = resid
    normed = (resid * norm_scale(resid) * gain_ref[...]).astype(bfloat)
    sent_ref[...] = dot_nn(dispatch_ref[...], normed).astype(bfloat)


def expert_kernel(spot_ref, rows_ref, grad_ref, first_ref, second_ref, *refs):
    pieces, (router_ref, back_ref, scaled_ref, logits_ref) = refs[:6], refs[6:10]
    hidden_refs, pre_refs, others = refs[10:12], refs[12:14], refs[14:]
    for i, ref in enumerate(pieces):
        start = sum(p.shape[0] for p in pieces[i - i % 3 : i])
        others[i // 3][start : start + ref.shape[0], :] = ref[...]
    rows, grad_rows = rows_ref[...], grad_ref[...]
    count = rows.shape[0]
    half = first_ref.shape[1] // 2
    logits = dot_nn(rows, router_ref[...])
    expd = jnp.exp(logits - jnp.max(logits, axis=1, keepdims=True))
    probs = expd / jnp.sum(expd, axis=1, keepdims=True)
    hot = (lax.broadcasted_iota(jnp.int32, (1, logits.shape[1]), 1) == spot_ref[0]).astype(single)
    gate = jnp.sum(probs * hot, axis=1, keepdims=True)
    scaled_ref[...] = (gate * grad_rows.astype(single)).astype(bfloat)
    grad_gate = jnp.zeros((count, 1), single)
    back = [jnp.zeros((count, half), single), jnp.zeros((count, half), single)]
    for other, (first, second) in enumerate(((first_ref, second_ref), others)):
        for piece in range(2):
            cols = slice(piece * half, (piece + 1) * half)
            pre = dot_nn(rows, first[:, cols])
            pull = dot_nt(grad_rows, second[cols, :])
            normal = 0.5 * (1.0 + lax.erf(pre * (0.5**0.5)))
            density = jnp.exp(-0.5 * pre * pre) * 0.3989422804014327
            hidden = pre * normal
            grad_gate += jnp.sum(hidden * pull, axis=1, keepdims=True)
            grad_pre = (gate * pull * (normal + pre * density)).astype(bfloat)
            hidden_refs[other][:, cols] = hidden.astype(bfloat)
            pre_refs[other][:, cols] = grad_pre
            for side in range(2):
                ends = slice(side * half, (side + 1) * half)
                back[side] += dot_nt(grad_pre, first[ends, cols])
    grad_logits = (grad_gate * probs * (hot - gate)).astype(bfloat)
    logits_ref[...] = grad_logits
    for side in range(2):
        ends = slice(side * half, (side + 1) * half)
        made = back[side] + dot_nt(grad_logits, router_ref[ends, :])
        back_ref[:, ends] = made.astype(back_ref.dtype)


def expert(spot, rows, grad_rows, first, second, pieces, w_router, kind):
    wide = rows.shape
    units = (rows.shape[0], first.shape[1])
    shapes = [(wide, kind), (wide, bfloat), ((wide[0], w_router.shape[1]), bfloat)]
    return call(
        expert_kernel, "expert", shapes + [(units, bfloat)] * 4, 7,
        spot, rows, grad_rows, first, second, *pieces, w_router, in_smem=(0,),
        scratch=[pltpu.VMEM(first.shape, bfloat), pltpu.VMEM(second.shape, bfloat)],
    )


def made_kernel(near_own, near_other, far_own, far_other, second_ref, *refs):
    pieces, (near_ref, far_ref) = refs[:3], refs[3:]
    for own, other, out in ((near_own, near_other, near_ref), (far_own, far_other, far_ref)):
        made = dot_nn(own[...], second_ref[...])
        start = 0
        for ref in pieces:
            made += dot_nn(other[:, start : start + ref.shape[0]], ref[...])
            start += ref.shape[0]
        out[...] = made.astype(out.dtype)


def add_kernel(left_ref, right_ref, out_ref):
    out_ref[...] = (left_ref[...] + right_ref[...].astype(single)).astype(bfloat)


def turn_kernel(*refs):
    *ins, out_ref = refs
    n = len(ins)
    for q in range(n):
        out_ref[q] = sum(ins[r][(q - r) % n].astype(single) for r in range(n)).astype(bfloat)


def sums_kernel(near_rows, far_rows, near_pre, far_pre, near_hidden, far_hidden,
                near_scaled, far_scaled, near_logits, far_logits, *refs):
    *outs, router_ref = refs
    half = outs[0].shape[0]
    for i in range(2):
        ends = slice(i * half, (i + 1) * half)
        made = dot_tn(near_rows[:, ends], near_pre[...]) + dot_tn(far_rows[:, ends], far_pre[...])
        outs[i][...] = made.astype(bfloat)
    for i in range(2):
        ends = slice(i * half, (i + 1) * half)
        made = dot_tn(near_hidden[:, ends], near_scaled[...])
        made += dot_tn(far_hidden[:, ends], far_scaled[...])
        outs[2 + i][...] = made.astype(bfloat)
    router_ref[...] = dot_tn(near_logits[...], near_rows[...]) + dot_tn(far_logits[...], far_rows[...])


def own_kernel(near_left, far_left, near_right, far_right, top_ref, low_ref, out_ref):
    half = top_ref.shape[0]
    for i, got in enumerate((top_ref, low_ref)):
        ends = slice(i * half, (i + 1) * half)
        made = dot_tn(near_left[:, ends], near_right[...]) + dot_tn(far_left[:, ends], far_right[...])
        out_ref[ends, :] = made + got[...].astype(single)


def layer_kernel(made_ref, dispatch_ref, resid_ref, gain_ref, router_ref, hot_ref, out_ref):
    resid = resid_ref[...]
    normed = (resid * norm_scale(resid) * gain_ref[...]).astype(bfloat)
    logits = dot_nn(normed, router_ref[...])
    expd = jnp.exp(logits - jnp.max(logits, axis=1, keepdims=True))
    probs = expd / jnp.sum(expd, axis=1, keepdims=True)
    gate = jnp.sum(probs * hot_ref[...].astype(single), axis=1, keepdims=True)
    out_ref[...] = (resid + gate * dot_nn(dispatch_ref[...], made_ref[...])).astype(bfloat)


def last_kernel(n, *refs):
    parts, (w_ref, x_ref, gain_ref, resid_ref, out_ref) = refs[:n], refs[n:]
    width = w_ref.shape[1] // n
    grad_normed = jnp.zeros(x_ref.shape, single)
    for r in range(n):
        cols = slice(r * width, (r + 1) * width)
        grad_normed += dot_nt(unpack_rows(parts[r][...]), w_ref[:, cols])
    row_data = x_ref[...].astype(single)
    back = norm_back(grad_normed, row_data, norm_scale(row_data), gain_ref[...])
    out_ref[...] = (resid_ref[...] + back).astype(bfloat)


def post_kernel(n, back_ref, dispatch_ref, resid_ref, grad_ref, gain_ref, w_ref, *refs):
    attn_refs, (resid_out, branch_ref, gain_out) = refs[:n], refs[n:]
    width = w_ref.shape[0] // n
    grad_normed = dot_nn(dispatch_ref[...], back_ref[...])
    resid = resid_ref[...]
    scale = norm_scale(resid)
    gain_out[...] = jnp.sum(grad_normed * resid * scale, axis=0, keepdims=True)
    grad_resid = grad_ref[...].astype(single) + norm_back(grad_normed, resid, scale, gain_ref[...])
    resid_out[...] = grad_resid
    branch = grad_resid.astype(bfloat)
    branch_ref[...] = branch
    grad_attn = dot_nt(branch, w_ref[...]).astype(bfloat)
    for r in range(n):
        attn_refs[r][...] = pack_rows(grad_attn[:, r * width : (r + 1) * width])


def shift(block, by):
    n = lax.axis_size("ctx")
    return lax.ppermute(block, "ctx", [(i, (i + by) % n) for i in range(n)])


def swap_plane(block, mask):
    count = lax.axis_size(PLANE)
    return lax.ppermute(block, PLANE, [(i, i ^ mask) for i in range(count)])


def to_plane(blocks):
    return lax.all_to_all(blocks, PLANE, split_axis=0, concat_axis=0, tiled=True)


def sum_first(parts):
    return jnp.sum(parts.astype(single), axis=0).astype(bfloat)


def gather_ctx(piece):
    n = lax.axis_size("ctx")
    return jnp.stack([piece] + [shift(piece, r) for r in range(1, n)])


def gather_chips(stack):
    count = lax.axis_size(PLANE)
    core = lax.axis_size("expert")
    return {mask: swap_plane(stack, mask) if mask else stack for mask in range(count) if not mask & core}


def gather_cores(held):
    core = lax.axis_size("expert")
    held = {**held, **{mask | core: swap_plane(held[mask], core) for mask in held}}
    return [held[mask] for mask in sorted(held)]


def tied(*arrays):
    return lax.optimization_barrier(arrays)


def late_extras(extra, heads, experts):
    rows = sum(extra[1:], extra[0]).T
    table = jnp.concatenate([e[:NB].T[1 : 1 + heads] for e in extra], axis=0)
    return rows[0], rows[1 + heads], table, rows[2 + heads : 2 + heads + experts]


def place_late_kernel(count, n, heads, experts, spot_ref, *refs):
    spot, place = spot_ref[0], spot_ref[1]
    ins, outs, small, extra_ref = refs[:count], refs[count : count + 3], refs[count + 3 : -1], refs[-1]
    step = ins[0].shape[1]
    width = heads * HD
    for mask in range(count):
        rows = pl.ds(pl.multiple_of((spot ^ mask) * step, step), step)
        for c in range(n):
            block = ins[mask][lax.rem(place - c + n, n)].astype(single)
            for i in range(3):
                outs[i][rows, c * width : (c + 1) * width] = block[:, i * width : (i + 1) * width]
            extra_ref[c, rows, :] = block[:, 3 * width :]
    made = late_extras([extra_ref[c] for c in range(n)], heads, experts)
    for ref, value in zip(small, made):
        ref[...] = value


def place_output_kernel(count, n, spot_ref, *refs):
    spot, place = spot_ref[0], spot_ref[1]
    step = refs[0].shape[1]
    for mask in range(count):
        for c in range(n):
            start = (c * count + (spot ^ mask)) * step
            block = refs[mask][lax.rem(place - c + n, n)]
            refs[count][pl.ds(pl.multiple_of(start, step), step), :] = block.astype(single)


def placed(kernel, spots, held, shapes, scratch=()):
    vmem = pl.BlockSpec(memory_space=pltpu.VMEM)
    return pl.pallas_call(
        kernel,
        out_shape=[jax.ShapeDtypeStruct(s, single) for s in shapes],
        in_specs=[pl.BlockSpec(memory_space=pltpu.SMEM)] + [vmem] * len(held),
        out_specs=[vmem] * len(shapes),
        scratch_shapes=scratch,
        compiler_params=pltpu.CompilerParams(vmem_limit_bytes=VMEM_LIMIT),
        cost_estimate=pl.CostEstimate(
            flops=int(5 * PER_MICRO), bytes_accessed=12_000_000, transcendentals=0
        ),
        name="placed",
    )(spots, *held)


def spots():
    return jnp.stack([lax.axis_index(PLANE), lax.axis_index("ctx")]).astype(jnp.int32)


def place_late(held, heads, model_width, experts):
    n, step, wide = held[0].shape
    width = heads * HD
    if step % 8:
        place, spot = lax.axis_index("ctx"), lax.axis_index(PLANE)
        whole = jnp.zeros((n, model_width, wide), single)
        for mask, stack in enumerate(held):
            for r in range(n):
                where = ((place - r) % n, (spot ^ mask) * step, 0)
                whole = lax.dynamic_update_slice(whole, stack[r : r + 1].astype(single), where)
        own = [whole[:, :, i * width : (i + 1) * width] for i in range(3)]
        own = [o.transpose(1, 0, 2).reshape(model_width, n * width) for o in own]
        return own + list(late_extras([w[:, 3 * width :] for w in whole], heads, experts))
    shapes = [(model_width, n * width)] * 3
    shapes += [(model_width,), (model_width,), (n * heads, NB), (experts, model_width)]
    kernel = functools.partial(place_late_kernel, len(held), n, heads, experts)
    scratch = [pltpu.VMEM((n, model_width, wide - 3 * width), single)]
    return placed(kernel, spots(), held, shapes, scratch)


def place_output(held):
    n, step, wide = held[0].shape
    count = len(held)
    if step % 8:
        place, spot = lax.axis_index("ctx"), lax.axis_index(PLANE)
        whole = jnp.zeros((n, count * step, wide), single)
        for mask, stack in enumerate(held):
            for r in range(n):
                where = ((place - r) % n, (spot ^ mask) * step, 0)
                whole = lax.dynamic_update_slice(whole, stack[r : r + 1].astype(single), where)
        return whole.reshape(n * count * step, wide)
    kernel = functools.partial(place_output_kernel, count, n)
    return placed(kernel, spots(), held, [(n * count * step, wide)])[0]


def shards(
    tokens,
    cotangent,
    routes,
    buckets,
    gain_attn,
    w_query,
    w_key,
    w_value,
    w_output,
    bias_table,
    gain_ffn,
    w_router,
    w_in,
    w_out,
):
    seq_dev, block_len, model_width = tokens.shape
    n = lax.axis_size("ctx")
    experts = lax.axis_size(PLANE)
    heads = H // n
    width = heads * HD
    full_len = block_len * n
    tok_count = seq_dev * block_len
    capacity = max(2, (5 * tok_count + 4 * experts - 1) // (4 * experts))
    slots = experts * capacity
    place = lax.axis_index("ctx")
    spot = lax.axis_index(PLANE)
    place_in = place.astype(jnp.int32).reshape(1)

    block = tokens.reshape(tok_count, model_width)
    blocks = [block] + [shift(block, r) for r in range(1, n)]

    own_heads = [
        lax.dynamic_slice_in_dim(w, place * width, width, 1) for w in (w_query, w_key, w_value)
    ]
    w_local = jnp.concatenate(own_heads, axis=1)
    turned = [
        lax.dynamic_slice_in_dim(w_output, (place - r) % n * width, width, 0) for r in range(n)
    ]
    w_turned = jnp.concatenate(turned, axis=0)
    w_all = jnp.concatenate(
        [
            lax.dynamic_slice_in_dim(w, (place - r) % n * width, width, 1)
            for r in range(n)
            for w in (w_query, w_key, w_value)
        ],
        axis=1,
    )
    bucket_hot = (buckets[:, None] == jnp.arange(NB, dtype=jnp.int32)[None, :]).astype(single)
    table_local = lax.dynamic_slice_in_dim(bias_table, place * heads, heads, 1)
    rel = lax.dot_general(
        table_local, bucket_hot, (((0,), (1,)), ((), ())), precision=exact_prec
    )
    rel = jnp.pad(rel, ((0, 0), (0, 1)))
    route_flat = routes.reshape(tok_count)
    route_hot = (
        route_flat[:, None] == jnp.arange(experts, dtype=jnp.int32)[None, :]
    ).astype(bfloat)
    earlier = jnp.tril(jnp.ones((tok_count, tok_count), bfloat), -1)
    counts = dot_nn(earlier, route_hot)
    slot_index = jnp.sum(counts * route_hot.astype(single), axis=1).astype(jnp.int32)
    target = jnp.where(slot_index < capacity, route_flat * capacity + slot_index, -1)
    dispatch_mat = (target[:, None] == jnp.arange(slots, dtype=jnp.int32)[None, :]).astype(bfloat)
    dispatch_turned = dispatch_mat.T
    gain_one, gain_two = gain_attn.reshape(1, -1), gain_ffn.reshape(1, -1)
    spot_in = spot.astype(jnp.int32).reshape(1)
    buckets_row = jnp.pad(buckets, (0, 1)).reshape(1, -1)

    grad_block = cotangent.reshape(tok_count, model_width)
    grad_sent = dot_nn(dispatch_turned, grad_block).astype(bfloat)
    grad_near = to_plane(grad_sent.reshape(experts, capacity, model_width))
    grad_near = grad_near.reshape(slots, model_width)

    pair = [(i, i ^ 1) for i in range(n)]
    half = model_width // 2

    def swap(piece):
        return lax.ppermute(piece, "ctx", pair)

    first_own, second_own = w_in[0], w_out[0]
    low, high = (cut * model_width // 8 for cut in CUTS)
    pieces = [w[a:b] for w in (first_own, second_own) for a, b in ((0, low), (low, high), (high, None))]
    pieces[0] = swap(pieces[0])
    blocks, pieces, gain_one, gain_two, grad_near, w_local, w_turned, rel, dispatches = tied(
        blocks, pieces, gain_one, gain_two, grad_near, w_local, w_turned, rel,
        (dispatch_mat, dispatch_turned),
    )
    dispatch_mat, dispatch_turned = dispatches
    pieces[1] = swap(pieces[1])

    normed_all, qkv, lse, *attn_parts = attend(place_in, blocks, gain_one, w_local, rel, heads)
    attn_parts, pieces = tied(attn_parts, pieces)
    attn_turned = [attn_parts[0]] + [shift(attn_parts[r], r) for r in range(1, n)]
    pieces[2], pieces[3] = swap(pieces[2]), swap(pieces[3])
    attn_turned, grad_near, pieces, w_all = tied(attn_turned, grad_near, pieces, w_all)
    grad_far = shift(grad_near, n // 2)
    pieces[4] = swap(pieces[4])
    rows_shape = (tok_count, model_width)
    sent, resid, attn_rows = call(
        functools.partial(middle_kernel, n),
        "middle",
        [((slots, model_width), bfloat), (rows_shape, single), (rows_shape, bfloat)],
        3,
        *attn_turned, block, w_turned, gain_two, dispatch_turned,
    )
    near = to_plane(sent.reshape(experts, capacity, model_width)).reshape(slots, model_width)
    near, grad_far, pieces = tied(near, grad_far, pieces)
    far = shift(near, n // 2)
    pieces[5] = swap(pieces[5])

    near_back, near_scaled, near_logits, *near_parts = expert(
        spot_in, near, grad_near, first_own, second_own, pieces, w_router, single
    )
    far, near_back = tied(far, near_back)
    far_back, far_scaled, far_logits, *far_parts = expert(
        spot_in, far, grad_far, first_own, second_own, pieces, w_router, bfloat
    )
    back_got = shift(far_back, n // 2)

    *sends, grad_router = call(
        sums_kernel,
        "sums",
        [((half, model_width), bfloat)] * 4 + [((experts, model_width), single)],
        5,
        near, far, near_parts[3], far_parts[3], near_parts[1], far_parts[1],
        near_scaled, far_scaled, near_logits, far_logits,
    )
    sends, far_parts = tied(sends, far_parts)
    sends[0] = swap(sends[0])
    near_made, far_made = call(
        made_kernel,
        "made",
        [((slots, model_width), single), ((slots, model_width), bfloat)],
        5,
        *near_parts[:2], *far_parts[:2], second_own, *pieces[3:],
    )
    back_got, sends, far_made, near_made, grad_router = tied(
        back_got, sends, far_made, near_made, grad_router
    )
    sends[1] = swap(sends[1])
    (back_sum,) = call(add_kernel, "add", [((slots, model_width), bfloat)], 1, near_back, back_got)
    back_home = to_plane(back_sum.reshape(experts, capacity, model_width))

    *attn_grads, grad_resid, grad_branch, grad_gain_ffn = call(
        functools.partial(post_kernel, n),
        "post",
        [((tok_count // 2, 2 * width), bfloat)] * n
        + [(rows_shape, single), (rows_shape, bfloat), ((1, model_width), single)],
        4,
        back_home.reshape(slots, model_width), dispatch_mat, resid, grad_block, gain_two, w_turned,
    )
    attn_grads, grad_branch, sends = tied(attn_grads, grad_branch, sends)
    attn_grads = [attn_grads[0]] + [shift(attn_grads[r], n - r) for r in range(1, n)]

    count = lax.axis_size(PLANE)
    grad_output = dot_tn(attn_rows, grad_branch).astype(bfloat)
    grad_output = grad_output.reshape(n, count, width // count, model_width)
    grad_output = lax.all_to_all(grad_output, PLANE, split_axis=1, concat_axis=1, tiled=True)
    more = jnp.concatenate([grad_gain_ffn, grad_router], axis=0)
    more = jnp.pad(more, ((0, -(3 * width + 1 + heads + more.shape[0]) % 128), (0, 0)))
    *attn_grads, far_made, sends[2], more, grad_resid = tied(
        *attn_grads, far_made, sends[2], more, grad_resid
    )
    made_got = shift(far_made, n // 2)
    sends[2] = lax.ppermute(sends[2], "ctx", pair)

    *parts, late = attend_back(
        place_in, attn_grads, qkv, lse, rel, w_local, normed_all, gain_one, buckets_row, more, heads
    )
    late, made_got, sends, grad_output = tied(late, made_got, sends, grad_output)
    late = to_plane(late.reshape(count, model_width // count, -1))
    grad_output = sum_first(grad_output.transpose(1, 0, 2, 3))
    turns = [grad_output] + [shift(grad_output, r) for r in range(1, n)]
    parts_got = {r: shift(parts[r], r) for r in range(1, n) if r != n // 2}
    (made_sum,) = call(add_kernel, "add", [((slots, model_width), bfloat)], 1, near_made, made_got)
    late, made_sum, turns, far_parts = tied(late, made_sum, turns, far_parts)
    late_stack = gather_ctx(sum_first(late))
    made_home = to_plane(made_sum.reshape(experts, capacity, model_width))
    (output_stack,) = call(turn_kernel, "turn", [(grad_output.shape, bfloat)], 1, *turns)
    (grad_first,) = call(
        own_kernel, "own", [((model_width, model_width), single)], 4,
        near, far, near_parts[2], far_parts[2], *sends[:2],
    )
    output_held = gather_chips(output_stack)
    late_stack, sends, parts, parts_got, made_home, grad_first = tied(
        late_stack, sends, parts, parts_got, made_home, grad_first
    )
    late_held = gather_chips(late_stack)
    parts_got[n // 2] = shift(parts[n // 2], n // 2)
    sends[3] = swap(sends[3])
    output_all = place_output(gather_cores(output_held))
    (layer_out,) = call(
        layer_kernel, "layer", [(rows_shape, bfloat)], 3,
        made_home.reshape(slots, model_width), dispatch_mat, resid, gain_two, w_router, route_hot,
    )
    (grad_tokens,) = call(
        functools.partial(last_kernel, n), "last", [(rows_shape, bfloat)], 4,
        parts[0], *(parts_got[r] for r in range(1, n)), w_all, block, gain_one, grad_resid,
    )
    (grad_second,) = call(
        own_kernel, "own", [((model_width, model_width), single)], 4,
        near_parts[0], far_parts[0], near_scaled, far_scaled, *sends[2:],
    )
    late_held, layer_out, grad_tokens, grad_second, output_all = tied(
        late_held, layer_out, grad_tokens, grad_second, output_all
    )
    grads = place_late(gather_cores(late_held), heads, model_width, experts)
    grad_query, grad_key, grad_value, grad_gain_attn, grad_gain_ffn, grad_table, grad_router = grads
    return (
        layer_out.reshape(seq_dev, block_len, model_width).astype(bfloat),
        grad_tokens.reshape(seq_dev, block_len, model_width).astype(bfloat),
        grad_gain_attn,
        grad_query,
        grad_key,
        grad_value,
        output_all,
        grad_table.T,
        grad_gain_ffn,
        grad_router.T,
        grad_first[None],
        grad_second[None],
    )


def solution(mesh):
    spread = P(("dp", "expert"), "ctx", None)
    first = P(("dp", "expert"), None, "ctx")
    return jax.shard_map(
        shards,
        mesh=mesh,
        in_specs=(spread,) * 3 + (P(),) * 9 + (first, spread),
        out_specs=(spread,) * 2 + (P(),) * 8 + (first, spread),
        check_vma=False,
    )
```

```python
import functools
import math

import jax
import jax.numpy as jnp
from jax import lax
from jax.experimental import pallas as pl
from jax.experimental.pallas import tpu as pltpu
from jax.sharding import PartitionSpec as P

H = 12
HD = 64
NB = 32
PLANE = ("dp", "expert")

epsilon = 1e-06
exact_prec = lax.Precision.HIGHEST
bfloat = jnp.bfloat16
single = jnp.float32
VMEM_LIMIT = 56 * 1024 * 1024
ROOM = 8 * 1024 * 1024
TIGHT = ("last", "own", "layer")
PER_MICRO = 1.15e9
CUTS = (2, 6)


def norm_scale(row_data):
    return lax.rsqrt(jnp.mean(row_data * row_data, axis=-1, keepdims=True) + epsilon)


def norm_back(grad_in, row_data, scale, gain):
    weighted = grad_in * gain
    inner = jnp.mean(weighted * row_data, axis=-1, keepdims=True)
    return scale * weighted - row_data * (scale * scale * scale) * inner


def dot_nn(left, right):
    return lax.dot_general(
        left, right, (((1,), (0,)), ((), ())), preferred_element_type=single
    )


def dot_nt(left, right):
    return lax.dot_general(
        left, right, (((1,), (1,)), ((), ())), preferred_element_type=single
    )


def dot_tn(left, right):
    return lax.dot_general(
        left, right, (((0,), (0,)), ((), ())), preferred_element_type=single
    )


def pack_rows(rows):
    half = rows.shape[0] // 2
    return jnp.concatenate([rows[:half], rows[half:]], axis=1)


def unpack_rows(packed):
    width = packed.shape[1] // 2
    return jnp.concatenate([packed[:, :width], packed[:, width:]], axis=0)


def bias_strip(rel_row, rows, width):
    spread = jnp.broadcast_to(rel_row, (rows, width))
    return pltpu.roll(spread, width - (rows - 1), 1, stride=1, stride_axis=0)


def fold_strip(strip):
    rows = strip.shape[0]
    while rows > 1:
        rows //= 2
        strip = strip[rows:] + pltpu.roll(strip[:rows], rows, 1)
    return strip


def attend_kernel(n, heads, place_ref, *refs):
    blocks = refs[:n]
    gain_ref, w_ref, rel_ref, normed_ref, qkv_ref, lse_ref, *out_refs, strip_ref, out_ref = refs[n:]
    place = place_ref[0]
    block_len = blocks[0].shape[0]
    full_len = n * block_len
    width = heads * HD
    for r in range(n):
        start = pl.multiple_of(lax.rem(place - r + n, n) * block_len, block_len)
        row_data = blocks[r][...].astype(single)
        normed = (row_data * norm_scale(row_data) * gain_ref[...]).astype(bfloat)
        normed_ref[pl.ds(start, block_len), :] = normed
        qkv_ref[pl.ds(start, block_len), :] = dot_nn(normed, w_ref[...]).astype(bfloat)
    for h in range(heads):
        strip_ref[h] = bias_strip(rel_ref[h : h + 1, :], block_len, 2 * full_len)
    lse_ref[...] = jnp.zeros_like(lse_ref)

    def tile(t, carry):
        rows = pl.ds(pl.multiple_of(t * block_len, block_len), block_len)
        skew = pl.ds(pl.multiple_of((n - 1 - t) * block_len, block_len), full_len)
        made = []
        for h in range(heads):
            query = qkv_ref[rows, h * HD : (h + 1) * HD]
            key = qkv_ref[:, width + h * HD : width + (h + 1) * HD]
            value = qkv_ref[:, 2 * width + h * HD : 2 * width + (h + 1) * HD]
            scores = dot_nt(query, key) + strip_ref[h, :, skew]
            top = jnp.max(scores, axis=1, keepdims=True)
            expd = jnp.exp(scores - top)
            total = jnp.sum(expd, axis=1, keepdims=True)
            made.append(dot_nn(expd.astype(bfloat), value) / total)
            lse_ref[rows, h : h + 1] = top + jnp.log(total)
        joined = jnp.concatenate(made, axis=1).astype(bfloat)
        out_ref[lax.rem(t - place + n, n)] = pack_rows(joined)
        return carry

    lax.fori_loop(0, n, tile, 0, unroll=1)
    for r in range(n):
        out_refs[r][...] = out_ref[r]


def attend(place, blocks, gain, w_local, rel, heads):
    n = len(blocks)
    block_len, model_width = blocks[0].shape
    full_len = n * block_len
    width = heads * HD
    vmem = pl.BlockSpec(memory_space=pltpu.VMEM)
    return pl.pallas_call(
        functools.partial(attend_kernel, n, heads),
        out_shape=(
            jax.ShapeDtypeStruct((full_len, model_width), bfloat),
            jax.ShapeDtypeStruct((full_len, 3 * width), bfloat),
            jax.ShapeDtypeStruct((full_len, 128), single),
            *[jax.ShapeDtypeStruct((block_len // 2, 2 * width), bfloat)] * n,
        ),
        in_specs=[pl.BlockSpec(memory_space=pltpu.SMEM)] + [vmem] * (n + 3),
        out_specs=(vmem,) * (n + 3),
        scratch_shapes=[
            pltpu.VMEM((heads, block_len, 2 * full_len), single),
            pltpu.VMEM((n, block_len // 2, 2 * width), bfloat),
        ],
        compiler_params=pltpu.CompilerParams(vmem_limit_bytes=VMEM_LIMIT),
        cost_estimate=pl.CostEstimate(
            flops=int(11 * PER_MICRO),
            bytes_accessed=0,
            transcendentals=0,
        ),
        name="attend",
    )(place, *blocks, gain, w_local, rel)


def attend_back_kernel(n, heads, place_ref, *refs):
    blocks = refs[:n]
    (qkv_ref, lse_ref, rel_ref, w_ref, normed_ref, gain_ref, buckets_ref, grad_gain_ref, router_ref,
     part_ref, late_ref,
     da_ref, strip_ref, sums_ref, key_acc, value_acc, dqkv_ref, rel_out_ref) = refs[n:]
    place = place_ref[0]
    block_len = blocks[0].shape[0] * 2
    full_len = n * block_len
    width = heads * HD
    model_width = normed_ref.shape[1]
    for r in range(n):
        start = pl.multiple_of(lax.rem(place + r, n) * block_len, block_len)
        da_ref[pl.ds(start, block_len), :] = unpack_rows(blocks[r][...])
    for h in range(heads):
        strip_ref[h] = bias_strip(rel_ref[h : h + 1, :], block_len, 2 * full_len)
    sums_ref[...] = jnp.zeros_like(sums_ref)
    key_acc[...] = jnp.zeros_like(key_acc)
    value_acc[...] = jnp.zeros_like(value_acc)

    def tile(t, carry):
        rows = pl.ds(pl.multiple_of(t * block_len, block_len), block_len)
        skew = pl.ds(pl.multiple_of((n - 1 - t) * block_len, block_len), full_len)
        for h in range(heads):
            query = qkv_ref[rows, h * HD : (h + 1) * HD]
            key = qkv_ref[:, width + h * HD : width + (h + 1) * HD]
            value = qkv_ref[:, 2 * width + h * HD : 2 * width + (h + 1) * HD]
            grad_attn = da_ref[rows, h * HD : (h + 1) * HD]
            scores = dot_nt(query, key) + strip_ref[h, :, skew]
            soft = jnp.exp(scores - lse_ref[rows, h : h + 1])
            value_acc[h] += dot_tn(grad_attn, soft.astype(bfloat))
            grad_soft = dot_nt(grad_attn, value)
            delta = jnp.sum(soft * grad_soft, axis=1, keepdims=True)
            grad_wide = soft * (grad_soft - delta)
            sums_ref[h, :, skew] += grad_wide
            grad_scores = grad_wide.astype(bfloat)
            dqkv_ref[rows, h * HD : (h + 1) * HD] = dot_nn(grad_scores, key).astype(bfloat)
            key_acc[h] += dot_tn(query, grad_scores)
        return carry

    lax.fori_loop(0, n, tile, 0, unroll=4)
    for h in range(heads):
        dqkv_ref[:, width + h * HD : width + (h + 1) * HD] = key_acc[h].T.astype(bfloat)
        dqkv_ref[:, 2 * width + h * HD : 2 * width + (h + 1) * HD] = value_acc[h].T.astype(bfloat)
        rel_out_ref[h : h + 1, :] = fold_strip(sums_ref[h])
    for r in range(n):
        part_ref[r] = pack_rows(dqkv_ref[r * block_len : (r + 1) * block_len, :])
    made = dot_tn(normed_ref[...], dqkv_ref[...])
    late_ref[:, : 3 * width] = made.astype(bfloat)
    total = jnp.sum(made * w_ref[...].astype(single), axis=1, keepdims=True)
    kinds = lax.broadcasted_iota(jnp.int32, (NB, 2 * full_len), 0)
    hot = (kinds == buckets_ref[...]).astype(single)
    table = lax.dot_general(
        rel_out_ref[...], hot, (((1,), (1,)), ((), ())),
        precision=exact_prec, preferred_element_type=single,
    )
    table = jnp.concatenate([table, jnp.zeros((heads, model_width - NB), single)], axis=1)
    extra = [1.0 / gain_ref[...], table, grad_gain_ref[...], router_ref[...]]
    short = late_ref.shape[1] - 3 * width - sum(e.shape[0] for e in extra)
    extra = jnp.concatenate(extra + [jnp.zeros((short, model_width), single)], axis=0).T
    late_ref[:, 3 * width :] = extra.astype(bfloat)
    late_ref[:, 3 * width : 3 * width + 1] = (extra[:, :1] * total).astype(bfloat)


def attend_back(place, blocks, qkv, lse, rel, w_local, normed, gain, buckets, grad_gain, router, heads):
    n = len(blocks)
    full_len, model_width = normed.shape
    block_len = full_len // n
    width = heads * HD
    late_width = -(-(3 * width + 2 + heads + router.shape[0]) // 128) * 128
    vmem = pl.BlockSpec(memory_space=pltpu.VMEM)
    return pl.pallas_call(
        functools.partial(attend_back_kernel, n, heads),
        out_shape=(
            jax.ShapeDtypeStruct((n, block_len // 2, 6 * width), bfloat),
            jax.ShapeDtypeStruct((model_width, late_width), bfloat),
        ),
        in_specs=[pl.BlockSpec(memory_space=pltpu.SMEM)] + [vmem] * (n + 9),
        out_specs=(vmem,) * 2,
        scratch_shapes=[
            pltpu.VMEM((full_len, width), bfloat),
            pltpu.VMEM((heads, block_len, 2 * full_len), single),
            pltpu.VMEM((heads, block_len, 2 * full_len), single),
            pltpu.VMEM((heads, HD, full_len), single),
            pltpu.VMEM((heads, HD, full_len), single),
            pltpu.VMEM((full_len, 3 * width), bfloat),
            pltpu.VMEM((heads, 2 * full_len), single),
        ],
        compiler_params=pltpu.CompilerParams(vmem_limit_bytes=VMEM_LIMIT),
        cost_estimate=pl.CostEstimate(
            flops=int(19 * PER_MICRO),
            bytes_accessed=0,
            transcendentals=0,
        ),
        name="attend_back",
    )(place, *blocks, qkv, lse, rel, w_local, normed, gain, buckets, grad_gain, router)


def call(kernel, name, shapes, micros, *args, in_smem=(), scratch=()):
    vmem = pl.BlockSpec(memory_space=pltpu.VMEM)
    smem = pl.BlockSpec(memory_space=pltpu.SMEM)
    held = [(a.shape, a.dtype) for a in args] + list(shapes) + [(v.shape, v.dtype) for v in scratch]
    held = sum(math.prod(s) * jnp.dtype(t).itemsize for s, t in held)
    return pl.pallas_call(
        kernel,
        out_shape=[jax.ShapeDtypeStruct(s, t) for s, t in shapes],
        in_specs=[smem if i in in_smem else vmem for i in range(len(args))],
        out_specs=[vmem] * len(shapes),
        scratch_shapes=scratch,
        compiler_params=pltpu.CompilerParams(vmem_limit_bytes=held + ROOM if name in TIGHT else VMEM_LIMIT),
        cost_estimate=pl.CostEstimate(
            flops=int(micros * PER_MICRO), bytes_accessed=0, transcendentals=0
        ),
        name=name,
    )(*args)


def middle_kernel(n, *refs):
    parts = refs[:n]
    x_ref, w_ref, gain_ref, dispatch_ref, sent_ref, resid_ref, attn_ref = refs[n:]
    width = w_ref.shape[0] // n
    for r in range(n):
        attn_ref[:, r * width : (r + 1) * width] = unpack_rows(parts[r][...])
    resid = x_ref[...].astype(single) + dot_nn(attn_ref[...], w_ref[...])
    resid_ref[...] = resid
    normed = (resid * norm_scale(resid) * gain_ref[...]).astype(bfloat)
    sent_ref[...] = dot_nn(dispatch_ref[...], normed).astype(bfloat)


def expert_kernel(spot_ref, rows_ref, grad_ref, first_ref, second_ref, *refs):
    pieces, (router_ref, back_ref, scaled_ref, logits_ref) = refs[:6], refs[6:10]
    hidden_refs, pre_refs, others, sum_ref = refs[10:12], refs[12:14], refs[14:16], refs[16]
    for i, ref in enumerate(pieces):
        start = sum(p.shape[0] for p in pieces[i - i % 3 : i])
        others[i // 3][start : start + ref.shape[0], :] = ref[...]
    rows, grad_rows = rows_ref[...], grad_ref[...]
    count = rows.shape[0]
    half = first_ref.shape[1] // 2
    logits = dot_nn(rows, router_ref[...])
    expd = jnp.exp(logits - jnp.max(logits, axis=1, keepdims=True))
    probs = expd / jnp.sum(expd, axis=1, keepdims=True)
    hot = (lax.broadcasted_iota(jnp.int32, (1, logits.shape[1]), 1) == spot_ref[0]).astype(single)
    gate = jnp.sum(probs * hot, axis=1, keepdims=True)
    scaled_ref[...] = (gate * grad_rows.astype(single)).astype(bfloat)

    def step(piece, grad_gate):
        cols = pl.ds(pl.multiple_of(piece * half, half), half)
        back = jnp.zeros((count, 2 * half), single)
        for other, (first, second) in enumerate(((first_ref, second_ref), others)):
            pre = dot_nn(rows, first[:, cols])
            pull = dot_nt(grad_rows, second[cols, :])
            normal = 0.5 * (1.0 + lax.erf(pre * (0.5**0.5)))
            density = jnp.exp(-0.5 * pre * pre) * 0.3989422804014327
            hidden = pre * normal
            grad_gate += jnp.sum(hidden * pull, axis=1, keepdims=True)
            grad_pre = (gate * pull * (normal + pre * density)).astype(bfloat)
            hidden_refs[other][:, cols] = hidden.astype(bfloat)
            pre_refs[other][:, cols] = grad_pre
            back += dot_nt(grad_pre, first[:, cols])
        sum_ref[...] += back
        return grad_gate

    sum_ref[...] = jnp.zeros_like(sum_ref)
    grad_gate = lax.fori_loop(0, 2, step, jnp.zeros((count, 1), single))
    grad_logits = (grad_gate * probs * (hot - gate)).astype(bfloat)
    logits_ref[...] = grad_logits
    made = sum_ref[...] + dot_nt(grad_logits, router_ref[...])
    back_ref[...] = made.astype(back_ref.dtype)


def expert(spot, rows, grad_rows, first, second, pieces, w_router, kind):
    wide = rows.shape
    units = (rows.shape[0], first.shape[1])
    shapes = [(wide, kind), (wide, bfloat), ((wide[0], w_router.shape[1]), bfloat)]
    return call(
        expert_kernel, "expert", shapes + [(units, bfloat)] * 4, 7,
        spot, rows, grad_rows, first, second, *pieces, w_router, in_smem=(0,),
        scratch=[
            pltpu.VMEM(first.shape, bfloat),
            pltpu.VMEM(second.shape, bfloat),
            pltpu.VMEM(wide, single),
        ],
    )


def made_kernel(near_own, near_other, far_own, far_other, second_ref, *refs):
    pieces, (near_ref, far_ref, held_ref) = refs[:3], refs[3:]
    start = 0
    for ref in pieces:
        held_ref[start : start + ref.shape[0], :] = ref[...]
        start += ref.shape[0]
    for own, other, out in ((near_own, near_other, near_ref), (far_own, far_other, far_ref)):
        made = dot_nn(own[...], second_ref[...]) + dot_nn(other[...], held_ref[...])
        out[...] = made.astype(out.dtype)


def sums_kernel(near_left, far_left, near_right, far_right, top_ref, low_ref):
    cut = top_ref.shape[0]
    for ends, out in ((slice(0, cut), top_ref), (slice(cut, None), low_ref)):
        made = dot_tn(near_left[:, ends], near_right[...]) + dot_tn(far_left[:, ends], far_right[...])
        out[...] = made.astype(bfloat)


def own_kernel(near_left, far_left, near_right, far_right, top_ref, low_ref, out_ref):
    cut = top_ref.shape[0]
    for ends, got in ((slice(0, cut), top_ref), (slice(cut, None), low_ref)):
        made = dot_tn(near_left[:, ends], near_right[...]) + dot_tn(far_left[:, ends], far_right[...])
        out_ref[ends, :] = made + got[...].astype(single)


def join_kernel(late_ref, *refs):
    *blocks, out_ref = refs
    count, step, wide = late_ref.shape
    late = late_ref[0].astype(single)
    for i in range(1, count):
        late += late_ref[i].astype(single)
    out_ref[:, :wide] = late.astype(bfloat)
    total = sum(b[...].astype(single) for b in blocks[1:]) + blocks[0][...].astype(single)
    rows = total.shape[0]
    cuts = step // rows
    width = total.shape[1] // cuts
    folded = jnp.concatenate([total[:, i * width : (i + 1) * width] for i in range(cuts)], axis=0)
    spare = jnp.zeros((step, out_ref.shape[1] - wide - width), single)
    out_ref[:, wide:] = jnp.concatenate([folded, spare], axis=1).astype(bfloat)


def stack_kernel(*refs):
    *ins, out_ref = refs
    for i, ref in enumerate(ins):
        out_ref[i] = ref[...]


def layer_kernel(made_ref, dispatch_ref, resid_ref, gain_ref, router_ref, hot_ref, out_ref):
    resid = resid_ref[...]
    normed = (resid * norm_scale(resid) * gain_ref[...]).astype(bfloat)
    logits = dot_nn(normed, router_ref[...])
    expd = jnp.exp(logits - jnp.max(logits, axis=1, keepdims=True))
    probs = expd / jnp.sum(expd, axis=1, keepdims=True)
    gate = jnp.sum(probs * hot_ref[...].astype(single), axis=1, keepdims=True)
    out_ref[...] = (resid + gate * dot_nn(dispatch_ref[...], made_ref[...])).astype(bfloat)


def last_kernel(n, *refs):
    parts_ref, w_ref, x_ref, gain_ref, resid_ref, out_ref = refs
    width = w_ref.shape[1] // n
    grad_normed = jnp.zeros(x_ref.shape, single)
    for r in range(n):
        cols = slice(r * width, (r + 1) * width)
        grad_normed += dot_nt(unpack_rows(parts_ref[r]), w_ref[:, cols])
    row_data = x_ref[...].astype(single)
    back = norm_back(grad_normed, row_data, norm_scale(row_data), gain_ref[...])
    out_ref[...] = (resid_ref[...] + back).astype(bfloat)


def post_kernel(n, back_ref, dispatch_ref, resid_ref, grad_ref, gain_ref, w_ref, *refs):
    attn_refs, (resid_out, branch_ref, gain_out) = refs[:n], refs[n:]
    width = w_ref.shape[0] // n
    grad_normed = dot_nn(dispatch_ref[...], back_ref[...])
    resid = resid_ref[...]
    scale = norm_scale(resid)
    gain_out[...] = jnp.sum(grad_normed * resid * scale, axis=0, keepdims=True)
    grad_resid = grad_ref[...].astype(single) + norm_back(grad_normed, resid, scale, gain_ref[...])
    resid_out[...] = grad_resid
    branch = grad_resid.astype(bfloat)
    branch_ref[...] = branch
    grad_attn = dot_nt(branch, w_ref[...]).astype(bfloat)
    for r in range(n):
        attn_refs[r][...] = pack_rows(grad_attn[:, r * width : (r + 1) * width])


def shift(block, by):
    n = lax.axis_size("ctx")
    return lax.ppermute(block, "ctx", [(i, (i + by) % n) for i in range(n)])


def swap_plane(block, mask):
    count = lax.axis_size(PLANE)
    return lax.ppermute(block, PLANE, [(i, i ^ mask) for i in range(count)])


def to_plane(blocks):
    return lax.all_to_all(blocks, PLANE, split_axis=0, concat_axis=0, tiled=True)


def sum_first(parts):
    return jnp.sum(parts.astype(single), axis=0).astype(bfloat)


def gather_chips(stack):
    count = lax.axis_size(PLANE)
    core = lax.axis_size("expert")
    return {mask: swap_plane(stack, mask) if mask else stack for mask in range(count) if not mask & core}


def gather_cores(held):
    core = lax.axis_size("expert")
    held = {**held, **{mask | core: swap_plane(held[mask], core) for mask in held}}
    return [held[mask] for mask in sorted(held)]


def tied(*arrays):
    return lax.optimization_barrier(arrays)


def late_extras(extra, heads, experts):
    rows = sum(extra[1:], extra[0]).T
    table = jnp.concatenate([e[:NB].T[1 : 1 + heads] for e in extra], axis=0)
    return rows[0], rows[1 + heads], table, rows[2 + heads : 2 + heads + experts]


def place_kernel(count, n, heads, experts, spot_ref, *refs):
    spot, place = spot_ref[0], spot_ref[1]
    ins, outs, small, extra_ref = refs[:count], refs[count : count + 4], refs[count + 4 : -1], refs[-1]
    step = ins[0].shape[1]
    width = heads * HD
    wide = 3 * width + extra_ref.shape[2]
    for mask in range(count):
        there = spot ^ mask
        rows = pl.ds(pl.multiple_of(there * step, step), step)
        for c in range(n):
            block = ins[mask][lax.rem(place - c + n, n)].astype(single)
            for i in range(3):
                outs[i][rows, c * width : (c + 1) * width] = block[:, i * width : (i + 1) * width]
            extra_ref[c, rows, :] = block[:, 3 * width : wide]
            part = step // n
            at = pl.ds(pl.multiple_of(c * width + there * part, part), part)
            for i in range(n):
                outs[3][at, i * width : (i + 1) * width] = block[
                    i * part : (i + 1) * part, wide : wide + width
                ]
    made = late_extras([extra_ref[c] for c in range(n)], heads, experts)
    for ref, value in zip(small, made):
        ref[...] = value


def placed(kernel, spots, held, shapes, scratch=()):
    vmem = pl.BlockSpec(memory_space=pltpu.VMEM)
    return pl.pallas_call(
        kernel,
        out_shape=[jax.ShapeDtypeStruct(s, single) for s in shapes],
        in_specs=[pl.BlockSpec(memory_space=pltpu.SMEM)] + [vmem] * len(held),
        out_specs=[vmem] * len(shapes),
        scratch_shapes=scratch,
        compiler_params=pltpu.CompilerParams(vmem_limit_bytes=VMEM_LIMIT),
        cost_estimate=pl.CostEstimate(
            flops=int(5 * PER_MICRO), bytes_accessed=0, transcendentals=0
        ),
        name="placed",
    )(spots, *held)


def spots():
    return jnp.stack([lax.axis_index(PLANE), lax.axis_index("ctx")]).astype(jnp.int32)


def place_all(held, heads, model_width, experts, late_width):
    n, step, _ = held[0].shape
    width = heads * HD
    shapes = [(model_width, n * width)] * 3 + [(n * width, model_width)]
    if step % (8 * n):
        place, spot = lax.axis_index("ctx"), lax.axis_index(PLANE)
        whole = jnp.zeros((n, len(held), *held[0].shape[1:]), single)
        for mask, stack in enumerate(held):
            for r in range(n):
                where = ((place - r) % n, spot ^ mask, 0, 0)
                whole = lax.dynamic_update_slice(whole, stack[r][None, None].astype(single), where)
        late = whole.reshape(n, model_width, -1)
        own = [late[:, :, i * width : (i + 1) * width] for i in range(3)]
        own = [o.transpose(1, 0, 2).reshape(model_width, n * width) for o in own]
        last = whole[..., late_width : late_width + width]
        last = last.reshape(n, len(held), n, step // n, width).transpose(0, 1, 3, 2, 4)
        extra = [w[:, 3 * width : late_width] for w in late]
        return own + [last.reshape(n * width, model_width)] + list(late_extras(extra, heads, experts))
    shapes += [(model_width,), (model_width,), (n * heads, NB), (experts, model_width)]
    kernel = functools.partial(place_kernel, len(held), n, heads, experts)
    scratch = [pltpu.VMEM((n, model_width, late_width - 3 * width), single)]
    return placed(kernel, spots(), held, shapes, scratch)


def shards(
    tokens,
    cotangent,
    routes,
    buckets,
    gain_attn,
    w_query,
    w_key,
    w_value,
    w_output,
    bias_table,
    gain_ffn,
    w_router,
    w_in,
    w_out,
):
    seq_dev, block_len, model_width = tokens.shape
    n = lax.axis_size("ctx")
    experts = lax.axis_size(PLANE)
    heads = H // n
    width = heads * HD
    full_len = block_len * n
    tok_count = seq_dev * block_len
    capacity = max(2, (5 * tok_count + 4 * experts - 1) // (4 * experts))
    slots = experts * capacity
    place = lax.axis_index("ctx")
    spot = lax.axis_index(PLANE)
    place_in = place.astype(jnp.int32).reshape(1)

    block = tokens.reshape(tok_count, model_width)
    blocks = [block] + [shift(block, r) for r in range(1, n)]

    own_heads = [
        lax.dynamic_slice_in_dim(w, place * width, width, 1) for w in (w_query, w_key, w_value)
    ]
    w_local = jnp.concatenate(own_heads, axis=1)
    turned = [
        lax.dynamic_slice_in_dim(w_output, (place - r) % n * width, width, 0) for r in range(n)
    ]
    w_turned = jnp.concatenate(turned, axis=0)
    w_all = jnp.concatenate(
        [
            w[:, r * width : (r + 1) * width]
            for r in range(n)
            for w in (w_query, w_key, w_value)
        ],
        axis=1,
    )
    bucket_hot = (buckets[:, None] == jnp.arange(NB, dtype=jnp.int32)[None, :]).astype(single)
    table_local = lax.dynamic_slice_in_dim(bias_table, place * heads, heads, 1)
    rel = lax.dot_general(
        table_local, bucket_hot, (((0,), (1,)), ((), ())), precision=exact_prec
    )
    rel = jnp.pad(rel, ((0, 0), (0, 1)))
    route_flat = routes.reshape(tok_count)
    route_hot = (
        route_flat[:, None] == jnp.arange(experts, dtype=jnp.int32)[None, :]
    ).astype(bfloat)
    earlier = jnp.tril(jnp.ones((tok_count, tok_count), bfloat), -1)
    counts = dot_nn(earlier, route_hot)
    slot_index = jnp.sum(counts * route_hot.astype(single), axis=1).astype(jnp.int32)
    target = jnp.where(slot_index < capacity, route_flat * capacity + slot_index, -1)
    dispatch_mat = (target[:, None] == jnp.arange(slots, dtype=jnp.int32)[None, :]).astype(bfloat)
    dispatch_turned = dispatch_mat.T
    gain_one, gain_two = gain_attn.reshape(1, -1), gain_ffn.reshape(1, -1)
    spot_in = spot.astype(jnp.int32).reshape(1)
    buckets_row = jnp.pad(buckets, (0, 1)).reshape(1, -1)

    grad_block = cotangent.reshape(tok_count, model_width)
    grad_sent = dot_nn(dispatch_turned, grad_block).astype(bfloat)
    grad_near = to_plane(grad_sent.reshape(experts, capacity, model_width))
    grad_near = grad_near.reshape(slots, model_width)

    pair = [(i, i ^ 1) for i in range(n)]
    half = model_width // 2

    def swap(piece):
        return lax.ppermute(piece, "ctx", pair)

    first_own, second_own = w_in[0], w_out[0]
    low, high = (cut * model_width // 8 for cut in CUTS)
    pieces = [w[a:b] for w in (first_own, second_own) for a, b in ((0, low), (low, high), (high, None))]
    pieces[0] = swap(pieces[0])
    blocks, pieces, gain_one, gain_two, grad_near, w_local, w_turned, rel, dispatches = tied(
        blocks, pieces, gain_one, gain_two, grad_near, w_local, w_turned, rel,
        (dispatch_mat, dispatch_turned),
    )
    dispatch_mat, dispatch_turned = dispatches
    pieces[1] = swap(pieces[1])

    normed_all, qkv, lse, *attn_parts = attend(place_in, blocks, gain_one, w_local, rel, heads)
    attn_parts, pieces = tied(attn_parts, pieces)
    attn_turned = [attn_parts[0]] + [shift(attn_parts[r], r) for r in range(1, n)]
    pieces[2], pieces[3] = swap(pieces[2]), swap(pieces[3])
    attn_turned, grad_near, pieces, w_all = tied(attn_turned, grad_near, pieces, w_all)
    grad_far = shift(grad_near, n // 2)
    pieces[4] = swap(pieces[4])
    rows_shape = (tok_count, model_width)
    sent, resid, attn_rows = call(
        functools.partial(middle_kernel, n),
        "middle",
        [((slots, model_width), bfloat), (rows_shape, single), (rows_shape, bfloat)],
        3,
        *attn_turned, block, w_turned, gain_two, dispatch_turned,
    )
    near = to_plane(sent.reshape(experts, capacity, model_width)).reshape(slots, model_width)
    near, grad_far, pieces = tied(near, grad_far, pieces)
    far = shift(near, n // 2)
    pieces[5] = swap(pieces[5])

    near_back, near_scaled, near_logits, *near_parts = expert(
        spot_in, near, grad_near, first_own, second_own, pieces, w_router, single
    )
    far, near_back = tied(far, near_back)
    far_back, far_scaled, far_logits, *far_parts = expert(
        spot_in, far, grad_far, first_own, second_own, pieces, w_router, bfloat
    )
    back_got = shift(far_back, n // 2)

    cut = 19 * model_width // 48
    cuts = [((cut, model_width), bfloat), ((model_width - cut, model_width), bfloat)]
    near_made, far_made = call(
        made_kernel,
        "made",
        [((slots, model_width), single), ((slots, model_width), bfloat)],
        0,
        *near_parts[:2], *far_parts[:2], second_own, *pieces[3:],
        scratch=[pltpu.VMEM(second_own.shape, bfloat)],
    )
    sends = list(call(sums_kernel, "sums", cuts, 0, near, far, near_parts[3], far_parts[3]))
    sends[0] = swap(sends[0])
    back_got, sends, near_made, far_made, near_parts, far_parts = tied(
        back_got, sends, near_made, far_made, near_parts, far_parts
    )
    sends[1] = swap(sends[1])
    back_sum = (near_back + back_got.astype(single)).astype(bfloat)
    back_home = to_plane(back_sum.reshape(experts, capacity, model_width))
    third = model_width // 3
    thirds = [((third, model_width), bfloat), ((model_width - third, model_width), bfloat)]
    sends += call(
        sums_kernel, "sums", thirds, 3, near_parts[1], far_parts[1], near_scaled, far_scaled
    )
    grad_router = dot_tn(near_logits, near) + dot_tn(far_logits, far)

    *attn_grads, grad_resid, grad_branch, grad_gain_ffn = call(
        functools.partial(post_kernel, n),
        "post",
        [((tok_count // 2, 2 * width), bfloat)] * n
        + [(rows_shape, single), (rows_shape, bfloat), ((1, model_width), single)],
        4,
        back_home.reshape(slots, model_width), dispatch_mat, resid, grad_block, gain_two, w_turned,
    )
    attn_grads, grad_branch, sends[0], *sends[2:] = tied(attn_grads, grad_branch, sends[0], *sends[2:])
    attn_grads = [attn_grads[0]] + [shift(attn_grads[r], n - r) for r in range(1, n)]

    count = lax.axis_size(PLANE)
    grad_output = dot_tn(attn_rows, grad_branch).astype(bfloat)
    grad_output = grad_output.reshape(n, count, width // count, model_width)
    grad_output = lax.all_to_all(grad_output, PLANE, split_axis=1, concat_axis=1, tiled=True)
    *attn_grads, far_made, sends[1], sends[2], grad_router = tied(
        *attn_grads, far_made, sends[1], sends[2], grad_router
    )
    made_got = shift(far_made, n // 2)
    sends[2] = lax.ppermute(sends[2], "ctx", pair)

    parts, late = attend_back(
        place_in, attn_grads, qkv, lse, rel, w_local, normed_all, gain_one, buckets_row,
        grad_gain_ffn, grad_router, heads
    )
    late, made_got, sends, grad_output = tied(late, made_got, sends, grad_output)
    late_width = late.shape[1]
    late = to_plane(late.reshape(count, model_width // count, late_width))
    grad_output = sum_first(grad_output.transpose(1, 0, 2, 3))
    shares = [grad_output[0]] + [shift(grad_output[r], n - r) for r in range(1, n)]
    made_sum = (near_made + made_got.astype(single)).astype(bfloat)
    shares, sends[3] = tied(shares, sends[3])
    sends[3] = swap(sends[3])
    late, made_sum, far_parts, shares = tied(late, made_sum, far_parts, shares)
    step = model_width // count
    (piece,) = call(
        join_kernel, "join", [((step, late_width + -(-width // 128) * 128), bfloat)], 1, late, *shares
    )
    pieces = [piece] + [shift(piece, r) for r in range(1, n)]
    made_home = to_plane(made_sum.reshape(experts, capacity, model_width))
    (grad_first,) = call(
        own_kernel, "own", [((model_width, model_width), single)], 4,
        near, far, near_parts[2], far_parts[2], *sends[:2],
    )
    pieces, parts, made_home, grad_first, sends = tied(pieces, parts, made_home, grad_first, sends)
    (stack,) = call(stack_kernel, "stack", [((n, *piece.shape), bfloat)], 1, *pieces)
    held = gather_chips(stack)
    parts = lax.all_to_all(parts, "ctx", split_axis=0, concat_axis=0, tiled=True)
    (layer_out,) = call(
        layer_kernel, "layer", [(rows_shape, bfloat)], 3,
        made_home.reshape(slots, model_width), dispatch_mat, resid, gain_two, w_router, route_hot,
    )
    (grad_tokens,) = call(
        functools.partial(last_kernel, n), "last", [(rows_shape, bfloat)], 4,
        parts, w_all, block, gain_one, grad_resid,
    )
    (grad_second,) = call(
        own_kernel, "own", [((model_width, model_width), single)], 4,
        near_parts[0], far_parts[0], near_scaled, far_scaled, *sends[2:],
    )
    held, layer_out, grad_tokens, grad_second = tied(held, layer_out, grad_tokens, grad_second)
    (grad_query, grad_key, grad_value, output_all, grad_gain_attn, grad_gain_ffn, grad_table,
     grad_router) = place_all(gather_cores(held), heads, model_width, experts, late_width)
    return (
        layer_out.reshape(seq_dev, block_len, model_width).astype(bfloat),
        grad_tokens.reshape(seq_dev, block_len, model_width).astype(bfloat),
        grad_gain_attn,
        grad_query,
        grad_key,
        grad_value,
        output_all,
        grad_table.T,
        grad_gain_ffn,
        grad_router.T,
        grad_first[None],
        grad_second[None],
    )


def solution(mesh):
    spread = P(("dp", "expert"), "ctx", None)
    first = P(("dp", "expert"), None, "ctx")
    return jax.shard_map(
        shards,
        mesh=mesh,
        in_specs=(spread,) * 3 + (P(),) * 9 + (first, spread),
        out_specs=(spread,) * 2 + (P(),) * 8 + (first, spread),
        check_vma=False,
    )
```

```python
import functools
import math

import jax
import jax.numpy as jnp
from jax import lax
from jax.experimental import pallas as pl
from jax.experimental.pallas import tpu as pltpu
from jax.sharding import PartitionSpec as P

H = 12
HD = 64
NB = 32
PLANE = ("dp", "expert")

epsilon = 1e-06
exact_prec = lax.Precision.HIGHEST
bfloat = jnp.bfloat16
single = jnp.float32
VMEM_LIMIT = 56 * 1024 * 1024
ROOM = 8 * 1024 * 1024
TIGHT = ("own", "layer")
PER_MICRO = 1.15e9
CUTS = (2, 6)


def norm_scale(row_data):
    return lax.rsqrt(jnp.mean(row_data * row_data, axis=-1, keepdims=True) + epsilon)


def norm_back(grad_in, row_data, scale, gain):
    weighted = grad_in * gain
    inner = jnp.mean(weighted * row_data, axis=-1, keepdims=True)
    return scale * weighted - row_data * (scale * scale * scale) * inner


def dot_nn(left, right):
    return lax.dot_general(
        left, right, (((1,), (0,)), ((), ())), preferred_element_type=single
    )


def dot_nt(left, right):
    return lax.dot_general(
        left, right, (((1,), (1,)), ((), ())), preferred_element_type=single
    )


def dot_tn(left, right):
    return lax.dot_general(
        left, right, (((0,), (0,)), ((), ())), preferred_element_type=single
    )


def pack_rows(rows):
    half = rows.shape[0] // 2
    return jnp.concatenate([rows[:half], rows[half:]], axis=1)


def unpack_rows(packed):
    width = packed.shape[1] // 2
    return jnp.concatenate([packed[:, :width], packed[:, width:]], axis=0)


def bias_strip(rel_row, rows, width):
    spread = jnp.broadcast_to(rel_row, (rows, width))
    return pltpu.roll(spread, width - (rows - 1), 1, stride=1, stride_axis=0)


def fold_strip(strip):
    rows = strip.shape[0]
    while rows > 1:
        rows //= 2
        strip = strip[rows:] + pltpu.roll(strip[:rows], rows, 1)
    return strip


def attend_kernel(n, heads, place_ref, *refs):
    blocks = refs[:n]
    gain_ref, w_ref, rel_ref, normed_ref, qkv_ref, lse_ref, *out_refs, strip_ref, out_ref = refs[n:]
    place = place_ref[0]
    block_len = blocks[0].shape[0]
    full_len = n * block_len
    width = heads * HD
    for r in range(n):
        start = pl.multiple_of(lax.rem(place - r + n, n) * block_len, block_len)
        row_data = blocks[r][...].astype(single)
        normed = (row_data * norm_scale(row_data) * gain_ref[...]).astype(bfloat)
        normed_ref[pl.ds(start, block_len), :] = normed
        qkv_ref[pl.ds(start, block_len), :] = dot_nn(normed, w_ref[...]).astype(bfloat)
    for h in range(heads):
        strip_ref[h] = bias_strip(rel_ref[h : h + 1, :], block_len, 2 * full_len)
    lse_ref[...] = jnp.zeros_like(lse_ref)

    def tile(t, carry):
        rows = pl.ds(pl.multiple_of(t * block_len, block_len), block_len)
        skew = pl.ds(pl.multiple_of((n - 1 - t) * block_len, block_len), full_len)
        made = []
        for h in range(heads):
            query = qkv_ref[rows, h * HD : (h + 1) * HD]
            key = qkv_ref[:, width + h * HD : width + (h + 1) * HD]
            value = qkv_ref[:, 2 * width + h * HD : 2 * width + (h + 1) * HD]
            scores = dot_nt(query, key) + strip_ref[h, :, skew]
            top = jnp.max(scores, axis=1, keepdims=True)
            expd = jnp.exp(scores - top)
            total = jnp.sum(expd, axis=1, keepdims=True)
            made.append(dot_nn(expd.astype(bfloat), value) / total)
            lse_ref[rows, h : h + 1] = top + jnp.log(total)
        joined = jnp.concatenate(made, axis=1).astype(bfloat)
        out_ref[lax.rem(t - place + n, n)] = pack_rows(joined)
        return carry

    lax.fori_loop(0, n, tile, 0, unroll=1)
    for r in range(n):
        out_refs[r][...] = out_ref[r]


def attend(place, blocks, gain, w_local, rel, heads):
    n = len(blocks)
    block_len, model_width = blocks[0].shape
    full_len = n * block_len
    width = heads * HD
    vmem = pl.BlockSpec(memory_space=pltpu.VMEM)
    return pl.pallas_call(
        functools.partial(attend_kernel, n, heads),
        out_shape=(
            jax.ShapeDtypeStruct((full_len, model_width), bfloat),
            jax.ShapeDtypeStruct((full_len, 3 * width), bfloat),
            jax.ShapeDtypeStruct((full_len, 128), single),
            *[jax.ShapeDtypeStruct((block_len // 2, 2 * width), bfloat)] * n,
        ),
        in_specs=[pl.BlockSpec(memory_space=pltpu.SMEM)] + [vmem] * (n + 3),
        out_specs=(vmem,) * (n + 3),
        scratch_shapes=[
            pltpu.VMEM((heads, block_len, 2 * full_len), single),
            pltpu.VMEM((n, block_len // 2, 2 * width), bfloat),
        ],
        compiler_params=pltpu.CompilerParams(vmem_limit_bytes=VMEM_LIMIT),
        cost_estimate=pl.CostEstimate(
            flops=int(11 * PER_MICRO),
            bytes_accessed=0,
            transcendentals=0,
        ),
        name="attend",
    )(place, *blocks, gain, w_local, rel)


def attend_back_kernel(n, heads, place_ref, *refs):
    blocks = refs[:n]
    (qkv_ref, lse_ref, rel_ref, w_ref, normed_ref, gain_ref, buckets_ref, grad_gain_ref, router_ref,
     part_ref, late_ref,
     da_ref, strip_ref, sums_ref, key_acc, value_acc, dqkv_ref, rel_out_ref) = refs[n:]
    place = place_ref[0]
    block_len = blocks[0].shape[0] * 2
    full_len = n * block_len
    width = heads * HD
    model_width = normed_ref.shape[1]
    for r in range(n):
        start = pl.multiple_of(lax.rem(place + r, n) * block_len, block_len)
        da_ref[pl.ds(start, block_len), :] = unpack_rows(blocks[r][...])
    for h in range(heads):
        strip_ref[h] = bias_strip(rel_ref[h : h + 1, :], block_len, 2 * full_len)
    sums_ref[...] = jnp.zeros_like(sums_ref)
    key_acc[...] = jnp.zeros_like(key_acc)
    value_acc[...] = jnp.zeros_like(value_acc)

    def tile(t, carry):
        rows = pl.ds(pl.multiple_of(t * block_len, block_len), block_len)
        skew = pl.ds(pl.multiple_of((n - 1 - t) * block_len, block_len), full_len)
        for h in range(heads):
            query = qkv_ref[rows, h * HD : (h + 1) * HD]
            key = qkv_ref[:, width + h * HD : width + (h + 1) * HD]
            value = qkv_ref[:, 2 * width + h * HD : 2 * width + (h + 1) * HD]
            grad_attn = da_ref[rows, h * HD : (h + 1) * HD]
            scores = dot_nt(query, key) + strip_ref[h, :, skew]
            soft = jnp.exp(scores - lse_ref[rows, h : h + 1])
            value_acc[h] += dot_tn(grad_attn, soft.astype(bfloat))
            grad_soft = dot_nt(grad_attn, value)
            delta = jnp.sum(soft * grad_soft, axis=1, keepdims=True)
            grad_wide = soft * (grad_soft - delta)
            sums_ref[h, :, skew] += grad_wide
            grad_scores = grad_wide.astype(bfloat)
            dqkv_ref[rows, h * HD : (h + 1) * HD] = dot_nn(grad_scores, key).astype(bfloat)
            key_acc[h] += dot_tn(query, grad_scores)
        return carry

    lax.fori_loop(0, n, tile, 0, unroll=4)
    for h in range(heads):
        dqkv_ref[:, width + h * HD : width + (h + 1) * HD] = key_acc[h].T.astype(bfloat)
        dqkv_ref[:, 2 * width + h * HD : 2 * width + (h + 1) * HD] = value_acc[h].T.astype(bfloat)
        rel_out_ref[h : h + 1, :] = fold_strip(sums_ref[h])
    for r in range(n):
        part_ref[r] = pack_rows(dqkv_ref[r * block_len : (r + 1) * block_len, :])
    made = dot_tn(normed_ref[...], dqkv_ref[...])
    late_ref[:, : 3 * width] = made.astype(bfloat)
    total = jnp.sum(made * w_ref[...].astype(single), axis=1, keepdims=True)
    kinds = lax.broadcasted_iota(jnp.int32, (NB, 2 * full_len), 0)
    hot = (kinds == buckets_ref[...]).astype(single)
    table = lax.dot_general(
        rel_out_ref[...], hot, (((1,), (1,)), ((), ())),
        precision=exact_prec, preferred_element_type=single,
    )
    table = jnp.concatenate([table, jnp.zeros((heads, model_width - NB), single)], axis=1)
    extra = [1.0 / gain_ref[...], table, grad_gain_ref[...], router_ref[...]]
    short = late_ref.shape[1] - 3 * width - sum(e.shape[0] for e in extra)
    extra = jnp.concatenate(extra + [jnp.zeros((short, model_width), single)], axis=0).T
    late_ref[:, 3 * width :] = extra.astype(bfloat)
    late_ref[:, 3 * width : 3 * width + 1] = (extra[:, :1] * total).astype(bfloat)


def attend_back(place, blocks, qkv, lse, rel, w_local, normed, gain, buckets, grad_gain, router, heads):
    n = len(blocks)
    full_len, model_width = normed.shape
    block_len = full_len // n
    width = heads * HD
    late_width = -(-(3 * width + 2 + heads + router.shape[0]) // 128) * 128
    vmem = pl.BlockSpec(memory_space=pltpu.VMEM)
    return pl.pallas_call(
        functools.partial(attend_back_kernel, n, heads),
        out_shape=(
            jax.ShapeDtypeStruct((n, block_len // 2, 6 * width), bfloat),
            jax.ShapeDtypeStruct((model_width, late_width), bfloat),
        ),
        in_specs=[pl.BlockSpec(memory_space=pltpu.SMEM)] + [vmem] * (n + 9),
        out_specs=(vmem,) * 2,
        scratch_shapes=[
            pltpu.VMEM((full_len, width), bfloat),
            pltpu.VMEM((heads, block_len, 2 * full_len), single),
            pltpu.VMEM((heads, block_len, 2 * full_len), single),
            pltpu.VMEM((heads, HD, full_len), single),
            pltpu.VMEM((heads, HD, full_len), single),
            pltpu.VMEM((full_len, 3 * width), bfloat),
            pltpu.VMEM((heads, 2 * full_len), single),
        ],
        compiler_params=pltpu.CompilerParams(vmem_limit_bytes=VMEM_LIMIT),
        cost_estimate=pl.CostEstimate(
            flops=int(19 * PER_MICRO),
            bytes_accessed=0,
            transcendentals=0,
        ),
        name="attend_back",
    )(place, *blocks, qkv, lse, rel, w_local, normed, gain, buckets, grad_gain, router)


def call(kernel, name, shapes, micros, *args, in_smem=(), scratch=()):
    vmem = pl.BlockSpec(memory_space=pltpu.VMEM)
    smem = pl.BlockSpec(memory_space=pltpu.SMEM)
    held = [(a.shape, a.dtype) for a in args] + list(shapes) + [(v.shape, v.dtype) for v in scratch]
    held = sum(math.prod(s) * jnp.dtype(t).itemsize for s, t in held)
    return pl.pallas_call(
        kernel,
        out_shape=[jax.ShapeDtypeStruct(s, t) for s, t in shapes],
        in_specs=[smem if i in in_smem else vmem for i in range(len(args))],
        out_specs=[vmem] * len(shapes),
        scratch_shapes=scratch,
        compiler_params=pltpu.CompilerParams(vmem_limit_bytes=held + ROOM if name in TIGHT else VMEM_LIMIT),
        cost_estimate=pl.CostEstimate(
            flops=int(micros * PER_MICRO), bytes_accessed=0, transcendentals=0
        ),
        name=name,
    )(*args)


def middle_kernel(n, *refs):
    parts = refs[:n]
    x_ref, w_ref, gain_ref, dispatch_ref, sent_ref, resid_ref, attn_ref = refs[n:]
    width = w_ref.shape[0] // n
    for r in range(n):
        attn_ref[:, r * width : (r + 1) * width] = unpack_rows(parts[r][...])
    resid = x_ref[...].astype(single) + dot_nn(attn_ref[...], w_ref[...])
    resid_ref[...] = resid
    normed = (resid * norm_scale(resid) * gain_ref[...]).astype(bfloat)
    sent_ref[...] = dot_nn(dispatch_ref[...], normed).astype(bfloat)


def expert_kernel(spot_ref, rows_ref, grad_ref, first_ref, second_ref, *refs):
    pieces, (router_ref, back_ref, scaled_ref, logits_ref) = refs[:6], refs[6:10]
    hidden_refs, pre_refs, others, sum_ref = refs[10:12], refs[12:14], refs[14:16], refs[16]
    for i, ref in enumerate(pieces):
        start = sum(p.shape[0] for p in pieces[i - i % 3 : i])
        others[i // 3][start : start + ref.shape[0], :] = ref[...]
    rows, grad_rows = rows_ref[...], grad_ref[...]
    count = rows.shape[0]
    half = first_ref.shape[1] // 2
    logits = dot_nn(rows, router_ref[...])
    expd = jnp.exp(logits - jnp.max(logits, axis=1, keepdims=True))
    probs = expd / jnp.sum(expd, axis=1, keepdims=True)
    hot = (lax.broadcasted_iota(jnp.int32, (1, logits.shape[1]), 1) == spot_ref[0]).astype(single)
    gate = jnp.sum(probs * hot, axis=1, keepdims=True)
    scaled_ref[...] = (gate * grad_rows.astype(single)).astype(bfloat)

    def step(piece, grad_gate):
        cols = pl.ds(pl.multiple_of(piece * half, half), half)
        back = jnp.zeros((count, 2 * half), single)
        for other, (first, second) in enumerate(((first_ref, second_ref), others)):
            pre = dot_nn(rows, first[:, cols])
            pull = dot_nt(grad_rows, second[cols, :])
            normal = 0.5 * (1.0 + lax.erf(pre * (0.5**0.5)))
            density = jnp.exp(-0.5 * pre * pre) * 0.3989422804014327
            hidden = pre * normal
            grad_gate += jnp.sum(hidden * pull, axis=1, keepdims=True)
            grad_pre = (gate * pull * (normal + pre * density)).astype(bfloat)
            hidden_refs[other][:, cols] = hidden.astype(bfloat)
            pre_refs[other][:, cols] = grad_pre
            back += dot_nt(grad_pre, first[:, cols])
        sum_ref[...] += back
        return grad_gate

    sum_ref[...] = jnp.zeros_like(sum_ref)
    grad_gate = lax.fori_loop(0, 2, step, jnp.zeros((count, 1), single))
    grad_logits = (grad_gate * probs * (hot - gate)).astype(bfloat)
    logits_ref[...] = grad_logits
    made = sum_ref[...] + dot_nt(grad_logits, router_ref[...])
    back_ref[...] = made.astype(back_ref.dtype)


def expert(spot, rows, grad_rows, first, second, pieces, w_router, kind):
    wide = rows.shape
    units = (rows.shape[0], first.shape[1])
    shapes = [(wide, kind), (wide, bfloat), ((wide[0], w_router.shape[1]), bfloat)]
    return call(
        expert_kernel, "expert", shapes + [(units, bfloat)] * 4, 7,
        spot, rows, grad_rows, first, second, *pieces, w_router, in_smem=(0,),
        scratch=[
            pltpu.VMEM(first.shape, bfloat),
            pltpu.VMEM(second.shape, bfloat),
            pltpu.VMEM(wide, single),
        ],
    )


def made_kernel(near_own, near_other, far_own, far_other, second_ref, *refs):
    pieces, (near_ref, far_ref, held_ref) = refs[:3], refs[3:]
    start = 0
    for ref in pieces:
        held_ref[start : start + ref.shape[0], :] = ref[...]
        start += ref.shape[0]
    for own, other, out in ((near_own, near_other, near_ref), (far_own, far_other, far_ref)):
        made = dot_nn(own[...], second_ref[...]) + dot_nn(other[...], held_ref[...])
        out[...] = made.astype(out.dtype)


def pieces_of(refs):
    start = 0
    for ref in refs:
        yield slice(start, start + ref.shape[0]), ref
        start += ref.shape[0]


def sums_kernel(near_left, far_left, near_right, far_right, *outs):
    for ends, out in pieces_of(outs):
        made = dot_tn(near_left[:, ends], near_right[...]) + dot_tn(far_left[:, ends], far_right[...])
        out[...] = made.astype(bfloat)


def own_kernel(near_left, far_left, near_right, far_right, *refs):
    *pieces, out_ref = refs
    for ends, got in pieces_of(pieces):
        made = dot_tn(near_left[:, ends], near_right[...]) + dot_tn(far_left[:, ends], far_right[...])
        out_ref[ends, :] = made + got[...].astype(single)


def join_kernel(late_ref, *refs):
    *blocks, out_ref = refs
    count, step, wide = late_ref.shape
    late = late_ref[0].astype(single)
    for i in range(1, count):
        late += late_ref[i].astype(single)
    out_ref[:, :wide] = late.astype(bfloat)
    total = sum(b[...].astype(single) for b in blocks[1:]) + blocks[0][...].astype(single)
    rows = total.shape[0]
    cuts = step // rows
    width = total.shape[1] // cuts
    folded = jnp.concatenate([total[:, i * width : (i + 1) * width] for i in range(cuts)], axis=0)
    spare = jnp.zeros((step, out_ref.shape[1] - wide - width), single)
    out_ref[:, wide:] = jnp.concatenate([folded, spare], axis=1).astype(bfloat)


def stack_kernel(*refs):
    *ins, out_ref = refs
    for i, ref in enumerate(ins):
        out_ref[i] = ref[...]


def layer_kernel(made_ref, dispatch_ref, resid_ref, gain_ref, router_ref, hot_ref, out_ref):
    resid = resid_ref[...]
    normed = (resid * norm_scale(resid) * gain_ref[...]).astype(bfloat)
    logits = dot_nn(normed, router_ref[...])
    expd = jnp.exp(logits - jnp.max(logits, axis=1, keepdims=True))
    probs = expd / jnp.sum(expd, axis=1, keepdims=True)
    gate = jnp.sum(probs * hot_ref[...].astype(single), axis=1, keepdims=True)
    out_ref[...] = (resid + gate * dot_nn(dispatch_ref[...], made_ref[...])).astype(bfloat)


def last_kernel(n, *refs):
    parts_ref, w_ref, x_ref, gain_ref, resid_ref, out_ref = refs
    width = w_ref.shape[1] // n
    grad_normed = jnp.zeros(x_ref.shape, single)
    for r in range(n):
        cols = slice(r * width, (r + 1) * width)
        grad_normed += dot_nt(unpack_rows(parts_ref[r]), w_ref[:, cols])
    row_data = x_ref[...].astype(single)
    back = norm_back(grad_normed, row_data, norm_scale(row_data), gain_ref[...])
    out_ref[...] = (resid_ref[...] + back).astype(bfloat)


def post_kernel(n, back_ref, dispatch_ref, resid_ref, grad_ref, gain_ref, w_ref, *refs):
    attn_refs, (resid_out, branch_ref, gain_out) = refs[:n], refs[n:]
    width = w_ref.shape[0] // n
    grad_normed = dot_nn(dispatch_ref[...], back_ref[...])
    resid = resid_ref[...]
    scale = norm_scale(resid)
    gain_out[...] = jnp.sum(grad_normed * resid * scale, axis=0, keepdims=True)
    grad_resid = grad_ref[...].astype(single) + norm_back(grad_normed, resid, scale, gain_ref[...])
    resid_out[...] = grad_resid
    branch = grad_resid.astype(bfloat)
    branch_ref[...] = branch
    grad_attn = dot_nt(branch, w_ref[...]).astype(bfloat)
    for r in range(n):
        attn_refs[r][...] = pack_rows(grad_attn[:, r * width : (r + 1) * width])


def shift(block, by):
    n = lax.axis_size("ctx")
    return lax.ppermute(block, "ctx", [(i, (i + by) % n) for i in range(n)])


def swap_plane(block, mask):
    count = lax.axis_size(PLANE)
    return lax.ppermute(block, PLANE, [(i, i ^ mask) for i in range(count)])


def to_plane(blocks):
    return lax.all_to_all(blocks, PLANE, split_axis=0, concat_axis=0, tiled=True)


def sum_first(parts):
    return jnp.sum(parts.astype(single), axis=0).astype(bfloat)


def gather_chips(stack):
    count = lax.axis_size(PLANE)
    core = lax.axis_size("expert")
    return {mask: swap_plane(stack, mask) if mask else stack for mask in range(count) if not mask & core}


def gather_cores(held):
    core = lax.axis_size("expert")
    held = {**held, **{mask | core: swap_plane(held[mask], core) for mask in held}}
    return [held[mask] for mask in sorted(held)]


def tied(*arrays):
    return lax.optimization_barrier(arrays)


def late_extras(extra, heads, experts):
    rows = sum(extra[1:], extra[0]).T
    table = jnp.concatenate([e[:NB].T[1 : 1 + heads] for e in extra], axis=0)
    return rows[0], rows[1 + heads], table, rows[2 + heads : 2 + heads + experts]


def place_kernel(count, n, heads, experts, spot_ref, *refs):
    spot, place = spot_ref[0], spot_ref[1]
    ins, outs, small, extra_ref = refs[:count], refs[count : count + 4], refs[count + 4 : -1], refs[-1]
    step = ins[0].shape[1]
    width = heads * HD
    wide = 3 * width + extra_ref.shape[2]
    for mask in range(count):
        there = spot ^ mask
        rows = pl.ds(pl.multiple_of(there * step, step), step)
        for c in range(n):
            block = ins[mask][lax.rem(place - c + n, n)].astype(single)
            for i in range(3):
                outs[i][rows, c * width : (c + 1) * width] = block[:, i * width : (i + 1) * width]
            extra_ref[c, rows, :] = block[:, 3 * width : wide]
            part = step // n
            at = pl.ds(pl.multiple_of(c * width + there * part, part), part)
            for i in range(n):
                outs[3][at, i * width : (i + 1) * width] = block[
                    i * part : (i + 1) * part, wide : wide + width
                ]
    made = late_extras([extra_ref[c] for c in range(n)], heads, experts)
    for ref, value in zip(small, made):
        ref[...] = value


def placed(kernel, spots, held, shapes, scratch=()):
    vmem = pl.BlockSpec(memory_space=pltpu.VMEM)
    return pl.pallas_call(
        kernel,
        out_shape=[jax.ShapeDtypeStruct(s, single) for s in shapes],
        in_specs=[pl.BlockSpec(memory_space=pltpu.SMEM)] + [vmem] * len(held),
        out_specs=[vmem] * len(shapes),
        scratch_shapes=scratch,
        compiler_params=pltpu.CompilerParams(vmem_limit_bytes=VMEM_LIMIT),
        cost_estimate=pl.CostEstimate(
            flops=int(5 * PER_MICRO), bytes_accessed=0, transcendentals=0
        ),
        name="placed",
    )(spots, *held)


def spots():
    return jnp.stack([lax.axis_index(PLANE), lax.axis_index("ctx")]).astype(jnp.int32)


def place_all(held, heads, model_width, experts, late_width):
    n, step, _ = held[0].shape
    width = heads * HD
    shapes = [(model_width, n * width)] * 3 + [(n * width, model_width)]
    if step % (8 * n):
        place, spot = lax.axis_index("ctx"), lax.axis_index(PLANE)
        whole = jnp.zeros((n, len(held), *held[0].shape[1:]), single)
        for mask, stack in enumerate(held):
            for r in range(n):
                where = ((place - r) % n, spot ^ mask, 0, 0)
                whole = lax.dynamic_update_slice(whole, stack[r][None, None].astype(single), where)
        late = whole.reshape(n, model_width, -1)
        own = [late[:, :, i * width : (i + 1) * width] for i in range(3)]
        own = [o.transpose(1, 0, 2).reshape(model_width, n * width) for o in own]
        last = whole[..., late_width : late_width + width]
        last = last.reshape(n, len(held), n, step // n, width).transpose(0, 1, 3, 2, 4)
        extra = [w[:, 3 * width : late_width] for w in late]
        return own + [last.reshape(n * width, model_width)] + list(late_extras(extra, heads, experts))
    shapes += [(model_width,), (model_width,), (n * heads, NB), (experts, model_width)]
    kernel = functools.partial(place_kernel, len(held), n, heads, experts)
    scratch = [pltpu.VMEM((n, model_width, late_width - 3 * width), single)]
    return placed(kernel, spots(), held, shapes, scratch)


def shards(
    tokens,
    cotangent,
    routes,
    buckets,
    gain_attn,
    w_query,
    w_key,
    w_value,
    w_output,
    bias_table,
    gain_ffn,
    w_router,
    w_in,
    w_out,
):
    seq_dev, block_len, model_width = tokens.shape
    n = lax.axis_size("ctx")
    experts = lax.axis_size(PLANE)
    heads = H // n
    width = heads * HD
    full_len = block_len * n
    tok_count = seq_dev * block_len
    capacity = max(2, (5 * tok_count + 4 * experts - 1) // (4 * experts))
    slots = experts * capacity
    place = lax.axis_index("ctx")
    spot = lax.axis_index(PLANE)
    place_in = place.astype(jnp.int32).reshape(1)

    block = tokens.reshape(tok_count, model_width)
    blocks = [block] + [shift(block, r) for r in range(1, n)]

    own_heads = [
        lax.dynamic_slice_in_dim(w, place * width, width, 1) for w in (w_query, w_key, w_value)
    ]
    w_local = jnp.concatenate(own_heads, axis=1)
    turned = [
        lax.dynamic_slice_in_dim(w_output, (place - r) % n * width, width, 0) for r in range(n)
    ]
    w_turned = jnp.concatenate(turned, axis=0)
    w_all = jnp.concatenate(
        [
            w[:, r * width : (r + 1) * width]
            for r in range(n)
            for w in (w_query, w_key, w_value)
        ],
        axis=1,
    )
    bucket_hot = (buckets[:, None] == jnp.arange(NB, dtype=jnp.int32)[None, :]).astype(single)
    table_local = lax.dynamic_slice_in_dim(bias_table, place * heads, heads, 1)
    rel = lax.dot_general(
        table_local, bucket_hot, (((0,), (1,)), ((), ())), precision=exact_prec
    )
    rel = jnp.pad(rel, ((0, 0), (0, 1)))
    route_flat = routes.reshape(tok_count)
    route_hot = (
        route_flat[:, None] == jnp.arange(experts, dtype=jnp.int32)[None, :]
    ).astype(bfloat)
    earlier = jnp.tril(jnp.ones((tok_count, tok_count), bfloat), -1)
    counts = dot_nn(earlier, route_hot)
    slot_index = jnp.sum(counts * route_hot.astype(single), axis=1).astype(jnp.int32)
    target = jnp.where(slot_index < capacity, route_flat * capacity + slot_index, -1)
    dispatch_mat = (target[:, None] == jnp.arange(slots, dtype=jnp.int32)[None, :]).astype(bfloat)
    dispatch_turned = dispatch_mat.T
    gain_one, gain_two = gain_attn.reshape(1, -1), gain_ffn.reshape(1, -1)
    spot_in = spot.astype(jnp.int32).reshape(1)
    buckets_row = jnp.pad(buckets, (0, 1)).reshape(1, -1)

    grad_block = cotangent.reshape(tok_count, model_width)
    grad_sent = dot_nn(dispatch_turned, grad_block).astype(bfloat)
    grad_near = to_plane(grad_sent.reshape(experts, capacity, model_width))
    grad_near = grad_near.reshape(slots, model_width)

    pair = [(i, i ^ 1) for i in range(n)]
    half = model_width // 2

    def swap(piece):
        return lax.ppermute(piece, "ctx", pair)

    first_own, second_own = w_in[0], w_out[0]
    low, high = (cut * model_width // 8 for cut in CUTS)
    pieces = [w[a:b] for w in (first_own, second_own) for a, b in ((0, low), (low, high), (high, None))]
    pieces[0] = swap(pieces[0])
    blocks, pieces, gain_one, gain_two, grad_near, w_local, w_turned, rel, dispatches = tied(
        blocks, pieces, gain_one, gain_two, grad_near, w_local, w_turned, rel,
        (dispatch_mat, dispatch_turned),
    )
    dispatch_mat, dispatch_turned = dispatches
    pieces[1] = swap(pieces[1])

    normed_all, qkv, lse, *attn_parts = attend(place_in, blocks, gain_one, w_local, rel, heads)
    attn_parts, pieces = tied(attn_parts, pieces)
    attn_turned = [attn_parts[0]] + [shift(attn_parts[r], r) for r in range(1, n)]
    pieces[2], pieces[3] = swap(pieces[2]), swap(pieces[3])
    attn_turned, grad_near, pieces, w_all = tied(attn_turned, grad_near, pieces, w_all)
    grad_far = shift(grad_near, n // 2)
    pieces[4] = swap(pieces[4])
    rows_shape = (tok_count, model_width)
    sent, resid, attn_rows = call(
        functools.partial(middle_kernel, n),
        "middle",
        [((slots, model_width), bfloat), (rows_shape, single), (rows_shape, bfloat)],
        3,
        *attn_turned, block, w_turned, gain_two, dispatch_turned,
    )
    near = to_plane(sent.reshape(experts, capacity, model_width)).reshape(slots, model_width)
    near, grad_far, pieces = tied(near, grad_far, pieces)
    far = shift(near, n // 2)
    pieces[5] = swap(pieces[5])

    near_back, near_scaled, near_logits, *near_parts = expert(
        spot_in, near, grad_near, first_own, second_own, pieces, w_router, single
    )
    far, near_back = tied(far, near_back)
    far_back, far_scaled, far_logits, *far_parts = expert(
        spot_in, far, grad_far, first_own, second_own, pieces, w_router, bfloat
    )
    back_got = shift(far_back, n // 2)

    cut = 19 * model_width // 48
    cuts = [((cut, model_width), bfloat), ((model_width - cut, model_width), bfloat)]
    near_made, far_made = call(
        made_kernel,
        "made",
        [((slots, model_width), single), ((slots, model_width), bfloat)],
        0,
        *near_parts[:2], *far_parts[:2], second_own, *pieces[3:],
        scratch=[pltpu.VMEM(second_own.shape, bfloat)],
    )
    sends = list(call(sums_kernel, "sums", cuts, 0, near, far, near_parts[3], far_parts[3]))
    sends[0] = swap(sends[0])
    back_got, sends, near_made, far_made, near_parts, far_parts = tied(
        back_got, sends, near_made, far_made, near_parts, far_parts
    )
    sends[1] = swap(sends[1])
    back_sum = (near_back + back_got.astype(single)).astype(bfloat)
    back_home = to_plane(back_sum.reshape(experts, capacity, model_width))
    third = model_width // 3
    thirds = [((third, model_width), bfloat)] * 2 + [((model_width - 2 * third, model_width), bfloat)]
    sends += call(
        sums_kernel, "sums", thirds, 3, near_parts[1], far_parts[1], near_scaled, far_scaled
    )
    grad_router = dot_tn(near_logits, near) + dot_tn(far_logits, far)

    *attn_grads, grad_resid, grad_branch, grad_gain_ffn = call(
        functools.partial(post_kernel, n),
        "post",
        [((tok_count // 2, 2 * width), bfloat)] * n
        + [(rows_shape, single), (rows_shape, bfloat), ((1, model_width), single)],
        4,
        back_home.reshape(slots, model_width), dispatch_mat, resid, grad_block, gain_two, w_turned,
    )
    attn_grads, grad_branch, sends[0], *sends[2:] = tied(attn_grads, grad_branch, sends[0], *sends[2:])
    attn_grads = [attn_grads[0]] + [shift(attn_grads[r], n - r) for r in range(1, n)]

    count = lax.axis_size(PLANE)
    grad_output = dot_tn(attn_rows, grad_branch).astype(bfloat)
    grad_output = grad_output.reshape(n, count, width // count, model_width)
    grad_output = lax.all_to_all(grad_output, PLANE, split_axis=1, concat_axis=1, tiled=True)
    *attn_grads, far_made, sends[1], sends[2], grad_router = tied(
        *attn_grads, far_made, sends[1], sends[2], grad_router
    )
    made_got = shift(far_made, n // 2)
    sends[2] = lax.ppermute(sends[2], "ctx", pair)

    parts, late = attend_back(
        place_in, attn_grads, qkv, lse, rel, w_local, normed_all, gain_one, buckets_row,
        grad_gain_ffn, grad_router, heads
    )
    late, made_got, sends, grad_output = tied(late, made_got, sends, grad_output)
    late_width = late.shape[1]
    late = to_plane(late.reshape(count, model_width // count, late_width))
    grad_output = sum_first(grad_output.transpose(1, 0, 2, 3))
    shares = [grad_output[0]] + [shift(grad_output[r], n - r) for r in range(1, n)]
    made_sum = (near_made + made_got.astype(single)).astype(bfloat)
    sends[3] = swap(sends[3])
    late, made_sum, far_parts, shares, sends = tied(late, made_sum, far_parts, shares, sends)
    step = model_width // count
    (piece,) = call(
        join_kernel, "join", [((step, late_width + -(-width // 128) * 128), bfloat)], 1, late, *shares
    )
    pieces = [piece] + [shift(piece, r) for r in range(1, n)]
    made_home = to_plane(made_sum.reshape(experts, capacity, model_width))
    (grad_first,) = call(
        own_kernel, "own", [((model_width, model_width), single)], 4,
        near, far, near_parts[2], far_parts[2], *sends[:2],
    )
    pieces, parts, made_home, grad_first, sends = tied(pieces, parts, made_home, grad_first, sends)
    (stack,) = call(stack_kernel, "stack", [((n, *piece.shape), bfloat)], 1, *pieces)
    held = gather_chips(stack)
    sends[4] = swap(sends[4])
    (layer_out,) = call(
        layer_kernel, "layer", [(rows_shape, bfloat)], 3,
        made_home.reshape(slots, model_width), dispatch_mat, resid, gain_two, w_router, route_hot,
    )
    layer_out, parts = tied(layer_out, parts)
    parts = lax.all_to_all(parts, "ctx", split_axis=0, concat_axis=0, tiled=True)
    (grad_tokens,) = call(
        functools.partial(last_kernel, n), "last", [(rows_shape, bfloat)], 4,
        parts, w_all, block, gain_one, grad_resid,
    )
    (grad_second,) = call(
        own_kernel, "own", [((model_width, model_width), single)], 4,
        near_parts[0], far_parts[0], near_scaled, far_scaled, *sends[2:],
    )
    held, layer_out, grad_second = tied(held, layer_out, grad_second)
    (grad_query, grad_key, grad_value, output_all, grad_gain_attn, grad_gain_ffn, grad_table,
     grad_router) = place_all(gather_cores(held), heads, model_width, experts, late_width)
    return (
        layer_out.reshape(seq_dev, block_len, model_width).astype(bfloat),
        grad_tokens.reshape(seq_dev, block_len, model_width).astype(bfloat),
        grad_gain_attn,
        grad_query,
        grad_key,
        grad_value,
        output_all,
        grad_table.T,
        grad_gain_ffn,
        grad_router.T,
        grad_first[None],
        grad_second[None],
    )


def solution(mesh):
    spread = P(("dp", "expert"), "ctx", None)
    first = P(("dp", "expert"), None, "ctx")
    return jax.shard_map(
        shards,
        mesh=mesh,
        in_specs=(spread,) * 3 + (P(),) * 9 + (first, spread),
        out_specs=(spread,) * 2 + (P(),) * 8 + (first, spread),
        check_vma=False,
    )
```

```python
import functools
import math

import jax
import jax.numpy as jnp
from jax import lax
from jax.experimental import pallas as pl
from jax.experimental.pallas import tpu as pltpu
from jax.sharding import PartitionSpec as P

H = 12
HD = 64
NB = 32
PLANE = ("dp", "expert")

epsilon = 1e-06
exact_prec = lax.Precision.HIGHEST
bfloat = jnp.bfloat16
single = jnp.float32
VMEM_LIMIT = 56 * 1024 * 1024
ROOM = 8 * 1024 * 1024
TIGHT = ("own", "layer")
PER_MICRO = 1.15e9
CUTS = ((2, 12), (2, 12))


def norm_scale(row_data):
    return lax.rsqrt(jnp.mean(row_data * row_data, axis=-1, keepdims=True) + epsilon)


def norm_back(grad_in, row_data, scale, gain):
    weighted = grad_in * gain
    inner = jnp.mean(weighted * row_data, axis=-1, keepdims=True)
    return scale * weighted - row_data * (scale * scale * scale) * inner


def dot_nn(left, right):
    return lax.dot_general(
        left, right, (((1,), (0,)), ((), ())), preferred_element_type=single
    )


def dot_nt(left, right):
    return lax.dot_general(
        left, right, (((1,), (1,)), ((), ())), preferred_element_type=single
    )


def dot_tn(left, right):
    return lax.dot_general(
        left, right, (((0,), (0,)), ((), ())), preferred_element_type=single
    )


def pack_rows(rows):
    half = rows.shape[0] // 2
    return jnp.concatenate([rows[:half], rows[half:]], axis=1)


def unpack_rows(packed):
    width = packed.shape[1] // 2
    return jnp.concatenate([packed[:, :width], packed[:, width:]], axis=0)


def bias_strip(rel_row, rows, width):
    spread = jnp.broadcast_to(rel_row, (rows, width))
    return pltpu.roll(spread, width - (rows - 1), 1, stride=1, stride_axis=0)


def fold_strip(strip):
    rows = strip.shape[0]
    while rows > 1:
        rows //= 2
        strip = strip[rows:] + pltpu.roll(strip[:rows], rows, 1)
    return strip


def attend_kernel(n, heads, place_ref, *refs):
    blocks = refs[:n]
    gain_ref, w_ref, rel_ref, normed_ref, qkv_ref, lse_ref, *out_refs, strip_ref, out_ref = refs[n:]
    place = place_ref[0]
    block_len = blocks[0].shape[0]
    full_len = n * block_len
    width = heads * HD
    for r in range(n):
        start = pl.multiple_of(lax.rem(place - r + n, n) * block_len, block_len)
        row_data = blocks[r][...].astype(single)
        normed = (row_data * norm_scale(row_data) * gain_ref[...]).astype(bfloat)
        normed_ref[pl.ds(start, block_len), :] = normed
        qkv_ref[pl.ds(start, block_len), :] = dot_nn(normed, w_ref[...]).astype(bfloat)
    for h in range(heads):
        strip_ref[h] = bias_strip(rel_ref[h : h + 1, :], block_len, 2 * full_len)
    lse_ref[...] = jnp.zeros_like(lse_ref)

    def tile(t, carry):
        rows = pl.ds(pl.multiple_of(t * block_len, block_len), block_len)
        skew = pl.ds(pl.multiple_of((n - 1 - t) * block_len, block_len), full_len)
        made = []
        for h in range(heads):
            query = qkv_ref[rows, h * HD : (h + 1) * HD]
            key = qkv_ref[:, width + h * HD : width + (h + 1) * HD]
            value = qkv_ref[:, 2 * width + h * HD : 2 * width + (h + 1) * HD]
            scores = dot_nt(query, key) + strip_ref[h, :, skew]
            top = jnp.max(scores, axis=1, keepdims=True)
            expd = jnp.exp(scores - top)
            total = jnp.sum(expd, axis=1, keepdims=True)
            made.append(dot_nn(expd.astype(bfloat), value) / total)
            lse_ref[rows, h : h + 1] = top + jnp.log(total)
        joined = jnp.concatenate(made, axis=1).astype(bfloat)
        out_ref[lax.rem(t - place + n, n)] = pack_rows(joined)
        return carry

    lax.fori_loop(0, n, tile, 0, unroll=1)
    for r in range(n):
        out_refs[r][...] = out_ref[r]


def attend(place, blocks, gain, w_local, rel, heads):
    n = len(blocks)
    block_len, model_width = blocks[0].shape
    full_len = n * block_len
    width = heads * HD
    vmem = pl.BlockSpec(memory_space=pltpu.VMEM)
    return pl.pallas_call(
        functools.partial(attend_kernel, n, heads),
        out_shape=(
            jax.ShapeDtypeStruct((full_len, model_width), bfloat),
            jax.ShapeDtypeStruct((full_len, 3 * width), bfloat),
            jax.ShapeDtypeStruct((full_len, 128), single),
            *[jax.ShapeDtypeStruct((block_len // 2, 2 * width), bfloat)] * n,
        ),
        in_specs=[pl.BlockSpec(memory_space=pltpu.SMEM)] + [vmem] * (n + 3),
        out_specs=(vmem,) * (n + 3),
        scratch_shapes=[
            pltpu.VMEM((heads, block_len, 2 * full_len), single),
            pltpu.VMEM((n, block_len // 2, 2 * width), bfloat),
        ],
        compiler_params=pltpu.CompilerParams(vmem_limit_bytes=VMEM_LIMIT),
        cost_estimate=pl.CostEstimate(
            flops=int(11 * PER_MICRO),
            bytes_accessed=0,
            transcendentals=0,
        ),
        name="attend",
    )(place, *blocks, gain, w_local, rel)


def attend_back_kernel(n, heads, place_ref, *refs):
    blocks = refs[:n]
    (qkv_ref, lse_ref, rel_ref, w_ref, normed_ref, gain_ref, buckets_ref, grad_gain_ref, router_ref,
     part_ref, late_ref,
     da_ref, strip_ref, sums_ref, key_acc, value_acc, dqkv_ref, rel_out_ref) = refs[n:]
    place = place_ref[0]
    block_len = blocks[0].shape[0] * 2
    full_len = n * block_len
    width = heads * HD
    model_width = normed_ref.shape[1]
    for r in range(n):
        start = pl.multiple_of(lax.rem(place + r, n) * block_len, block_len)
        da_ref[pl.ds(start, block_len), :] = unpack_rows(blocks[r][...])
    for h in range(heads):
        strip_ref[h] = bias_strip(rel_ref[h : h + 1, :], block_len, 2 * full_len)
    sums_ref[...] = jnp.zeros_like(sums_ref)
    key_acc[...] = jnp.zeros_like(key_acc)
    value_acc[...] = jnp.zeros_like(value_acc)

    def tile(t, carry):
        rows = pl.ds(pl.multiple_of(t * block_len, block_len), block_len)
        skew = pl.ds(pl.multiple_of((n - 1 - t) * block_len, block_len), full_len)
        for h in range(heads):
            query = qkv_ref[rows, h * HD : (h + 1) * HD]
            key = qkv_ref[:, width + h * HD : width + (h + 1) * HD]
            value = qkv_ref[:, 2 * width + h * HD : 2 * width + (h + 1) * HD]
            grad_attn = da_ref[rows, h * HD : (h + 1) * HD]
            scores = dot_nt(query, key) + strip_ref[h, :, skew]
            soft = jnp.exp(scores - lse_ref[rows, h : h + 1])
            value_acc[h] += dot_tn(grad_attn, soft.astype(bfloat))
            grad_soft = dot_nt(grad_attn, value)
            delta = jnp.sum(soft * grad_soft, axis=1, keepdims=True)
            grad_wide = soft * (grad_soft - delta)
            sums_ref[h, :, skew] += grad_wide
            grad_scores = grad_wide.astype(bfloat)
            dqkv_ref[rows, h * HD : (h + 1) * HD] = dot_nn(grad_scores, key).astype(bfloat)
            key_acc[h] += dot_tn(query, grad_scores)
        return carry

    lax.fori_loop(0, n, tile, 0, unroll=4)
    for h in range(heads):
        dqkv_ref[:, width + h * HD : width + (h + 1) * HD] = key_acc[h].T.astype(bfloat)
        dqkv_ref[:, 2 * width + h * HD : 2 * width + (h + 1) * HD] = value_acc[h].T.astype(bfloat)
        rel_out_ref[h : h + 1, :] = fold_strip(sums_ref[h])
    for r in range(n):
        part_ref[r] = pack_rows(dqkv_ref[r * block_len : (r + 1) * block_len, :])
    made = dot_tn(normed_ref[...], dqkv_ref[...])
    late_ref[:, : 3 * width] = made.astype(bfloat)
    total = jnp.sum(made * w_ref[...].astype(single), axis=1, keepdims=True)
    kinds = lax.broadcasted_iota(jnp.int32, (NB, 2 * full_len), 0)
    hot = (kinds == buckets_ref[...]).astype(single)
    table = lax.dot_general(
        rel_out_ref[...], hot, (((1,), (1,)), ((), ())),
        precision=exact_prec, preferred_element_type=single,
    )
    table = jnp.concatenate([table, jnp.zeros((heads, model_width - NB), single)], axis=1)
    extra = [1.0 / gain_ref[...], table, grad_gain_ref[...], router_ref[...]]
    short = late_ref.shape[1] - 3 * width - sum(e.shape[0] for e in extra)
    extra = jnp.concatenate(extra + [jnp.zeros((short, model_width), single)], axis=0).T
    late_ref[:, 3 * width :] = extra.astype(bfloat)
    late_ref[:, 3 * width : 3 * width + 1] = (extra[:, :1] * total).astype(bfloat)


def attend_back(place, blocks, qkv, lse, rel, w_local, normed, gain, buckets, grad_gain, router, heads):
    n = len(blocks)
    full_len, model_width = normed.shape
    block_len = full_len // n
    width = heads * HD
    late_width = -(-(3 * width + 2 + heads + router.shape[0]) // 128) * 128
    vmem = pl.BlockSpec(memory_space=pltpu.VMEM)
    return pl.pallas_call(
        functools.partial(attend_back_kernel, n, heads),
        out_shape=(
            jax.ShapeDtypeStruct((n, block_len // 2, 6 * width), bfloat),
            jax.ShapeDtypeStruct((model_width, late_width), bfloat),
        ),
        in_specs=[pl.BlockSpec(memory_space=pltpu.SMEM)] + [vmem] * (n + 9),
        out_specs=(vmem,) * 2,
        scratch_shapes=[
            pltpu.VMEM((full_len, width), bfloat),
            pltpu.VMEM((heads, block_len, 2 * full_len), single),
            pltpu.VMEM((heads, block_len, 2 * full_len), single),
            pltpu.VMEM((heads, HD, full_len), single),
            pltpu.VMEM((heads, HD, full_len), single),
            pltpu.VMEM((full_len, 3 * width), bfloat),
            pltpu.VMEM((heads, 2 * full_len), single),
        ],
        compiler_params=pltpu.CompilerParams(vmem_limit_bytes=VMEM_LIMIT),
        cost_estimate=pl.CostEstimate(
            flops=int(19 * PER_MICRO),
            bytes_accessed=0,
            transcendentals=0,
        ),
        name="attend_back",
    )(place, *blocks, qkv, lse, rel, w_local, normed, gain, buckets, grad_gain, router)


def call(kernel, name, shapes, micros, *args, in_smem=(), scratch=()):
    vmem = pl.BlockSpec(memory_space=pltpu.VMEM)
    smem = pl.BlockSpec(memory_space=pltpu.SMEM)
    held = [(a.shape, a.dtype) for a in args] + list(shapes) + [(v.shape, v.dtype) for v in scratch]
    held = sum(math.prod(s) * jnp.dtype(t).itemsize for s, t in held)
    return pl.pallas_call(
        kernel,
        out_shape=[jax.ShapeDtypeStruct(s, t) for s, t in shapes],
        in_specs=[smem if i in in_smem else vmem for i in range(len(args))],
        out_specs=[vmem] * len(shapes),
        scratch_shapes=scratch,
        compiler_params=pltpu.CompilerParams(vmem_limit_bytes=held + ROOM if name in TIGHT else VMEM_LIMIT),
        cost_estimate=pl.CostEstimate(
            flops=int(micros * PER_MICRO), bytes_accessed=0, transcendentals=0
        ),
        name=name,
    )(*args)


def middle_kernel(n, *refs):
    parts = refs[:n]
    x_ref, w_ref, gain_ref, dispatch_ref, sent_ref, resid_ref, attn_ref = refs[n:]
    width = w_ref.shape[0] // n
    for r in range(n):
        attn_ref[:, r * width : (r + 1) * width] = unpack_rows(parts[r][...])
    resid = x_ref[...].astype(single) + dot_nn(attn_ref[...], w_ref[...])
    resid_ref[...] = resid
    normed = (resid * norm_scale(resid) * gain_ref[...]).astype(bfloat)
    sent_ref[...] = dot_nn(dispatch_ref[...], normed).astype(bfloat)


def expert_kernel(spot_ref, rows_ref, grad_ref, first_ref, second_ref, *refs):
    pieces, (router_ref, back_ref, scaled_ref, logits_ref) = refs[:6], refs[6:10]
    hidden_refs, pre_refs, others, sum_ref = refs[10:12], refs[12:14], refs[14:16], refs[16]
    for i, ref in enumerate(pieces):
        start = sum(p.shape[0] for p in pieces[i - i % 3 : i])
        others[i // 3][start : start + ref.shape[0], :] = ref[...]
    rows, grad_rows = rows_ref[...], grad_ref[...]
    count = rows.shape[0]
    half = first_ref.shape[1] // 2
    logits = dot_nn(rows, router_ref[...])
    expd = jnp.exp(logits - jnp.max(logits, axis=1, keepdims=True))
    probs = expd / jnp.sum(expd, axis=1, keepdims=True)
    hot = (lax.broadcasted_iota(jnp.int32, (1, logits.shape[1]), 1) == spot_ref[0]).astype(single)
    gate = jnp.sum(probs * hot, axis=1, keepdims=True)
    scaled_ref[...] = (gate * grad_rows.astype(single)).astype(bfloat)

    def step(piece, grad_gate):
        cols = pl.ds(pl.multiple_of(piece * half, half), half)
        back = jnp.zeros((count, 2 * half), single)
        for other, (first, second) in enumerate(((first_ref, second_ref), others)):
            pre = dot_nn(rows, first[:, cols])
            pull = dot_nt(grad_rows, second[cols, :])
            normal = 0.5 * (1.0 + lax.erf(pre * (0.5**0.5)))
            density = jnp.exp(-0.5 * pre * pre) * 0.3989422804014327
            hidden = pre * normal
            grad_gate += jnp.sum(hidden * pull, axis=1, keepdims=True)
            grad_pre = (gate * pull * (normal + pre * density)).astype(bfloat)
            hidden_refs[other][:, cols] = hidden.astype(bfloat)
            pre_refs[other][:, cols] = grad_pre
            back += dot_nt(grad_pre, first[:, cols])
        sum_ref[...] += back
        return grad_gate

    sum_ref[...] = jnp.zeros_like(sum_ref)
    grad_gate = lax.fori_loop(0, 2, step, jnp.zeros((count, 1), single))
    grad_logits = (grad_gate * probs * (hot - gate)).astype(bfloat)
    logits_ref[...] = grad_logits
    made = sum_ref[...] + dot_nt(grad_logits, router_ref[...])
    back_ref[...] = made.astype(back_ref.dtype)


def expert(spot, rows, grad_rows, first, second, pieces, w_router, kind):
    wide = rows.shape
    units = (rows.shape[0], first.shape[1])
    shapes = [(wide, kind), (wide, bfloat), ((wide[0], w_router.shape[1]), bfloat)]
    return call(
        expert_kernel, "expert", shapes + [(units, bfloat)] * 4, 7,
        spot, rows, grad_rows, first, second, *pieces, w_router, in_smem=(0,),
        scratch=[
            pltpu.VMEM(first.shape, bfloat),
            pltpu.VMEM(second.shape, bfloat),
            pltpu.VMEM(wide, single),
        ],
    )


def made_kernel(near_own, near_other, far_own, far_other, second_ref, *refs):
    pieces, (near_ref, far_ref, held_ref) = refs[:3], refs[3:]
    start = 0
    for ref in pieces:
        held_ref[start : start + ref.shape[0], :] = ref[...]
        start += ref.shape[0]
    for own, other, out in ((near_own, near_other, near_ref), (far_own, far_other, far_ref)):
        made = dot_nn(own[...], second_ref[...]) + dot_nn(other[...], held_ref[...])
        out[...] = made.astype(out.dtype)


def pieces_of(refs):
    start = 0
    for ref in refs:
        yield slice(start, start + ref.shape[0]), ref
        start += ref.shape[0]


def sums_kernel(near_left, far_left, near_right, far_right, *outs):
    for ends, out in pieces_of(outs):
        made = dot_tn(near_left[:, ends], near_right[...]) + dot_tn(far_left[:, ends], far_right[...])
        out[...] = made.astype(bfloat)


def own_kernel(near_left, far_left, near_right, far_right, *refs):
    *pieces, out_ref = refs
    for ends, got in pieces_of(pieces):
        made = dot_tn(near_left[:, ends], near_right[...]) + dot_tn(far_left[:, ends], far_right[...])
        out_ref[ends, :] = made + got[...].astype(single)


def join_kernel(late_ref, *refs):
    *blocks, out_ref = refs
    count, step, wide = late_ref.shape
    late = late_ref[0].astype(single)
    for i in range(1, count):
        late += late_ref[i].astype(single)
    out_ref[:, :wide] = late.astype(bfloat)
    total = sum(b[...].astype(single) for b in blocks[1:]) + blocks[0][...].astype(single)
    rows = total.shape[0]
    cuts = step // rows
    width = total.shape[1] // cuts
    folded = jnp.concatenate([total[:, i * width : (i + 1) * width] for i in range(cuts)], axis=0)
    spare = jnp.zeros((step, out_ref.shape[1] - wide - width), single)
    out_ref[:, wide:] = jnp.concatenate([folded, spare], axis=1).astype(bfloat)


def stack_kernel(*refs):
    *ins, out_ref = refs
    for i, ref in enumerate(ins):
        out_ref[i] = ref[...]


def layer_kernel(made_ref, dispatch_ref, resid_ref, gain_ref, router_ref, hot_ref, out_ref):
    resid = resid_ref[...]
    normed = (resid * norm_scale(resid) * gain_ref[...]).astype(bfloat)
    logits = dot_nn(normed, router_ref[...])
    expd = jnp.exp(logits - jnp.max(logits, axis=1, keepdims=True))
    probs = expd / jnp.sum(expd, axis=1, keepdims=True)
    gate = jnp.sum(probs * hot_ref[...].astype(single), axis=1, keepdims=True)
    out_ref[...] = (resid + gate * dot_nn(dispatch_ref[...], made_ref[...])).astype(bfloat)


def last_kernel(n, *refs):
    parts_ref, w_ref, x_ref, gain_ref, resid_ref, out_ref = refs
    width = w_ref.shape[1] // n
    grad_normed = jnp.zeros(x_ref.shape, single)
    for r in range(n):
        cols = slice(r * width, (r + 1) * width)
        grad_normed += dot_nt(unpack_rows(parts_ref[r]), w_ref[:, cols])
    row_data = x_ref[...].astype(single)
    back = norm_back(grad_normed, row_data, norm_scale(row_data), gain_ref[...])
    out_ref[...] = (resid_ref[...] + back).astype(bfloat)


def post_kernel(n, back_ref, dispatch_ref, resid_ref, grad_ref, gain_ref, w_ref, *refs):
    attn_refs, (resid_out, branch_ref, gain_out) = refs[:n], refs[n:]
    width = w_ref.shape[0] // n
    grad_normed = dot_nn(dispatch_ref[...], back_ref[...])
    resid = resid_ref[...]
    scale = norm_scale(resid)
    gain_out[...] = jnp.sum(grad_normed * resid * scale, axis=0, keepdims=True)
    grad_resid = grad_ref[...].astype(single) + norm_back(grad_normed, resid, scale, gain_ref[...])
    resid_out[...] = grad_resid
    branch = grad_resid.astype(bfloat)
    branch_ref[...] = branch
    grad_attn = dot_nt(branch, w_ref[...]).astype(bfloat)
    for r in range(n):
        attn_refs[r][...] = pack_rows(grad_attn[:, r * width : (r + 1) * width])


def shift(block, by):
    n = lax.axis_size("ctx")
    return lax.ppermute(block, "ctx", [(i, (i + by) % n) for i in range(n)])


def swap_plane(block, mask):
    count = lax.axis_size(PLANE)
    return lax.ppermute(block, PLANE, [(i, i ^ mask) for i in range(count)])


def to_plane(blocks):
    return lax.all_to_all(blocks, PLANE, split_axis=0, concat_axis=0, tiled=True)


def sum_first(parts):
    return jnp.sum(parts.astype(single), axis=0).astype(bfloat)


def gather_chips(stack):
    count = lax.axis_size(PLANE)
    core = lax.axis_size("expert")
    return {mask: swap_plane(stack, mask) if mask else stack for mask in range(count) if not mask & core}


def gather_cores(held):
    core = lax.axis_size("expert")
    held = {**held, **{mask | core: swap_plane(held[mask], core) for mask in held}}
    return [held[mask] for mask in sorted(held)]


def tied(*arrays):
    return lax.optimization_barrier(arrays)


def late_extras(extra, heads, experts):
    rows = sum(extra[1:], extra[0]).T
    table = jnp.concatenate([e[:NB].T[1 : 1 + heads] for e in extra], axis=0)
    return rows[0], rows[1 + heads], table, rows[2 + heads : 2 + heads + experts]


def place_kernel(count, n, heads, experts, spot_ref, *refs):
    spot, place = spot_ref[0], spot_ref[1]
    ins, outs, small, extra_ref = refs[:count], refs[count : count + 4], refs[count + 4 : -1], refs[-1]
    step = ins[0].shape[1]
    width = heads * HD
    wide = 3 * width + extra_ref.shape[2]
    for mask in range(count):
        there = spot ^ mask
        rows = pl.ds(pl.multiple_of(there * step, step), step)
        for c in range(n):
            block = ins[mask][lax.rem(place - c + n, n)].astype(single)
            for i in range(3):
                outs[i][rows, c * width : (c + 1) * width] = block[:, i * width : (i + 1) * width]
            extra_ref[c, rows, :] = block[:, 3 * width : wide]
            part = step // n
            at = pl.ds(pl.multiple_of(c * width + there * part, part), part)
            for i in range(n):
                outs[3][at, i * width : (i + 1) * width] = block[
                    i * part : (i + 1) * part, wide : wide + width
                ]
    made = late_extras([extra_ref[c] for c in range(n)], heads, experts)
    for ref, value in zip(small, made):
        ref[...] = value


def placed(kernel, spots, held, shapes, scratch=()):
    vmem = pl.BlockSpec(memory_space=pltpu.VMEM)
    return pl.pallas_call(
        kernel,
        out_shape=[jax.ShapeDtypeStruct(s, single) for s in shapes],
        in_specs=[pl.BlockSpec(memory_space=pltpu.SMEM)] + [vmem] * len(held),
        out_specs=[vmem] * len(shapes),
        scratch_shapes=scratch,
        compiler_params=pltpu.CompilerParams(vmem_limit_bytes=VMEM_LIMIT),
        cost_estimate=pl.CostEstimate(
            flops=int(5 * PER_MICRO), bytes_accessed=0, transcendentals=0
        ),
        name="placed",
    )(spots, *held)


def spots():
    return jnp.stack([lax.axis_index(PLANE), lax.axis_index("ctx")]).astype(jnp.int32)


def place_all(held, heads, model_width, experts, late_width):
    n, step, _ = held[0].shape
    width = heads * HD
    shapes = [(model_width, n * width)] * 3 + [(n * width, model_width)]
    if step % (8 * n):
        place, spot = lax.axis_index("ctx"), lax.axis_index(PLANE)
        whole = jnp.zeros((n, len(held), *held[0].shape[1:]), single)
        for mask, stack in enumerate(held):
            for r in range(n):
                where = ((place - r) % n, spot ^ mask, 0, 0)
                whole = lax.dynamic_update_slice(whole, stack[r][None, None].astype(single), where)
        late = whole.reshape(n, model_width, -1)
        own = [late[:, :, i * width : (i + 1) * width] for i in range(3)]
        own = [o.transpose(1, 0, 2).reshape(model_width, n * width) for o in own]
        last = whole[..., late_width : late_width + width]
        last = last.reshape(n, len(held), n, step // n, width).transpose(0, 1, 3, 2, 4)
        extra = [w[:, 3 * width : late_width] for w in late]
        return own + [last.reshape(n * width, model_width)] + list(late_extras(extra, heads, experts))
    shapes += [(model_width,), (model_width,), (n * heads, NB), (experts, model_width)]
    kernel = functools.partial(place_kernel, len(held), n, heads, experts)
    scratch = [pltpu.VMEM((n, model_width, late_width - 3 * width), single)]
    return placed(kernel, spots(), held, shapes, scratch)


def shards(
    tokens,
    cotangent,
    routes,
    buckets,
    gain_attn,
    w_query,
    w_key,
    w_value,
    w_output,
    bias_table,
    gain_ffn,
    w_router,
    w_in,
    w_out,
):
    seq_dev, block_len, model_width = tokens.shape
    n = lax.axis_size("ctx")
    experts = lax.axis_size(PLANE)
    heads = H // n
    width = heads * HD
    full_len = block_len * n
    tok_count = seq_dev * block_len
    capacity = max(2, (5 * tok_count + 4 * experts - 1) // (4 * experts))
    slots = experts * capacity
    place = lax.axis_index("ctx")
    spot = lax.axis_index(PLANE)
    place_in = place.astype(jnp.int32).reshape(1)

    block = tokens.reshape(tok_count, model_width)
    blocks = [block] + [shift(block, r) for r in range(1, n)]

    own_heads = [
        lax.dynamic_slice_in_dim(w, place * width, width, 1) for w in (w_query, w_key, w_value)
    ]
    w_local = jnp.concatenate(own_heads, axis=1)
    turned = [
        lax.dynamic_slice_in_dim(w_output, (place - r) % n * width, width, 0) for r in range(n)
    ]
    w_turned = jnp.concatenate(turned, axis=0)
    w_all = jnp.concatenate(
        [
            w[:, r * width : (r + 1) * width]
            for r in range(n)
            for w in (w_query, w_key, w_value)
        ],
        axis=1,
    )
    bucket_hot = (buckets[:, None] == jnp.arange(NB, dtype=jnp.int32)[None, :]).astype(single)
    table_local = lax.dynamic_slice_in_dim(bias_table, place * heads, heads, 1)
    rel = lax.dot_general(
        table_local, bucket_hot, (((0,), (1,)), ((), ())), precision=exact_prec
    )
    rel = jnp.pad(rel, ((0, 0), (0, 1)))
    route_flat = routes.reshape(tok_count)
    route_hot = (
        route_flat[:, None] == jnp.arange(experts, dtype=jnp.int32)[None, :]
    ).astype(bfloat)
    earlier = jnp.tril(jnp.ones((tok_count, tok_count), bfloat), -1)
    counts = dot_nn(earlier, route_hot)
    slot_index = jnp.sum(counts * route_hot.astype(single), axis=1).astype(jnp.int32)
    target = jnp.where(slot_index < capacity, route_flat * capacity + slot_index, -1)
    dispatch_mat = (target[:, None] == jnp.arange(slots, dtype=jnp.int32)[None, :]).astype(bfloat)
    dispatch_turned = dispatch_mat.T
    gain_one, gain_two = gain_attn.reshape(1, -1), gain_ffn.reshape(1, -1)
    spot_in = spot.astype(jnp.int32).reshape(1)
    buckets_row = jnp.pad(buckets, (0, 1)).reshape(1, -1)

    grad_block = cotangent.reshape(tok_count, model_width)
    grad_sent = dot_nn(dispatch_turned, grad_block).astype(bfloat)
    grad_near = to_plane(grad_sent.reshape(experts, capacity, model_width))
    grad_near = grad_near.reshape(slots, model_width)

    pair = [(i, i ^ 1) for i in range(n)]
    half = model_width // 2

    def swap(piece):
        return lax.ppermute(piece, "ctx", pair)

    first_own, second_own = w_in[0], w_out[0]
    pieces = []
    for w, cuts in zip((first_own, second_own), CUTS):
        low, high = (cut * model_width // 16 for cut in cuts)
        pieces += [w[:low], w[low:high], w[high:]]
    pieces[0] = swap(pieces[0])
    blocks, pieces, gain_one, gain_two, grad_near, w_local, w_turned, rel, dispatches = tied(
        blocks, pieces, gain_one, gain_two, grad_near, w_local, w_turned, rel,
        (dispatch_mat, dispatch_turned),
    )
    dispatch_mat, dispatch_turned = dispatches
    pieces[1] = swap(pieces[1])

    normed_all, qkv, lse, *attn_parts = attend(place_in, blocks, gain_one, w_local, rel, heads)
    attn_parts, pieces = tied(attn_parts, pieces)
    attn_turned = [attn_parts[0]] + [shift(attn_parts[r], r) for r in range(1, n)]
    pieces[2], pieces[3] = swap(pieces[2]), swap(pieces[3])
    attn_turned, grad_near, pieces, w_all = tied(attn_turned, grad_near, pieces, w_all)
    grad_far = shift(grad_near, n // 2)
    pieces[4] = swap(pieces[4])
    rows_shape = (tok_count, model_width)
    sent, resid, attn_rows = call(
        functools.partial(middle_kernel, n),
        "middle",
        [((slots, model_width), bfloat), (rows_shape, single), (rows_shape, bfloat)],
        3,
        *attn_turned, block, w_turned, gain_two, dispatch_turned,
    )
    near = to_plane(sent.reshape(experts, capacity, model_width)).reshape(slots, model_width)
    near, grad_far, pieces = tied(near, grad_far, pieces)
    far = shift(near, n // 2)
    pieces[5] = swap(pieces[5])

    near_back, near_scaled, near_logits, *near_parts = expert(
        spot_in, near, grad_near, first_own, second_own, pieces, w_router, single
    )
    far, near_back = tied(far, near_back)
    far_back, far_scaled, far_logits, *far_parts = expert(
        spot_in, far, grad_far, first_own, second_own, pieces, w_router, bfloat
    )
    back_got = shift(far_back, n // 2)

    cut = 16 * model_width // 48
    cuts = [((cut, model_width), bfloat), ((model_width - cut, model_width), bfloat)]
    near_made, far_made = call(
        made_kernel,
        "made",
        [((slots, model_width), single), ((slots, model_width), bfloat)],
        0,
        *near_parts[:2], *far_parts[:2], second_own, *pieces[3:],
        scratch=[pltpu.VMEM(second_own.shape, bfloat)],
    )
    sends = list(call(sums_kernel, "sums", cuts, 0, near, far, near_parts[3], far_parts[3]))
    sends[0] = swap(sends[0])
    back_got, sends, near_made, far_made, near_parts, far_parts = tied(
        back_got, sends, near_made, far_made, near_parts, far_parts
    )
    sends[1] = swap(sends[1])
    back_sum = (near_back + back_got.astype(single)).astype(bfloat)
    back_home = to_plane(back_sum.reshape(experts, capacity, model_width))
    sizes = [20 * model_width // 48, 12 * model_width // 48]
    thirds = [((rows, model_width), bfloat) for rows in (*sizes, model_width - sum(sizes))]
    sends += call(
        sums_kernel, "sums", thirds, 3, near_parts[1], far_parts[1], near_scaled, far_scaled
    )
    grad_router = dot_tn(near_logits, near) + dot_tn(far_logits, far)

    *attn_grads, grad_resid, grad_branch, grad_gain_ffn = call(
        functools.partial(post_kernel, n),
        "post",
        [((tok_count // 2, 2 * width), bfloat)] * n
        + [(rows_shape, single), (rows_shape, bfloat), ((1, model_width), single)],
        4,
        back_home.reshape(slots, model_width), dispatch_mat, resid, grad_block, gain_two, w_turned,
    )
    attn_grads, grad_branch, sends[0], *sends[2:] = tied(attn_grads, grad_branch, sends[0], *sends[2:])
    attn_grads = [attn_grads[0]] + [shift(attn_grads[r], n - r) for r in range(1, n)]

    count = lax.axis_size(PLANE)
    grad_output = dot_tn(attn_rows, grad_branch).astype(bfloat)
    grad_output = grad_output.reshape(n, count, width // count, model_width)
    grad_output = lax.all_to_all(grad_output, PLANE, split_axis=1, concat_axis=1, tiled=True)
    *attn_grads, far_made, sends[1], sends[2], grad_router = tied(
        *attn_grads, far_made, sends[1], sends[2], grad_router
    )
    made_got = shift(far_made, n // 2)
    sends[2] = lax.ppermute(sends[2], "ctx", pair)

    parts, late = attend_back(
        place_in, attn_grads, qkv, lse, rel, w_local, normed_all, gain_one, buckets_row,
        grad_gain_ffn, grad_router, heads
    )
    late, made_got, sends, grad_output = tied(late, made_got, sends, grad_output)
    late_width = late.shape[1]
    late = to_plane(late.reshape(count, model_width // count, late_width))
    grad_output = sum_first(grad_output.transpose(1, 0, 2, 3))
    shares = [grad_output[0]] + [shift(grad_output[r], n - r) for r in range(1, n)]
    made_sum = (near_made + made_got.astype(single)).astype(bfloat)
    sends[3] = swap(sends[3])
    late, made_sum, far_parts, shares, sends = tied(late, made_sum, far_parts, shares, sends)
    step = model_width // count
    (piece,) = call(
        join_kernel, "join", [((step, late_width + -(-width // 128) * 128), bfloat)], 1, late, *shares
    )
    pieces = [piece] + [shift(piece, r) for r in range(1, n)]
    made_home = to_plane(made_sum.reshape(experts, capacity, model_width))
    (grad_first,) = call(
        own_kernel, "own", [((model_width, model_width), single)], 4,
        near, far, near_parts[2], far_parts[2], *sends[:2],
    )
    pieces, parts, made_home, grad_first, sends = tied(pieces, parts, made_home, grad_first, sends)
    (stack,) = call(stack_kernel, "stack", [((n, *piece.shape), bfloat)], 1, *pieces)
    held = gather_chips(stack)
    sends[4] = swap(sends[4])
    (layer_out,) = call(
        layer_kernel, "layer", [(rows_shape, bfloat)], 3,
        made_home.reshape(slots, model_width), dispatch_mat, resid, gain_two, w_router, route_hot,
    )
    layer_out, parts = tied(layer_out, parts)
    parts = lax.all_to_all(parts, "ctx", split_axis=0, concat_axis=0, tiled=True)
    (grad_tokens,) = call(
        functools.partial(last_kernel, n), "last", [(rows_shape, bfloat)], 4,
        parts, w_all, block, gain_one, grad_resid,
    )
    (grad_second,) = call(
        own_kernel, "own", [((model_width, model_width), single)], 4,
        near_parts[0], far_parts[0], near_scaled, far_scaled, *sends[2:],
    )
    held, layer_out, grad_second = tied(held, layer_out, grad_second)
    (grad_query, grad_key, grad_value, output_all, grad_gain_attn, grad_gain_ffn, grad_table,
     grad_router) = place_all(gather_cores(held), heads, model_width, experts, late_width)
    return (
        layer_out.reshape(seq_dev, block_len, model_width).astype(bfloat),
        grad_tokens.reshape(seq_dev, block_len, model_width).astype(bfloat),
        grad_gain_attn,
        grad_query,
        grad_key,
        grad_value,
        output_all,
        grad_table.T,
        grad_gain_ffn,
        grad_router.T,
        grad_first[None],
        grad_second[None],
    )


def solution(mesh):
    spread = P(("dp", "expert"), "ctx", None)
    first = P(("dp", "expert"), None, "ctx")
    return jax.shard_map(
        shards,
        mesh=mesh,
        in_specs=(spread,) * 3 + (P(),) * 9 + (first, spread),
        out_specs=(spread,) * 2 + (P(),) * 8 + (first, spread),
        check_vma=False,
    )
```
